512 devices in a mesh: cell: 64 (over x, z, core), view: 8 (over y).
Axes of the slice: x: 4, y: 8, z: 8, core: 2. Of those that a mesh axis runs over, the one named last changes fastest.
Arguments:
- gaussians: float32 [512, 59, 256], P('cell'), may hold values from -7 to 6, as said below
- first_moment: float32 [512, 59, 256], P('cell'), may hold values from -1.2 to 1.2
- second_moment: float32 [512, 59, 256], P('cell'), may hold values from 0.001 to 0.1
- cameras: float32 [8, 6], P('view'), may hold values from -0.15 to 0.15
- visible_blocks: int32 [8, 128], P('view', 'cell'), may hold values from 0 to 511, as said below
- tile_ids: int32 [8, 128], P('view', 'cell'), may hold values from 0 to 127, each once within a row
- tile_order: int32 [8, 128, 4], P('view', 'cell'), may hold values from 0 to 127
- tile_length: int32 [8, 128], P('view', 'cell'), may hold values from 1 to 4
- targets: bfloat16 [8, 128, 3, 256], P('view', 'cell'), may hold values from 0 to 1
Outputs:
- new_gaussians: float32 [512, 59, 256], P('cell')
- new_first_moment: float32 [512, 59, 256], P('cell')
- new_second_moment: float32 [512, 59, 256], P('cell')
- camera_grad: float32 [8, 6], P('view')
The draws below stay inside these ranges and needn't reach their ends.
Inputs may be any that keep to these rules, and one draw needn't show every extreme that they name: `visible_blocks`: entries c * 2 to (c + 1) * 2 - 1 of each view's list are distinct blocks owned by cell c, that is blocks c * 8 to (c + 1) * 8 - 1. `gaussians`: centres have x and y in [-1.5, 1.5] and z in [3, 6]; log scales lie in [-1.5, 0]; the first quaternion entry lies in [0.5, 1.5], the others in [-1, 1]; opacity logits lie in [-7, -4]; harmonics lie in [-4, 4].
All inputs are finite; a program needn't handle non-finite values.
Results may differ from the reference program's by a relative error of at most 0.0003.
Values sent between devices are 32-bit elements; how exact they have to be, the bound alone decides.
No kernel may reach another device: no remote copies, remote signals or barrier semaphores. Data moves between devices by JAX's collectives and lax.ppermute only.
A program may use at most 128 MiB of HBM per device.

```python
import math
import jax
import jax.numpy as jnp
import numpy as np
from jax import lax

BLOCK = 256
PARAMS = 59
TILE = 16
PIX = 256
DEPTH = 4
OWN_BLK = 8
VIS_OWN = 2
BLOCKS = 512
VISIBLE = 128
TILES = 128
VIEWS = 8


def draw_gaussians(key, part):
    key = jax.random.fold_in(key, 5)
    lower_table = np.zeros(59, np.float32)
    upper_table = np.zeros(59, np.float32)
    scale_table = np.zeros(59, np.float32)
    lower_table[0:2] = -1.5
    upper_table[0:2] = 1.5
    lower_table[2] = 3.0
    upper_table[2] = 6.0
    lower_table[3:6] = -1.5
    upper_table[3:6] = 0.0
    lower_table[6] = 0.5
    upper_table[6] = 1.5
    lower_table[7:10] = -1.0
    upper_table[7:10] = 1.0
    lower_table[10] = -7.0
    upper_table[10] = -4.0
    scale_table[11:59] = 0.3
    scale_table[11] = 1.0
    scale_table[27] = 1.0
    scale_table[43] = 1.0
    uniform_part = jax.random.uniform(jax.random.fold_in(key, 1), (BLOCKS, 59, BLOCK), jnp.float32)
    normal_part = jnp.clip(jax.random.normal(jax.random.fold_in(key, 2), (BLOCKS, 59, BLOCK), jnp.float32), -4.0, 4.0)
    lower_rows = jnp.asarray(lower_table)[None, :, None]
    upper_rows = jnp.asarray(upper_table)[None, :, None]
    scale_rows = jnp.asarray(scale_table)[None, :, None]
    values = jnp.where(scale_rows > 0.0, jnp.clip(normal_part * scale_rows, -4.0, 4.0), lower_rows + (upper_rows - lower_rows) * uniform_part)
    return values.astype(jnp.float32)


def move_front(perm, wanted, slot):
    found = jnp.argmax((perm == wanted).astype(jnp.int32)).astype(jnp.int32)
    displaced = perm[slot]
    return perm.at[found].set(displaced).at[slot].set(wanted)


def draw_visible_blocks(key, part):
    key = jax.random.fold_in(key, 7)
    cell_count = VISIBLE // VIS_OWN
    view_keys = jax.random.split(key, VIEWS * cell_count)
    perms = jax.vmap(lambda single_key: jax.random.permutation(single_key, OWN_BLK))(view_keys).astype(jnp.int32)
    forced = jax.vmap(lambda perm: move_front(move_front(perm, 0, 0), OWN_BLK - 1, 1))(perms)
    first_view = (jnp.arange(VIEWS * cell_count, dtype=jnp.int32) < cell_count)[:, None]
    perms = jnp.where(first_view, forced, perms)
    orders = perms[:, :VIS_OWN].reshape(VIEWS, cell_count, VIS_OWN)
    owners = (jnp.arange(cell_count, dtype=jnp.int32) * OWN_BLK)[None, :, None]
    return (orders + owners).reshape(VIEWS, cell_count * VIS_OWN).astype(jnp.int32)


def with_ends(entries, rng, low, top_value):
    shape = entries.shape
    place = [jax.random.randint(jax.random.fold_in(rng, axis), (), 0, shape[axis]) for axis in range(len(shape))]
    entries = entries.at[tuple(place)].set(low)
    longest = shape.index(max(shape))
    place[longest] = (place[longest] + 1) % shape[longest]
    return entries.at[tuple(place)].set(top_value)


def level_of(stream_key, shape, cuts, low, high):
    def one(dim, parts):
        steps = jax.random.uniform(jax.random.fold_in(jax.random.fold_in(stream_key, 6), dim), (parts,), jnp.float32, low / len(cuts), high / len(cuts))
        return jnp.repeat(jnp.exp(steps), shape[dim] // parts).reshape((-1,) + (1,) * (len(shape) - dim - 1))

    factor_of = one(*cuts[0])
    for cut in cuts[1:]:
        factor_of = factor_of * one(*cut)
    return factor_of


def scatter_about(rng, extent, deviation, bound, cuts=(), held_as=jnp.bfloat16):
    loudness = level_of(rng, extent, cuts, -0.22, 0.18) if cuts else 1.0
    values = jax.random.normal(rng, extent, jnp.float32) * deviation * loudness
    return jnp.minimum(jnp.maximum(values, -bound), bound).astype(held_as)


def setup_inputs(seed: int = 0) -> dict:
    key_of = jax.random.split(jax.random.key(seed), 10)
    gaussians = draw_gaussians(jax.random.fold_in(key_of[9], 71), 0)
    first_moment = scatter_about(key_of[1], (BLOCKS, PARAMS, BLOCK), 0.2, 1.2, ((0, 64),), jnp.float32)
    second_moment = jnp.clip(jnp.exp(math.log(0.1) - 4.6051702 * jax.random.uniform(key_of[2], (BLOCKS, PARAMS, BLOCK), jnp.float32) ** level_of(key_of[2], (BLOCKS, PARAMS, BLOCK), ((0, 64),), -0.2, 0.2)), 0.001, 0.1)
    cameras = jnp.clip(jax.random.uniform(key_of[3], (VIEWS, 6), jnp.float32, -0.15, 0.15) * level_of(key_of[3], (VIEWS, 6), ((0, 8),), -0.4, 0.0), -0.15, 0.15)
    visible_blocks = draw_visible_blocks(jax.random.fold_in(key_of[9], 71), 0)
    tile_ids = jax.vmap(lambda own: jax.random.permutation(own, TILES))(jax.random.split(key_of[5], VIEWS)).reshape((VIEWS, TILES)).astype(jnp.int32)
    tile_order = with_ends(jax.random.randint(key_of[6], (VIEWS, TILES, DEPTH), 0, VISIBLE), jax.random.fold_in(key_of[6], 1), 0, VISIBLE - 1).astype(jnp.int32)
    tile_length = with_ends(jax.random.randint(key_of[7], (VIEWS, TILES), 1, DEPTH + 1), jax.random.fold_in(key_of[7], 1), 1, DEPTH).astype(jnp.int32)
    targets = jnp.clip(1.0 * jax.random.uniform(key_of[8], (VIEWS, TILES, 3, PIX), jnp.float32) ** level_of(key_of[8], (VIEWS, TILES, 3, PIX), ((0, 8), (1, 64)), -0.2, 0.2), 0.0, 1.0).astype(jnp.bfloat16)
    return {"gaussians": gaussians, "first_moment": first_moment, "second_moment": second_moment, "cameras": cameras, "visible_blocks": visible_blocks, "tile_ids": tile_ids, "tile_order": tile_order, "tile_length": tile_length, "targets": targets}


def rotation_matrix(real_part, axis_x, axis_y, axis_z):
    return [[1.0 - 2.0 * (axis_y * axis_y + axis_z * axis_z), 2.0 * (axis_x * axis_y - real_part * axis_z), 2.0 * (axis_x * axis_z + real_part * axis_y)], [2.0 * (axis_x * axis_y + real_part * axis_z), 1.0 - 2.0 * (axis_x * axis_x + axis_z * axis_z), 2.0 * (axis_y * axis_z - real_part * axis_x)], [2.0 * (axis_x * axis_z - real_part * axis_y), 2.0 * (axis_y * axis_z + real_part * axis_x), 1.0 - 2.0 * (axis_x * axis_x + axis_y * axis_y)]]

def harmonic_basis(unit_x, unit_y, unit_z):
    square_x = unit_x * unit_x
    square_y = unit_y * unit_y
    square_z = unit_z * unit_z
    return [jnp.full_like(unit_x, 0.28209479177387814), -0.4886025119029199 * unit_y, 0.4886025119029199 * unit_z, -0.4886025119029199 * unit_x, 1.0925484305920792 * unit_x * unit_y, -1.0925484305920792 * unit_y * unit_z, 0.31539156525252005 * (2.0 * square_z - square_x - square_y), -1.0925484305920792 * unit_x * unit_z, 0.5462742152960396 * (square_x - square_y), -0.5900435899266435 * unit_y * (3.0 * square_x - square_y), 2.890611442640554 * unit_x * unit_y * unit_z, -0.4570457994644658 * unit_y * (4.0 * square_z - square_x - square_y), 0.3731763325901154 * unit_z * (2.0 * square_z - 3.0 * square_x - 3.0 * square_y), -0.4570457994644658 * unit_x * (4.0 * square_z - square_x - square_y), 1.445305721320277 * unit_z * (square_x - square_y), -0.5900435899266435 * unit_x * (square_x - 3.0 * square_y)]

def project(blocks, camera, focal_length, centre_x, centre_y):
    camera_norm = jnp.sqrt(1.0 + camera[0] * camera[0] + camera[1] * camera[1] + camera[2] * camera[2])
    view_rotation = rotation_matrix(1.0 / camera_norm, camera[0] / camera_norm, camera[1] / camera_norm, camera[2] / camera_norm)
    translation = [camera[3], camera[4], camera[5]]
    centers = [blocks[:, 0], blocks[:, 1], blocks[:, 2]]
    in_view = [view_rotation[i][0] * centers[0] + view_rotation[i][1] * centers[1] + view_rotation[i][2] * centers[2] + translation[i] for i in range(3)]
    anchor = [-(view_rotation[0][i] * translation[0] + view_rotation[1][i] * translation[1] + view_rotation[2][i] * translation[2]) for i in range(3)]
    toward = [centers[i] - anchor[i] for i in range(3)]
    length = jnp.sqrt(toward[0] * toward[0] + toward[1] * toward[1] + toward[2] * toward[2])
    harmonics = harmonic_basis(toward[0] / length, toward[1] / length, toward[2] / length)
    colours = []
    for c in range(3):
        summed = 0.5 + sum((harmonics[k] * blocks[:, 11 + 16 * c + k] for k in range(16)))
        colours.append(jnp.maximum(summed, 0.0))
    quaternion = blocks[:, 6:10]
    quaternion_norm = jnp.sqrt(lax.optimization_barrier(jnp.sum(quaternion * quaternion, axis=1)))
    own_rotation = rotation_matrix(quaternion[:, 0] / quaternion_norm, quaternion[:, 1] / quaternion_norm, quaternion[:, 2] / quaternion_norm, quaternion[:, 3] / quaternion_norm)
    scales = jnp.exp(blocks[:, 3:6])
    factor = [[own_rotation[i][j] * scales[:, j] for j in range(3)] for i in range(3)]
    inverse_depth = 1.0 / in_view[2]
    jacobian = [[focal_length * inverse_depth, 0.0 * inverse_depth, -focal_length * in_view[0] * inverse_depth * inverse_depth], [0.0 * inverse_depth, focal_length * inverse_depth, -focal_length * in_view[1] * inverse_depth * inverse_depth]]
    screen_rotation = [[sum((jacobian[a][i] * view_rotation[i][j] for i in range(3))) for j in range(3)] for a in range(2)]
    spread = [[sum((screen_rotation[a][j] * factor[j][k] for j in range(3))) for k in range(3)] for a in range(2)]
    variance_x = sum((spread[0][k] * spread[0][k] for k in range(3))) + 0.3
    covariance = sum((spread[0][k] * spread[1][k] for k in range(3)))
    variance_y = sum((spread[1][k] * spread[1][k] for k in range(3))) + 0.3
    determinant = variance_x * variance_y - covariance * covariance
    return jnp.stack([focal_length * in_view[0] * inverse_depth + centre_x, focal_length * in_view[1] * inverse_depth + centre_y, variance_y / determinant, -covariance / determinant, variance_x / determinant, jax.nn.sigmoid(blocks[:, 10]), colours[0], colours[1], colours[2]], axis=1)

def tile_loss(visible, order, lengths, tile_ids, targets):
    tile_count = order.shape[0]
    pixels = TILE * TILE
    offsets = jnp.arange(pixels)
    pixel_x = (tile_ids % 16 * TILE)[:, None].astype(jnp.float32) + (offsets % TILE)[None, :].astype(jnp.float32) + 0.5
    pixel_y = (tile_ids // 16 * TILE)[:, None].astype(jnp.float32) + (offsets // TILE)[None, :].astype(jnp.float32) + 0.5
    remain = jnp.ones((tile_count, pixels), jnp.float32)
    colour = jnp.zeros((tile_count, 3, pixels), jnp.float32)
    for depth_step in range(DEPTH):
        features_now = visible[order[:, depth_step]]
        live_mask = (depth_step < lengths).astype(jnp.float32)
        delta_x = pixel_x[:, :, None] - features_now[:, 0][:, None, :]
        delta_y = pixel_y[:, :, None] - features_now[:, 1][:, None, :]
        exponent = -0.5 * (features_now[:, 2][:, None, :] * delta_x * delta_x + features_now[:, 4][:, None, :] * delta_y * delta_y) - features_now[:, 3][:, None, :] * delta_x * delta_y
        coverage = live_mask[:, None, None] * features_now[:, 5][:, None, :] * jnp.exp(exponent)
        log_keep = jnp.log1p(-coverage)
        before = jnp.cumsum(log_keep, axis=2) - log_keep
        weight = coverage * remain[:, :, None] * jnp.exp(before)
        colour = colour + jnp.einsum('ncg,npg->ncp', features_now[:, 6:9], weight, precision=lax.Precision.HIGHEST)
        remain = remain * jnp.exp(lax.optimization_barrier(jnp.sum(log_keep, axis=2)))
    misfit = colour - targets
    return 0.5 * jnp.sum(misfit * misfit)

def adam_update(values, moment, second, gradient):
    moment_new = 0.9 * moment + 0.1 * gradient
    second_new = 0.999 * second + 0.001 * gradient * gradient
    update = 0.05 * (moment_new / (1.0 - 0.9 ** 10)) / (jnp.sqrt(second_new / (1.0 - 0.999 ** 10)) + 1e-08)
    return (values - update, moment_new, second_new)

def reference(gaussians, first_moment, second_moment, cameras, visible_blocks, tile_ids, tile_order, tile_length, targets):
    tile_total = tile_ids.shape[1]
    focal_length = 16.0 * TILE
    centre_x = 8.0 * TILE
    centre_y = tile_total * TILE / 32.0
    groups = tile_total // 16
    gradient = jnp.zeros_like(gaussians)
    camera_rows = []
    for view_index in range(VIEWS):
        chosen = visible_blocks[view_index].astype(jnp.int32)

        def owner_side(blocks, camera, chosen=chosen):
            return project(blocks[chosen], camera, focal_length, centre_x, centre_y)
        features, owner_pull = jax.vjp(owner_side, gaussians, cameras[view_index])
        pieces = (tile_order[view_index].reshape(groups, 16, DEPTH), tile_length[view_index].reshape(groups, 16), tile_ids[view_index].reshape(groups, 16), targets[view_index].astype(jnp.float32).reshape(groups, 16, 3, TILE * TILE))

        def view_total(visible, pieces=pieces):
            return jnp.sum(lax.map(lambda group_data: tile_loss(visible, group_data[0], group_data[1], group_data[2], group_data[3]), pieces))
        loss_value, render_pull = jax.vjp(view_total, features)
        screen = render_pull(jnp.ones_like(loss_value))[0]
        grad_blocks, grad_camera = owner_pull(screen)
        gradient = gradient + grad_blocks
        camera_rows.append(grad_camera)
    new_gaussians, new_first, new_second = adam_update(gaussians, first_moment, second_moment, gradient)
    return (new_gaussians, new_first, new_second, jnp.stack(camera_rows))
```

```python
import jax
import jax.numpy as jnp
from jax import lax
from jax.experimental import pallas as pl
from jax.experimental.pallas import tpu as pltpu
from jax.sharding import PartitionSpec as P

TILE = 16
PIX = 256
BLOCK = 256
LANES = 128
HALVES = 2
FEATURES = 9
CORES = 2
MSG = 40
VIEW_MSG = 48
LOG2E = 1.4426950408889634
F32 = jnp.float32
BF16 = jnp.bfloat16


def rotation_matrix(real_part, axis_x, axis_y, axis_z):
    return [
        [
            1.0 - 2.0 * (axis_y * axis_y + axis_z * axis_z),
            2.0 * (axis_x * axis_y - real_part * axis_z),
            2.0 * (axis_x * axis_z + real_part * axis_y),
        ],
        [
            2.0 * (axis_x * axis_y + real_part * axis_z),
            1.0 - 2.0 * (axis_x * axis_x + axis_z * axis_z),
            2.0 * (axis_y * axis_z - real_part * axis_x),
        ],
        [
            2.0 * (axis_x * axis_z - real_part * axis_y),
            2.0 * (axis_y * axis_z + real_part * axis_x),
            1.0 - 2.0 * (axis_x * axis_x + axis_y * axis_y),
        ],
    ]


def harmonic_basis(unit_x, unit_y, unit_z):
    square_x = unit_x * unit_x
    square_y = unit_y * unit_y
    square_z = unit_z * unit_z
    return [
        -0.4886025119029199 * unit_y,
        0.4886025119029199 * unit_z,
        -0.4886025119029199 * unit_x,
        1.0925484305920792 * unit_x * unit_y,
        -1.0925484305920792 * unit_y * unit_z,
        0.31539156525252005 * (2.0 * square_z - square_x - square_y),
        -1.0925484305920792 * unit_x * unit_z,
        0.5462742152960396 * (square_x - square_y),
        -0.5900435899266435 * unit_y * (3.0 * square_x - square_y),
        2.890611442640554 * unit_x * unit_y * unit_z,
        -0.4570457994644658 * unit_y * (4.0 * square_z - square_x - square_y),
        0.3731763325901154 * unit_z * (2.0 * square_z - 3.0 * square_x - 3.0 * square_y),
        -0.4570457994644658 * unit_x * (4.0 * square_z - square_x - square_y),
        1.445305721320277 * unit_z * (square_x - square_y),
        -0.5900435899266435 * unit_x * (square_x - 3.0 * square_y),
    ]


HARMONIC_0 = 0.28209479177387814


def camera_frame(camera):
    inverse_norm = 1.0 / jnp.sqrt(
        1.0 + camera[0] * camera[0] + camera[1] * camera[1] + camera[2] * camera[2]
    )
    rotation = rotation_matrix(
        inverse_norm, camera[0] * inverse_norm, camera[1] * inverse_norm, camera[2] * inverse_norm
    )
    shift = [camera[3], camera[4], camera[5]]
    centre = [
        -(rotation[0][i] * shift[0] + rotation[1][i] * shift[1] + rotation[2][i] * shift[2])
        for i in range(3)
    ]
    return [rotation[i][j] for i in range(3) for j in range(3)] + shift + centre


def shape_factor(scales, quaternion):
    inverse_norm = 1.0 / jnp.sqrt(sum(entry * entry for entry in quaternion))
    own = rotation_matrix(*[entry * inverse_norm for entry in quaternion])
    widths = [jnp.exp(entry) for entry in scales]
    return [own[i][j] * widths[j] for i in range(3) for j in range(3)]


def view_of(centers, factor, frame, focal_length, centre_x, centre_y):
    rotation = [frame[3 * i : 3 * i + 3] for i in range(3)]
    shift = frame[9:12]
    origin = frame[12:15]
    in_view = [
        rotation[i][0] * centers[0]
        + rotation[i][1] * centers[1]
        + rotation[i][2] * centers[2]
        + shift[i]
        for i in range(3)
    ]
    inverse_depth = 1.0 / in_view[2]
    near = focal_length * inverse_depth
    ratio_x = in_view[0] * inverse_depth
    ratio_y = in_view[1] * inverse_depth
    screen = [
        [near * (rotation[0][j] - ratio_x * rotation[2][j]) for j in range(3)],
        [near * (rotation[1][j] - ratio_y * rotation[2][j]) for j in range(3)],
    ]
    spread = [
        [sum(screen[a][j] * factor[3 * j + k] for j in range(3)) for k in range(3)]
        for a in range(2)
    ]
    variance_x = sum(spread[0][k] * spread[0][k] for k in range(3)) + 0.3
    covariance = sum(spread[0][k] * spread[1][k] for k in range(3))
    variance_y = sum(spread[1][k] * spread[1][k] for k in range(3)) + 0.3
    inverse_determinant = 1.0 / (variance_x * variance_y - covariance * covariance)
    toward = [centers[i] - origin[i] for i in range(3)]
    inverse_length = 1.0 / jnp.sqrt(
        toward[0] * toward[0] + toward[1] * toward[1] + toward[2] * toward[2]
    )
    basis = harmonic_basis(*[entry * inverse_length for entry in toward])
    return [
        focal_length * ratio_x + centre_x,
        focal_length * ratio_y + centre_y,
        variance_y * inverse_determinant,
        -covariance * inverse_determinant,
        variance_x * inverse_determinant,
    ] + basis


def colour_sum(basis, harmonic_of, channel):
    summed = 0.5 + HARMONIC_0 * harmonic_of(channel, 0)
    for k in range(15):
        summed = summed + basis[k] * harmonic_of(channel, k + 1)
    return summed


def sigmoid(logit):
    return 1.0 / (1.0 + jnp.exp(-logit))


def project_kernel(focal, visible_ref, camera_ref, gauss_ref, out_ref):
    owned = gauss_ref.shape[0]
    copies = out_ref.shape[0]
    base = lax.axis_index("cell") * owned
    camera = [jnp.full((1, LANES), camera_ref[0, i], F32) for i in range(6)]
    frame = [jnp.broadcast_to(entry, (owned, LANES)) for entry in camera_frame(camera)]
    place = lax.broadcasted_iota(jnp.int32, (owned, LANES), 0)
    out_ref[0, 36:MSG, :] = jnp.zeros((MSG - 36, LANES), F32)
    for half in range(HALVES):
        lanes = slice(half * LANES, (half + 1) * LANES)

        def row(k):
            return gauss_ref[:, k, lanes]

        factor = shape_factor([row(3 + i) for i in range(3)], [row(6 + i) for i in range(4)])
        seen = view_of([row(i) for i in range(3)], factor, frame, *focal)
        colours = [
            jnp.maximum(colour_sum(seen[5:], lambda c, k: row(11 + 16 * c + k), channel), 0.0)
            for channel in range(3)
        ]
        features = seen[:5] + [sigmoid(row(10))] + colours
        for sub in range(2):
            mine = place == visible_ref[0, sub] - base
            for f in range(FEATURES):
                at = sub * 18 + half * 9 + f
                out_ref[0, at : at + 1, :] = jnp.sum(
                    jnp.where(mine, features[f], 0.0), axis=0, keepdims=True
                )
    message = out_ref[0]
    for i in range(1, copies):
        out_ref[i] = message


def split(value):
    high = value.astype(BF16)
    return high, (value - high.astype(F32)).astype(BF16)


def dot(left, right):
    return jnp.dot(left, right, preferred_element_type=F32)


def exact_dot(left, right):
    return jnp.dot(left, right, preferred_element_type=F32, precision=lax.Precision.HIGHEST)


def transpose_dot(left, right):
    return lax.dot_general(
        left,
        right,
        (((1,), (1,)), ((), ())),
        preferred_element_type=F32,
        precision=lax.Precision.HIGHEST,
    )


def render_kernel(
    order_ref,
    length_ref,
    tile_ref,
    target_ref,
    near_ref,
    far_ref,
    near_out,
    far_out,
    feature_scr,
    weight_scr,
    ratio_scr,
):
    slots, depth = order_ref.shape[1], order_ref.shape[2]
    core = lax.rem(lax.axis_index("cell"), CORES)
    near_out[...] = jnp.zeros_like(near_out)
    far_out[...] = jnp.zeros_like(far_out)
    first = lax.broadcasted_iota(jnp.int32, (BLOCK, BLOCK), 0)
    second = lax.broadcasted_iota(jnp.int32, (BLOCK, BLOCK), 1)
    earlier = (first < second).astype(BF16)
    later = (first > second).astype(BF16)
    same = (first == second).astype(F32)
    pixel = lax.broadcasted_iota(jnp.int32, (16, PIX), 1)
    kind = lax.broadcasted_iota(jnp.int32, (16, PIX), 0)
    along = (pixel % TILE).astype(F32) - 7.5
    down = (pixel // TILE).astype(F32) - 7.5
    moments = jnp.where(kind == 0, 1.0, 0.0)
    for i, term in enumerate([along, down, along * along, along * down, down * down]):
        moments = jnp.where(kind == i + 1, term, moments)
    moments = moments.astype(BF16)
    step_x = lax.broadcasted_iota(jnp.int32, (TILE, BLOCK), 0).astype(F32) - 7.5
    targets = target_ref[...].astype(F32)
    pad = jnp.zeros((5, PIX), F32)

    for slot in range(slots):
        tile = tile_ref[0, slot]
        tile_x = (lax.rem(tile, 16) * TILE + 8).astype(F32)
        tile_y = (lax.div(tile, 16) * TILE + 8).astype(F32)
        length = length_ref[0, slot]
        target = jnp.concatenate([targets[0, slot], pad], axis=0)

        def forward(k, carry):
            log_remain, colour = carry
            block = order_ref[0, slot, k]
            chip = lax.div(block, 4)
            on_near = lax.rem(lax.div(block, 2), CORES) == core
            tall = jnp.where(on_near, near_ref[chip], far_ref[chip])
            taken = jnp.where(lax.rem(block, 2) == 0, tall[0:18], tall[18:36])
            feature_scr[k, 0:9, 0:LANES] = taken[0:9]
            feature_scr[k, 0:9, LANES:] = taken[9:18]
            feature = feature_scr.at[k]
            local_x = feature[0:1, :] - tile_x
            local_y = feature[1:2, :] - tile_y
            delta_x = step_x - local_x
            curve_x = (-0.5 * LOG2E) * feature[2:3, :] * delta_x * delta_x
            cross_x = (-LOG2E) * feature[3:4, :] * delta_x
            curve = (-0.5 * LOG2E) * feature[4:5, :]
            rows = []
            for i in range(TILE):
                delta_y = (i - 7.5) - local_y
                rows.append(curve_x + (cross_x * delta_y + curve * delta_y * delta_y))
            exponent = jnp.concatenate(rows, axis=0)
            alpha = feature[5:6, :] * jnp.exp2(exponent)
            keep = alpha * (
                -LOG2E
                - alpha * (LOG2E / 2.0 + alpha * (LOG2E / 3.0 + alpha * (LOG2E / 4.0)))
            )
            high, low = split(keep)
            before = dot(high, earlier) + dot(low, earlier)
            weight = alpha * jnp.exp2(before + log_remain)
            ratio_scr[k] = alpha * jnp.exp2(-keep)
            weight_scr[k] = weight
            rgb = jnp.concatenate([feature[6:9, :], jnp.zeros((5, BLOCK), F32)], axis=0)
            colour = colour + transpose_dot(weight, rgb)
            return (log_remain + jnp.sum(keep, axis=1, keepdims=True), colour)

        log_remain, colour = lax.fori_loop(
            0, length, forward, (jnp.zeros((PIX, 1), F32), jnp.zeros((PIX, 8), F32))
        )
        misfit = colour - transpose_dot(same, target)
        misfit_rows = misfit.T

        def backward(step, behind):
            k = length - 1 - step
            block = order_ref[0, slot, k]
            chip = lax.div(block, 4)
            on_near = lax.rem(lax.div(block, 2), CORES) == core
            feature = feature_scr.at[k]
            rgb = jnp.concatenate([feature[6:9, :], jnp.zeros((5, BLOCK), F32)], axis=0)
            weight = weight_scr[k]
            through = weight * exact_dot(misfit, rgb)
            high, low = split(through)
            after = dot(high, later) + dot(low, later) + behind
            slope = through - after * ratio_scr[k]
            high, low = split(slope)
            moment = dot(moments, high) + dot(moments, low)
            colour_grad = exact_dot(misfit_rows, weight)
            local_x = feature[0:1, :] - tile_x
            local_y = feature[1:2, :] - tile_y
            total = moment[0:1]
            mean_x = moment[1:2] - local_x * total
            mean_y = moment[2:3] - local_y * total
            square_x = moment[3:4] - local_x * (moment[1:2] + mean_x)
            mixed = moment[4:5] - local_x * moment[2:3] - local_y * mean_x
            square_y = moment[5:6] - local_y * (moment[2:3] + mean_y)
            conic_x, conic_xy, conic_y = feature[2:3, :], feature[3:4, :], feature[4:5, :]
            grad = jnp.concatenate(
                [
                    conic_x * mean_x + conic_xy * mean_y,
                    conic_y * mean_y + conic_xy * mean_x,
                    -0.5 * square_x,
                    -mixed,
                    -0.5 * square_y,
                    total / feature[5:6, :],
                    colour_grad[0:3],
                ],
                axis=0,
            )
            grad = jnp.concatenate([grad[:, :LANES], grad[:, LANES:]], axis=0)
            even = (lax.rem(block, 2) == 0).astype(F32)
            grad = jnp.concatenate([grad * even, grad * (1.0 - even)], axis=0)

            @pl.when(on_near)
            def _():
                near_out[chip, 0:36, :] += grad

            @pl.when(jnp.logical_not(on_near))
            def _():
                far_out[chip, 0:36, :] += grad

            return behind + jnp.sum(through, axis=1, keepdims=True)

        lax.fori_loop(0, length, backward, jnp.zeros((PIX, 1), F32))


def collect_kernel(owned, visible_ref, camera_ref, parts_ref, out_ref):
    base = lax.axis_index("cell") * owned
    total = parts_ref[0]
    for i in range(1, parts_ref.shape[0]):
        total = total + parts_ref[i]
    out_ref[0, 0:MSG, :] = total
    for i in range(6):
        out_ref[0, 36 + i : 37 + i, :] = jnp.full((1, LANES), camera_ref[0, i], F32)
    for sub in range(2):
        chosen = (visible_ref[0, sub] - base).astype(F32)
        out_ref[0, 42 + sub : 43 + sub, :] = jnp.full((1, LANES), chosen, F32)
    out_ref[0, 44:VIEW_MSG, :] = jnp.zeros((VIEW_MSG - 44, LANES), F32)
    message = out_ref[0]
    for i in range(1, out_ref.shape[0]):
        out_ref[i] = message


def update_kernel(
    focal,
    parts_ref,
    gauss_ref,
    first_ref,
    second_ref,
    gauss_out,
    first_out,
    second_out,
    camera_out,
    rows_scr,
    factor_scr,
    sum_scr,
    grad_scr,
    frame_scr,
):
    owned, params = gauss_ref.shape[0], gauss_ref.shape[1]
    views = parts_ref.shape[0]
    own_view = lax.axis_index("view")
    place = lax.broadcasted_iota(jnp.int32, (owned, LANES), 0).astype(F32)
    whole = (owned, LANES)
    for half in range(HALVES):
        lanes = slice(half * LANES, (half + 1) * LANES)
        for k in range(params):
            rows_scr[k] = gauss_ref[:, k, lanes]
        factor, factor_pull = jax.vjp(
            shape_factor,
            [rows_scr[3 + i] for i in range(3)],
            [rows_scr[6 + i] for i in range(4)],
        )
        for i in range(9):
            factor_scr[i] = factor[i]
        sum_scr[...] = jnp.zeros_like(sum_scr)

        def one_view(view, carry):
            def message(k):
                return parts_ref[view, k : k + 1, :]

            masks = [place == message(42 + sub) for sub in range(2)]
            screen = [
                sum(
                    jnp.where(masks[sub], message(sub * 18 + half * 9 + f), 0.0)
                    for sub in range(2)
                )
                for f in range(FEATURES)
            ]
            frame = [
                jnp.broadcast_to(entry, whole)
                for entry in camera_frame([message(36 + i) for i in range(6)])
            ]
            seen, pull = jax.vjp(
                lambda centers, factor, frame: view_of(centers, factor, frame, *focal),
                [rows_scr[i] for i in range(3)],
                [factor_scr[i] for i in range(9)],
                frame,
            )
            basis = seen[5:]
            basis_grad = [jnp.zeros(whole, F32)] * 15
            for channel in range(3):
                first_row = 11 + 16 * channel
                summed = colour_sum(basis, lambda c, k: rows_scr[11 + 16 * c + k], channel)
                gate = jnp.where(summed > 0.0, 1.0, jnp.where(summed == 0.0, 0.5, 0.0))
                colour = screen[6 + channel] * gate
                sum_scr[first_row] += HARMONIC_0 * colour
                for k in range(15):
                    basis_grad[k] = basis_grad[k] + colour * rows_scr[first_row + 1 + k]
                    sum_scr[first_row + 1 + k] += colour * basis[k]
            centre_grad, factor_grad, frame_grad = pull(screen[:5] + basis_grad)
            for i in range(3):
                sum_scr[i] += centre_grad[i]
            sum_scr[10] += screen[5]
            for i in range(9):
                sum_scr[params + i] += factor_grad[i]

            @pl.when(view == own_view)
            def _():
                for i in range(15):
                    frame_scr[half, i] = frame_grad[i]
                for i in range(6):
                    frame_scr[half, 15 + i] = jnp.broadcast_to(message(36 + i), whole)

            return carry

        lax.fori_loop(0, views, one_view, 0)
        scale_grad, quaternion_grad = factor_pull([sum_scr[params + i] for i in range(9)])
        opacity = sigmoid(rows_scr[10])
        for i in range(3):
            sum_scr[3 + i] = scale_grad[i]
        for i in range(4):
            sum_scr[6 + i] = quaternion_grad[i]
        sum_scr[10] = sum_scr[10] * opacity * (1.0 - opacity)
        for k in range(params):
            grad_scr[:, k, lanes] = sum_scr[k]

    _, frame_pull = jax.vjp(camera_frame, [frame_scr[0, 15 + i, 0:1, :] for i in range(6)])
    camera_grad = frame_pull(
        [
            jnp.sum(frame_scr[0, i] + frame_scr[1, i], axis=0, keepdims=True)
            for i in range(15)
        ]
    )[0]
    lane = lax.broadcasted_iota(jnp.int32, (1, LANES), 1)
    packed = jnp.zeros((1, LANES), F32)
    for i in range(6):
        packed = packed + jnp.where(
            lane == i, jnp.sum(camera_grad[i], axis=1, keepdims=True), 0.0
        )
    packed = jnp.broadcast_to(packed, camera_out.shape[1:])
    for i in range(camera_out.shape[0]):
        camera_out[i] = packed

    for block in range(owned):
        gradient = grad_scr[block]
        moment = 0.9 * first_ref[block] + 0.1 * gradient
        second = 0.999 * second_ref[block] + 0.001 * gradient * gradient
        first_out[block] = moment
        second_out[block] = second
        gauss_out[block] = gauss_ref[block] - (0.05 / (1.0 - 0.9**10)) * moment / (
            jnp.sqrt(second * (1.0 / (1.0 - 0.999**10))) + 1e-08
        )


VMEM = pl.BlockSpec(memory_space=pltpu.VMEM)
SMEM = pl.BlockSpec(memory_space=pltpu.SMEM)
PARAMETERS = pltpu.CompilerParams(vmem_limit_bytes=40 * 1024 * 1024)


def shards(
    gaussians,
    first_moment,
    second_moment,
    cameras,
    visible_blocks,
    tile_ids,
    tile_order,
    tile_length,
    targets,
):
    owned, params = gaussians.shape[0], gaussians.shape[1]
    cells = lax.axis_size("cell")
    views = lax.axis_size("view")
    chips = cells // CORES
    tile_total = cells * tile_ids.shape[1]
    focal = (16.0 * TILE, 8.0 * TILE, tile_total * TILE / 32.0)
    same_core = [[chip * CORES + core for chip in range(chips)] for core in range(CORES)]
    swap = [(cell, cell ^ 1) for cell in range(cells)]

    with jax.named_scope("project"):
        message = pl.pallas_call(
            lambda *refs: project_kernel(focal, *refs),
            out_shape=jax.ShapeDtypeStruct((chips, MSG, LANES), F32),
            in_specs=[SMEM, SMEM, VMEM],
            out_specs=VMEM,
            compiler_params=PARAMETERS,
            name="project",
        )(visible_blocks, cameras, gaussians)
    with jax.named_scope("gather"):
        near = lax.all_to_all(message, "cell", 0, 0, axis_index_groups=same_core, tiled=True)
        far = lax.ppermute(near, "cell", swap)
    depth = tile_order.shape[2]
    with jax.named_scope("render"):
        near_grad, far_grad = pl.pallas_call(
            render_kernel,
            out_shape=[jax.ShapeDtypeStruct((chips, MSG, LANES), F32)] * 2,
            in_specs=[SMEM, SMEM, SMEM, VMEM, VMEM, VMEM],
            out_specs=[VMEM, VMEM],
            scratch_shapes=[
                pltpu.VMEM((depth, 16, BLOCK), F32),
                pltpu.VMEM((depth, PIX, BLOCK), F32),
                pltpu.VMEM((depth, PIX, BLOCK), F32),
            ],
            compiler_params=PARAMETERS,
            name="render",
        )(tile_order, tile_length, tile_ids, targets, near, far)
    with jax.named_scope("scatter"):
        pair = near_grad + lax.ppermute(far_grad, "cell", swap)
        parts = lax.all_to_all(pair, "cell", 0, 0, axis_index_groups=same_core, tiled=True)
    with jax.named_scope("collect"):
        own = pl.pallas_call(
            lambda *refs: collect_kernel(owned, *refs),
            out_shape=jax.ShapeDtypeStruct((views, VIEW_MSG, LANES), F32),
            in_specs=[SMEM, SMEM, VMEM],
            out_specs=VMEM,
            compiler_params=PARAMETERS,
            name="collect",
        )(visible_blocks, cameras, parts)
        every = lax.all_to_all(own, "view", 0, 0, tiled=True)
    with jax.named_scope("update"):
        state = jax.ShapeDtypeStruct(gaussians.shape, F32)
        new_gaussians, new_first, new_second, camera_part = pl.pallas_call(
            lambda *refs: update_kernel(focal, *refs),
            out_shape=[state, state, state, jax.ShapeDtypeStruct((cells, 1, LANES), F32)],
            in_specs=[VMEM] * 4,
            out_specs=[VMEM] * 4,
            scratch_shapes=[
                pltpu.VMEM((params, owned, LANES), F32),
                pltpu.VMEM((9, owned, LANES), F32),
                pltpu.VMEM((params + 9, owned, LANES), F32),
                pltpu.VMEM(gaussians.shape, F32),
                pltpu.VMEM((HALVES, 21, owned, LANES), F32),
            ],
            compiler_params=PARAMETERS,
            name="update",
        )(every, gaussians, first_moment, second_moment)
    with jax.named_scope("camera"):
        camera_parts = lax.all_to_all(camera_part, "cell", 0, 0, tiled=True)
        camera_total = jnp.sum(camera_parts, axis=0)[:, :6]
    return (new_gaussians, new_first, new_second, camera_total)


def solution(mesh):
    return jax.shard_map(
        shards,
        mesh=mesh,
        in_specs=(
            P("cell", None, None),
            P("cell", None, None),
            P("cell", None, None),
            P("view", None),
            P("view", "cell"),
            P("view", "cell"),
            P("view", "cell", None),
            P("view", "cell"),
            P("view", "cell", None, None),
        ),
        out_specs=(
            P("cell", None, None),
            P("cell", None, None),
            P("cell", None, None),
            P("view", None),
        ),
        check_vma=False,
    )
```

```python
import jax
import jax.numpy as jnp
from jax import lax
from jax.experimental import pallas as pl
from jax.experimental.pallas import tpu as pltpu
from jax.sharding import PartitionSpec as P

TILE = 16
PIX = 256
BLOCK = 256
LANES = 128
HALVES = 2
FEATURES = 9
CORES = 2
ROWS = 4
VIEW_MSG = 11
LOG2E = 1.4426950408889634
F32 = jnp.float32
BF16 = jnp.bfloat16


def rotation_matrix(real_part, axis_x, axis_y, axis_z):
    return [
        [
            1.0 - 2.0 * (axis_y * axis_y + axis_z * axis_z),
            2.0 * (axis_x * axis_y - real_part * axis_z),
            2.0 * (axis_x * axis_z + real_part * axis_y),
        ],
        [
            2.0 * (axis_x * axis_y + real_part * axis_z),
            1.0 - 2.0 * (axis_x * axis_x + axis_z * axis_z),
            2.0 * (axis_y * axis_z - real_part * axis_x),
        ],
        [
            2.0 * (axis_x * axis_z - real_part * axis_y),
            2.0 * (axis_y * axis_z + real_part * axis_x),
            1.0 - 2.0 * (axis_x * axis_x + axis_y * axis_y),
        ],
    ]


def harmonic_basis(unit_x, unit_y, unit_z):
    square_x = unit_x * unit_x
    square_y = unit_y * unit_y
    square_z = unit_z * unit_z
    return [
        -0.4886025119029199 * unit_y,
        0.4886025119029199 * unit_z,
        -0.4886025119029199 * unit_x,
        1.0925484305920792 * unit_x * unit_y,
        -1.0925484305920792 * unit_y * unit_z,
        0.31539156525252005 * (2.0 * square_z - square_x - square_y),
        -1.0925484305920792 * unit_x * unit_z,
        0.5462742152960396 * (square_x - square_y),
        -0.5900435899266435 * unit_y * (3.0 * square_x - square_y),
        2.890611442640554 * unit_x * unit_y * unit_z,
        -0.4570457994644658 * unit_y * (4.0 * square_z - square_x - square_y),
        0.3731763325901154 * unit_z * (2.0 * square_z - 3.0 * square_x - 3.0 * square_y),
        -0.4570457994644658 * unit_x * (4.0 * square_z - square_x - square_y),
        1.445305721320277 * unit_z * (square_x - square_y),
        -0.5900435899266435 * unit_x * (square_x - 3.0 * square_y),
    ]


HARMONIC_0 = 0.28209479177387814


def camera_frame(camera):
    inverse_norm = 1.0 / jnp.sqrt(
        1.0 + camera[0] * camera[0] + camera[1] * camera[1] + camera[2] * camera[2]
    )
    rotation = rotation_matrix(
        inverse_norm, camera[0] * inverse_norm, camera[1] * inverse_norm, camera[2] * inverse_norm
    )
    shift = [camera[3], camera[4], camera[5]]
    centre = [
        -(rotation[0][i] * shift[0] + rotation[1][i] * shift[1] + rotation[2][i] * shift[2])
        for i in range(3)
    ]
    return [rotation[i][j] for i in range(3) for j in range(3)] + shift + centre


def shape_factor(scales, quaternion):
    inverse_norm = 1.0 / jnp.sqrt(sum(entry * entry for entry in quaternion))
    own = rotation_matrix(*[entry * inverse_norm for entry in quaternion])
    widths = [jnp.exp(entry) for entry in scales]
    return [own[i][j] * widths[j] for i in range(3) for j in range(3)]


def view_of(centers, factor, frame, focal_length, centre_x, centre_y):
    rotation = [frame[3 * i : 3 * i + 3] for i in range(3)]
    shift = frame[9:12]
    origin = frame[12:15]
    in_view = [
        rotation[i][0] * centers[0]
        + rotation[i][1] * centers[1]
        + rotation[i][2] * centers[2]
        + shift[i]
        for i in range(3)
    ]
    inverse_depth = 1.0 / in_view[2]
    near = focal_length * inverse_depth
    ratio_x = in_view[0] * inverse_depth
    ratio_y = in_view[1] * inverse_depth
    screen = [
        [near * (rotation[0][j] - ratio_x * rotation[2][j]) for j in range(3)],
        [near * (rotation[1][j] - ratio_y * rotation[2][j]) for j in range(3)],
    ]
    spread = [
        [sum(screen[a][j] * factor[3 * j + k] for j in range(3)) for k in range(3)]
        for a in range(2)
    ]
    variance_x = sum(spread[0][k] * spread[0][k] for k in range(3)) + 0.3
    covariance = sum(spread[0][k] * spread[1][k] for k in range(3))
    variance_y = sum(spread[1][k] * spread[1][k] for k in range(3)) + 0.3
    inverse_determinant = 1.0 / (variance_x * variance_y - covariance * covariance)
    toward = [centers[i] - origin[i] for i in range(3)]
    inverse_length = 1.0 / jnp.sqrt(
        toward[0] * toward[0] + toward[1] * toward[1] + toward[2] * toward[2]
    )
    basis = harmonic_basis(*[entry * inverse_length for entry in toward])
    return [
        focal_length * ratio_x + centre_x,
        focal_length * ratio_y + centre_y,
        variance_y * inverse_determinant,
        -covariance * inverse_determinant,
        variance_x * inverse_determinant,
    ] + basis


def colour_sum(basis, harmonic_of, channel):
    summed = 0.5 + HARMONIC_0 * harmonic_of(channel, 0)
    for k in range(15):
        summed = summed + basis[k] * harmonic_of(channel, k + 1)
    return summed


def sigmoid(logit):
    return 1.0 / (1.0 + jnp.exp(-logit))


def features_of(row, camera, focal):
    shape = row(0).shape
    frame = [jnp.broadcast_to(entry, shape) for entry in camera_frame(camera)]
    factor = shape_factor([row(3 + i) for i in range(3)], [row(6 + i) for i in range(4)])
    seen = view_of([row(i) for i in range(3)], factor, frame, *focal)
    colours = [
        jnp.maximum(colour_sum(seen[5:], lambda c, k: row(11 + 16 * c + k), channel), 0.0)
        for channel in range(3)
    ]
    return seen[:5] + [sigmoid(row(10))] + colours


def halves_of(gauss_ref):
    return lambda k: jnp.concatenate(
        [gauss_ref[k, :, half * LANES : (half + 1) * LANES] for half in range(HALVES)], axis=0
    )


def pick(visible_ref, owned):
    base = lax.axis_index("cell") * owned
    place = lax.broadcasted_iota(jnp.int32, (owned, LANES), 0)
    masks = [place == visible_ref[0, sub] - base for sub in range(2)]
    return lambda value: [
        jnp.sum(
            jnp.where(mask, value[half * owned : (half + 1) * owned], 0.0), axis=0, keepdims=True
        )
        for mask in masks
        for half in range(HALVES)
    ]


def camera_rows(camera_ref):
    return [jnp.full((1, LANES), camera_ref[0, i], F32) for i in range(6)]


def project_kernel(focal, visible_ref, camera_ref, gauss_ref, out_ref):
    features = features_of(halves_of(gauss_ref), camera_rows(camera_ref), focal)
    picked = pick(visible_ref, gauss_ref.shape[1])
    for f in range(FEATURES):
        out_ref[0, f] = jnp.concatenate(picked(features[f]), axis=0)
    message = out_ref[0]
    for i in range(1, out_ref.shape[0]):
        out_ref[i] = message


def slope_kernel(focal, visible_ref, camera_ref, gauss_ref, out_ref):
    camera = camera_rows(camera_ref)
    whole = halves_of(gauss_ref)
    picked = pick(visible_ref, gauss_ref.shape[1])
    held = [jnp.concatenate(picked(whole(k)), axis=0) for k in range(gauss_ref.shape[0])]
    for i in range(6):
        tangents = [jnp.full((1, LANES), 1.0 if j == i else 0.0, F32) for j in range(6)]
        _, slopes = jax.jvp(
            lambda *entries: features_of(held.__getitem__, entries, focal), camera, tangents
        )
        for f in range(FEATURES):
            out_ref[i, f] = slopes[f]


def split(value):
    high = value.astype(BF16)
    return high, (value - high.astype(F32)).astype(BF16)


def dot(left, right):
    return jnp.dot(left, right, preferred_element_type=F32)


def both_dots(pair, right):
    return dot(pair[0], right) + dot(pair[1], right)


def transpose_dot(left, right):
    return lax.dot_general(
        left, right, (((1,), (1,)), ((), ())), preferred_element_type=F32
    )


def stacked(value, rows):
    high, low = split(value)
    return jnp.concatenate(
        [high.astype(F32), low.astype(F32), jnp.zeros((rows - 6, value.shape[1]), F32)], axis=0
    ).astype(BF16)


def render_kernel(
    order_ref,
    length_ref,
    tile_ref,
    target_ref,
    near_ref,
    far_ref,
    near_out,
    far_out,
    feature_scr,
    rgb_scr,
    weight_scr,
    high_scr,
    low_scr,
    ratio_scr,
):
    slots = order_ref.shape[1]
    core = lax.rem(lax.axis_index("cell"), CORES)
    near_out[...] = jnp.zeros_like(near_out)
    far_out[...] = jnp.zeros_like(far_out)
    first = lax.broadcasted_iota(jnp.int32, (BLOCK, BLOCK), 0)
    second = lax.broadcasted_iota(jnp.int32, (BLOCK, BLOCK), 1)
    earlier = (first < second).astype(BF16)
    later = (first > second).astype(BF16)
    ones = jnp.ones((BLOCK, LANES), BF16)
    step_x = lax.broadcasted_iota(jnp.int32, (TILE, BLOCK), 0).astype(F32) - 7.5
    part = lax.broadcasted_iota(jnp.int32, (ROWS, LANES), 0)
    targets = target_ref[...].astype(F32)

    def spread_over(value):
        return jnp.concatenate([value, value], axis=1)

    for slot in range(slots):
        tile = tile_ref[0, slot]
        tile_x = (lax.rem(tile, 16) * TILE + 8).astype(F32)
        tile_y = (lax.div(tile, 16) * TILE + 8).astype(F32)
        length = length_ref[0, slot]

        def forward(k, carry):
            log_remain, colour = carry
            block = order_ref[0, slot, k]
            chip = lax.div(block, 4)
            on_near = lax.rem(lax.div(block, 2), CORES) == core
            even = lax.rem(block, 2) == 0
            for f in range(FEATURES):
                entry = jnp.where(on_near, near_ref[chip, f], far_ref[chip, f])
                entry = jnp.where(even, entry[0:2], entry[2:4])
                feature_scr[k, f : f + 1, 0:LANES] = entry[0:1]
                feature_scr[k, f : f + 1, LANES:] = entry[1:2]
            feature = feature_scr.at[k]
            rgb_scr[k] = stacked(feature[6:9, :], 16)
            delta_x = step_x - (feature[0:1, :] - tile_x)
            local_y = feature[1:2, :] - tile_y
            curve_x = (-0.5 * LOG2E) * feature[2:3, :] * delta_x * delta_x
            cross_x = (-LOG2E) * feature[3:4, :] * delta_x
            curve = (-0.5 * LOG2E) * feature[4:5, :]
            rows = []
            for i in range(TILE):
                delta_y = (i - 7.5) - local_y
                rows.append(curve_x + (cross_x * delta_y + curve * delta_y * delta_y))
            exponent = jnp.concatenate(rows, axis=0)
            alpha = feature[5:6, :] * jnp.exp2(exponent)
            keep = alpha * (
                -LOG2E
                - alpha * (LOG2E / 2.0 + alpha * (LOG2E / 3.0 + alpha * (LOG2E / 4.0)))
            )
            pair = split(keep)
            before = both_dots(pair, earlier) + spread_over(log_remain)
            weight = alpha * jnp.exp2(before)
            ratio_scr[k] = alpha * jnp.exp2(-keep)
            weight_scr[k] = weight
            high, low = split(weight)
            high_scr[k] = high
            low_scr[k] = low
            colour = colour + transpose_dot(high, rgb_scr[k]) + transpose_dot(low, rgb_scr[k])
            return (log_remain + both_dots(pair, ones), colour)

        _, colour = lax.fori_loop(
            0, length, forward, (jnp.zeros((PIX, LANES), F32), jnp.zeros((PIX, 16), F32))
        )
        turned = colour.T
        misfit = turned[0:3] + turned[3:6] - targets[0, slot]
        misfit_rows = stacked(misfit, 16)
        misfit_high, misfit_low = split(misfit)
        misfit_high = misfit_high.astype(F32)
        misfit_low = misfit_low.astype(F32)
        blank = jnp.zeros((10, PIX), F32)
        misfit_pair = tuple(
            jnp.concatenate([term, term, blank], axis=0).T.astype(BF16)
            for term in (misfit_high, misfit_low)
        )

        def backward(step, behind):
            k = length - 1 - step
            block = order_ref[0, slot, k]
            chip = lax.div(block, 4)
            on_near = lax.rem(lax.div(block, 2), CORES) == core
            side = lax.rem(block, 2) * 2
            feature = feature_scr.at[k]
            through = weight_scr[k] * both_dots(misfit_pair, rgb_scr[k])
            pair = split(through)
            after = both_dots(pair, later) + spread_over(behind)
            slope = through - after * ratio_scr[k]
            flat = jnp.zeros((TILE, BLOCK), F32)
            tilt = jnp.zeros((TILE, BLOCK), F32)
            bend = jnp.zeros((TILE, BLOCK), F32)
            for i in range(TILE // 2):
                top = slope[i * TILE : (i + 1) * TILE]
                bottom = slope[(TILE - 1 - i) * TILE : (TILE - i) * TILE]
                away = 7.5 - i
                flat = flat + (top + bottom)
                tilt = tilt + away * (bottom - top)
                bend = bend + (away * away) * (top + bottom)
            colour_grad = dot(misfit_rows, high_scr[k]) + dot(misfit_rows, low_scr[k])
            delta_x = step_x - (feature[0:1, :] - tile_x)
            local_y = feature[1:2, :] - tile_y
            mean = tilt - local_y * flat
            bend = bend - local_y * (tilt + mean)

            def across(value):
                return jnp.sum(value, axis=0, keepdims=True)

            total, mean_x, mean_y = across(flat), across(delta_x * flat), across(mean)
            square_x = across(delta_x * delta_x * flat)
            mixed = across(delta_x * mean)
            square_y = across(bend)
            conic_x, conic_xy, conic_y = feature[2:3, :], feature[3:4, :], feature[4:5, :]
            grads = [
                conic_x * mean_x + conic_xy * mean_y,
                conic_y * mean_y + conic_xy * mean_x,
                -0.5 * square_x,
                -mixed,
                -0.5 * square_y,
                total / feature[5:6, :],
            ] + [colour_grad[i : i + 1] + colour_grad[i + 3 : i + 4] for i in range(3)]
            placed = [
                jnp.where(
                    part == side,
                    grad[:, :LANES],
                    jnp.where(part == side + 1, grad[:, LANES:], 0.0),
                )
                for grad in grads
            ]

            @pl.when(on_near)
            def _():
                for f in range(FEATURES):
                    near_out[chip, f] += placed[f]

            @pl.when(jnp.logical_not(on_near))
            def _():
                for f in range(FEATURES):
                    far_out[chip, f] += placed[f]

            return behind + both_dots(pair, ones)

        lax.fori_loop(0, length, backward, jnp.zeros((PIX, LANES), F32))


def collect_kernel(owned, visible_ref, camera_ref, parts_ref, slope_ref, out_ref, camera_out):
    base = lax.axis_index("cell") * owned
    total = parts_ref[0]
    for i in range(1, parts_ref.shape[0]):
        total = total + parts_ref[i]
    out_ref[0, 0:FEATURES] = total
    base_rows = [jnp.full((1, LANES), camera_ref[0, i], F32) for i in range(6)] + [
        jnp.full((1, LANES), (visible_ref[0, sub] - base).astype(F32), F32) for sub in range(2)
    ]
    for i in range(2):
        out_ref[0, FEATURES + i] = jnp.concatenate(base_rows[4 * i : 4 * i + 4], axis=0)
    message = out_ref[0]
    for i in range(1, out_ref.shape[0]):
        out_ref[i] = message
    lane = lax.broadcasted_iota(jnp.int32, (1, LANES), 1)
    packed = jnp.zeros((1, LANES), F32)
    for i in range(6):
        across = jnp.sum(
            jnp.sum(total * slope_ref[i], axis=0), axis=0, keepdims=True
        )
        packed = packed + jnp.where(lane == i, jnp.sum(across, axis=1, keepdims=True), 0.0)
    for i in range(camera_out.shape[0]):
        camera_out[i] = packed


def update_kernel(
    focal,
    parts_ref,
    gauss_ref,
    first_ref,
    second_ref,
    gauss_out,
    first_out,
    second_out,
    factor_scr,
    sum_scr,
):
    params, owned = gauss_ref.shape[0], gauss_ref.shape[1]
    views = parts_ref.shape[0]
    place = lax.broadcasted_iota(jnp.int32, (owned, LANES), 0).astype(F32)
    whole = (owned, LANES)
    for half in range(HALVES):
        lanes = slice(half * LANES, (half + 1) * LANES)

        def row(k, lanes=lanes):
            return gauss_ref[k, :, lanes]

        factor, factor_pull = jax.vjp(
            shape_factor,
            [row(3 + i) for i in range(3)],
            [row(6 + i) for i in range(4)],
        )
        for i in range(9):
            factor_scr[i] = factor[i]
        sum_scr[...] = jnp.zeros_like(sum_scr)

        def one_view(view, carry):
            def message(f, r):
                return parts_ref[view, f, r : r + 1, :]

            masks = [place == message(FEATURES + 1, 2 + sub) for sub in range(2)]
            screen = [
                sum(
                    jnp.where(masks[sub], message(f, sub * 2 + half), 0.0)
                    for sub in range(2)
                )
                for f in range(FEATURES)
            ]
            frame = [
                jnp.broadcast_to(entry, whole)
                for entry in camera_frame([message(FEATURES + i // 4, i % 4) for i in range(6)])
            ]
            seen, pull = jax.vjp(
                lambda centers, factor: view_of(centers, factor, frame, *focal),
                [row(i) for i in range(3)],
                [factor_scr[i] for i in range(9)],
            )
            basis = seen[5:]
            basis_grad = [jnp.zeros(whole, F32)] * 15
            for channel in range(3):
                first_row = 11 + 16 * channel
                summed = colour_sum(basis, lambda c, k: row(11 + 16 * c + k), channel)
                gate = jnp.where(summed > 0.0, 1.0, jnp.where(summed == 0.0, 0.5, 0.0))
                colour = screen[6 + channel] * gate
                sum_scr[first_row] += HARMONIC_0 * colour
                for k in range(15):
                    basis_grad[k] = basis_grad[k] + colour * row(first_row + 1 + k)
                    sum_scr[first_row + 1 + k] += colour * basis[k]
            centre_grad, factor_grad = pull(screen[:5] + basis_grad)
            for i in range(3):
                sum_scr[i] += centre_grad[i]
            sum_scr[10] += screen[5]
            for i in range(9):
                sum_scr[params + i] += factor_grad[i]
            return carry

        lax.fori_loop(0, views, one_view, 0)
        scale_grad, quaternion_grad = factor_pull([sum_scr[params + i] for i in range(9)])
        opacity = sigmoid(row(10))
        for i in range(3):
            sum_scr[3 + i] = scale_grad[i]
        for i in range(4):
            sum_scr[6 + i] = quaternion_grad[i]
        sum_scr[10] = sum_scr[10] * opacity * (1.0 - opacity)
        for k in range(params):
            gradient = sum_scr[k]
            moment = 0.9 * first_ref[k, :, lanes] + 0.1 * gradient
            second = 0.999 * second_ref[k, :, lanes] + 0.001 * gradient * gradient
            first_out[k, :, lanes] = moment
            second_out[k, :, lanes] = second
            gauss_out[k, :, lanes] = row(k) - (0.05 / (1.0 - 0.9**10)) * moment / (
                jnp.sqrt(second * (1.0 / (1.0 - 0.999**10))) + 1e-08
            )


VMEM = pl.BlockSpec(memory_space=pltpu.VMEM)
SMEM = pl.BlockSpec(memory_space=pltpu.SMEM)
PARAMETERS = pltpu.CompilerParams(vmem_limit_bytes=40 * 1024 * 1024)


def shards(
    gaussians,
    first_moment,
    second_moment,
    cameras,
    visible_blocks,
    tile_ids,
    tile_order,
    tile_length,
    targets,
):
    owned, params = gaussians.shape[0], gaussians.shape[1]
    gaussians, first_moment, second_moment = (
        array.transpose(1, 0, 2) for array in (gaussians, first_moment, second_moment)
    )
    cells = lax.axis_size("cell")
    views = lax.axis_size("view")
    chips = cells // CORES
    tile_total = cells * tile_ids.shape[1]
    focal = (16.0 * TILE, 8.0 * TILE, tile_total * TILE / 32.0)
    same_core = [[chip * CORES + core for chip in range(chips)] for core in range(CORES)]
    swap = [(cell, cell ^ 1) for cell in range(cells)]

    with jax.named_scope("project"):
        message = pl.pallas_call(
            lambda *refs: project_kernel(focal, *refs),
            out_shape=jax.ShapeDtypeStruct((chips, FEATURES, ROWS, LANES), F32),
            in_specs=[SMEM, SMEM, VMEM],
            out_specs=VMEM,
            compiler_params=PARAMETERS,
            name="project",
        )(visible_blocks, cameras, gaussians)
        slopes = pl.pallas_call(
            lambda *refs: slope_kernel(focal, *refs),
            out_shape=jax.ShapeDtypeStruct((6, FEATURES, ROWS, LANES), F32),
            in_specs=[SMEM, SMEM, VMEM],
            out_specs=VMEM,
            compiler_params=PARAMETERS,
            cost_estimate=pl.CostEstimate(
                flops=4_000_000, bytes_accessed=200_000, transcendentals=10_000
            ),
            name="slope",
        )(visible_blocks, cameras, gaussians)
    with jax.named_scope("gather"):
        near = lax.all_to_all(message, "cell", 0, 0, axis_index_groups=same_core, tiled=True)
        far = lax.ppermute(near, "cell", swap)
    depth = tile_order.shape[2]
    with jax.named_scope("render"):
        near_grad, far_grad = pl.pallas_call(
            render_kernel,
            out_shape=[jax.ShapeDtypeStruct((chips, FEATURES, ROWS, LANES), F32)] * 2,
            in_specs=[SMEM, SMEM, SMEM, VMEM, VMEM, VMEM],
            out_specs=[VMEM, VMEM],
            scratch_shapes=[
                pltpu.VMEM((depth, 16, BLOCK), F32),
                pltpu.VMEM((depth, 16, BLOCK), BF16),
                pltpu.VMEM((depth, PIX, BLOCK), F32),
                pltpu.VMEM((depth, PIX, BLOCK), BF16),
                pltpu.VMEM((depth, PIX, BLOCK), BF16),
                pltpu.VMEM((depth, PIX, BLOCK), F32),
            ],
            compiler_params=PARAMETERS,
            name="render",
        )(tile_order, tile_length, tile_ids, targets, near, far)
    with jax.named_scope("scatter"):
        pair = near_grad + lax.ppermute(far_grad, "cell", swap)
        parts = lax.all_to_all(pair, "cell", 0, 0, axis_index_groups=same_core, tiled=True)
    with jax.named_scope("collect"):
        own, camera_part = pl.pallas_call(
            lambda *refs: collect_kernel(owned, *refs),
            out_shape=[
                jax.ShapeDtypeStruct((views, VIEW_MSG, ROWS, LANES), F32),
                jax.ShapeDtypeStruct((1, 1, LANES), F32),
            ],
            in_specs=[SMEM, SMEM, VMEM, VMEM],
            out_specs=[VMEM, VMEM],
            compiler_params=PARAMETERS,
            name="collect",
        )(visible_blocks, cameras, parts, slopes)
        every = lax.all_to_all(own, "view", 0, 0, tiled=True)
    with jax.named_scope("camera"):
        camera_pair = camera_part + lax.ppermute(camera_part, "cell", swap)
        every, camera_pair = lax.optimization_barrier((every, camera_pair))
        camera_parts = lax.all_to_all(
            jnp.broadcast_to(camera_pair, (chips, 1, LANES)),
            "cell",
            0,
            0,
            axis_index_groups=same_core,
            tiled=True,
        )
    with jax.named_scope("update"):
        state = jax.ShapeDtypeStruct(gaussians.shape, F32)
        new_gaussians, new_first, new_second = pl.pallas_call(
            lambda *refs: update_kernel(focal, *refs),
            out_shape=[state, state, state],
            in_specs=[VMEM] * 4,
            out_specs=[VMEM] * 3,
            scratch_shapes=[
                pltpu.VMEM((9, owned, LANES), F32),
                pltpu.VMEM((params + 9, owned, LANES), F32),
            ],
            compiler_params=PARAMETERS,
            name="update",
        )(every, gaussians, first_moment, second_moment)
    with jax.named_scope("camera"):
        camera_total = jnp.sum(camera_parts, axis=0)[:, :6]
    return (
        new_gaussians.transpose(1, 0, 2),
        new_first.transpose(1, 0, 2),
        new_second.transpose(1, 0, 2),
        camera_total,
    )


def solution(mesh):
    return jax.shard_map(
        shards,
        mesh=mesh,
        in_specs=(
            P("cell", None, None),
            P("cell", None, None),
            P("cell", None, None),
            P("view", None),
            P("view", "cell"),
            P("view", "cell"),
            P("view", "cell", None),
            P("view", "cell"),
            P("view", "cell", None, None),
        ),
        out_specs=(
            P("cell", None, None),
            P("cell", None, None),
            P("cell", None, None),
            P("view", None),
        ),
        check_vma=False,
    )
```

```python
import functools

import jax
import jax.numpy as jnp
from jax import lax
from jax.experimental import pallas as pl
from jax.experimental.pallas import tpu as pltpu
from jax.sharding import PartitionSpec as P

TILE = 16
PIX = 256
BLOCK = 256
LANES = 128
HALVES = 2
FEATURES = 9
CORES = 2
ROWS = 4
VIEW_MSG = 11
LOG2E = 1.4426950408889634
F32 = jnp.float32
BF16 = jnp.bfloat16


def rotation_matrix(real_part, axis_x, axis_y, axis_z):
    return [
        [
            1.0 - 2.0 * (axis_y * axis_y + axis_z * axis_z),
            2.0 * (axis_x * axis_y - real_part * axis_z),
            2.0 * (axis_x * axis_z + real_part * axis_y),
        ],
        [
            2.0 * (axis_x * axis_y + real_part * axis_z),
            1.0 - 2.0 * (axis_x * axis_x + axis_z * axis_z),
            2.0 * (axis_y * axis_z - real_part * axis_x),
        ],
        [
            2.0 * (axis_x * axis_z - real_part * axis_y),
            2.0 * (axis_y * axis_z + real_part * axis_x),
            1.0 - 2.0 * (axis_x * axis_x + axis_y * axis_y),
        ],
    ]


def harmonic_basis(unit_x, unit_y, unit_z):
    square_x = unit_x * unit_x
    square_y = unit_y * unit_y
    square_z = unit_z * unit_z
    return [
        -0.4886025119029199 * unit_y,
        0.4886025119029199 * unit_z,
        -0.4886025119029199 * unit_x,
        1.0925484305920792 * unit_x * unit_y,
        -1.0925484305920792 * unit_y * unit_z,
        0.31539156525252005 * (2.0 * square_z - square_x - square_y),
        -1.0925484305920792 * unit_x * unit_z,
        0.5462742152960396 * (square_x - square_y),
        -0.5900435899266435 * unit_y * (3.0 * square_x - square_y),
        2.890611442640554 * unit_x * unit_y * unit_z,
        -0.4570457994644658 * unit_y * (4.0 * square_z - square_x - square_y),
        0.3731763325901154 * unit_z * (2.0 * square_z - 3.0 * square_x - 3.0 * square_y),
        -0.4570457994644658 * unit_x * (4.0 * square_z - square_x - square_y),
        1.445305721320277 * unit_z * (square_x - square_y),
        -0.5900435899266435 * unit_x * (square_x - 3.0 * square_y),
    ]


HARMONIC_0 = 0.28209479177387814


def camera_frame(camera):
    inverse_norm = 1.0 / jnp.sqrt(
        1.0 + camera[0] * camera[0] + camera[1] * camera[1] + camera[2] * camera[2]
    )
    rotation = rotation_matrix(
        inverse_norm, camera[0] * inverse_norm, camera[1] * inverse_norm, camera[2] * inverse_norm
    )
    shift = [camera[3], camera[4], camera[5]]
    centre = [
        -(rotation[0][i] * shift[0] + rotation[1][i] * shift[1] + rotation[2][i] * shift[2])
        for i in range(3)
    ]
    return [rotation[i][j] for i in range(3) for j in range(3)] + shift + centre


def shape_factor(scales, quaternion):
    inverse_norm = 1.0 / jnp.sqrt(sum(entry * entry for entry in quaternion))
    own = rotation_matrix(*[entry * inverse_norm for entry in quaternion])
    widths = [jnp.exp(entry) for entry in scales]
    return [own[i][j] * widths[j] for i in range(3) for j in range(3)]


def view_of(centers, factor, frame, focal_length, centre_x, centre_y):
    rotation = [frame[3 * i : 3 * i + 3] for i in range(3)]
    shift = frame[9:12]
    origin = frame[12:15]
    in_view = [
        rotation[i][0] * centers[0]
        + rotation[i][1] * centers[1]
        + rotation[i][2] * centers[2]
        + shift[i]
        for i in range(3)
    ]
    inverse_depth = 1.0 / in_view[2]
    near = focal_length * inverse_depth
    ratio_x = in_view[0] * inverse_depth
    ratio_y = in_view[1] * inverse_depth
    screen = [
        [near * (rotation[0][j] - ratio_x * rotation[2][j]) for j in range(3)],
        [near * (rotation[1][j] - ratio_y * rotation[2][j]) for j in range(3)],
    ]
    spread = [
        [sum(screen[a][j] * factor[3 * j + k] for j in range(3)) for k in range(3)]
        for a in range(2)
    ]
    variance_x = sum(spread[0][k] * spread[0][k] for k in range(3)) + 0.3
    covariance = sum(spread[0][k] * spread[1][k] for k in range(3))
    variance_y = sum(spread[1][k] * spread[1][k] for k in range(3)) + 0.3
    inverse_determinant = 1.0 / (variance_x * variance_y - covariance * covariance)
    toward = [centers[i] - origin[i] for i in range(3)]
    inverse_length = 1.0 / jnp.sqrt(
        toward[0] * toward[0] + toward[1] * toward[1] + toward[2] * toward[2]
    )
    basis = harmonic_basis(*[entry * inverse_length for entry in toward])
    return [
        focal_length * ratio_x + centre_x,
        focal_length * ratio_y + centre_y,
        variance_y * inverse_determinant,
        -covariance * inverse_determinant,
        variance_x * inverse_determinant,
    ] + basis


def colour_sum(basis, harmonic_of, channel):
    summed = 0.5 + HARMONIC_0 * harmonic_of(channel, 0)
    for k in range(15):
        summed = summed + basis[k] * harmonic_of(channel, k + 1)
    return summed


def sigmoid(logit):
    return 1.0 / (1.0 + jnp.exp(-logit))


def features_of(row, camera, focal):
    shape = row(0).shape
    frame = [jnp.broadcast_to(entry, shape) for entry in camera_frame(camera)]
    factor = shape_factor([row(3 + i) for i in range(3)], [row(6 + i) for i in range(4)])
    seen = view_of([row(i) for i in range(3)], factor, frame, *focal)
    colours = [
        jnp.maximum(colour_sum(seen[5:], lambda c, k: row(11 + 16 * c + k), channel), 0.0)
        for channel in range(3)
    ]
    return seen[:5] + [sigmoid(row(10))] + colours


def halves_of(gauss_ref):
    return lambda k: jnp.concatenate(
        [gauss_ref[k, :, half * LANES : (half + 1) * LANES] for half in range(HALVES)], axis=0
    )


def pick(visible_ref, owned):
    base = lax.axis_index("cell") * owned
    place = lax.broadcasted_iota(jnp.int32, (owned, LANES), 0)
    masks = [place == visible_ref[0, sub] - base for sub in range(2)]
    return lambda value: [
        jnp.sum(
            jnp.where(mask, value[half * owned : (half + 1) * owned], 0.0), axis=0, keepdims=True
        )
        for mask in masks
        for half in range(HALVES)
    ]


def camera_rows(camera_ref):
    return [jnp.full((1, LANES), camera_ref[0, i], F32) for i in range(6)]


def project_kernel(focal, visible_ref, camera_ref, gauss_ref, out_ref):
    features = features_of(halves_of(gauss_ref), camera_rows(camera_ref), focal)
    picked = pick(visible_ref, gauss_ref.shape[1])
    for f in range(FEATURES):
        out_ref[0, f] = jnp.concatenate(picked(features[f]), axis=0)
    message = out_ref[0]
    for i in range(1, out_ref.shape[0]):
        out_ref[i] = message


def slope_kernel(focal, visible_ref, camera_ref, gauss_ref, out_ref):
    camera = camera_rows(camera_ref)
    whole = halves_of(gauss_ref)
    picked = pick(visible_ref, gauss_ref.shape[1])
    held = [jnp.concatenate(picked(whole(k)), axis=0) for k in range(gauss_ref.shape[0])]
    for i in range(6):
        tangents = [jnp.full((1, LANES), 1.0 if j == i else 0.0, F32) for j in range(6)]
        _, slopes = jax.jvp(
            lambda *entries: features_of(held.__getitem__, entries, focal), camera, tangents
        )
        for f in range(FEATURES):
            out_ref[i, f] = slopes[f]


def split(value):
    high = value.astype(BF16)
    return high, (value - high.astype(F32)).astype(BF16)


def dot(left, right):
    return jnp.dot(left, right, preferred_element_type=F32)


def both_dots(pair, right):
    return dot(pair[0], right) + dot(pair[1], right)


def transpose_dot(left, right):
    return lax.dot_general(
        left, right, (((1,), (1,)), ((), ())), preferred_element_type=F32
    )


def stacked(value, rows):
    high, low = split(value)
    return jnp.concatenate(
        [high.astype(F32), low.astype(F32), jnp.zeros((rows - 6, value.shape[1]), F32)], axis=0
    ).astype(BF16)


def render_kernel(
    order_ref,
    length_ref,
    tile_ref,
    target_ref,
    near_ref,
    far_ref,
    near_out,
    far_out,
    feature_scr,
    rgb_scr,
    weight_scr,
    high_scr,
    low_scr,
    ratio_scr,
):
    slots = order_ref.shape[1]
    core = lax.rem(lax.axis_index("cell"), CORES)
    near_out[...] = jnp.zeros_like(near_out)
    far_out[...] = jnp.zeros_like(far_out)
    first = lax.broadcasted_iota(jnp.int32, (BLOCK, BLOCK), 0)
    second = lax.broadcasted_iota(jnp.int32, (BLOCK, BLOCK), 1)
    earlier = (first < second).astype(BF16)
    later = (first > second).astype(BF16)
    step_x = lax.broadcasted_iota(jnp.int32, (TILE, BLOCK), 0).astype(F32) - 7.5
    part = lax.broadcasted_iota(jnp.int32, (8, LANES), 0)
    targets = target_ref[...].astype(F32)

    places = []
    for slot in range(slots):
        tile = tile_ref[0, slot]
        places.append(
            (
                (lax.rem(tile, 16) * TILE + 8).astype(F32),
                (lax.div(tile, 16) * TILE + 8).astype(F32),
            )
        )
    longest = functools.reduce(jnp.maximum, [length_ref[0, slot] for slot in range(slots)])

    def owner(slot, k):
        block = order_ref[0, slot, k]
        on_near = lax.rem(lax.div(block, 2), CORES) == core
        return lax.div(block, 4), on_near, lax.rem(block, 2)

    def forward(k, carry):
        remains, colours = carry
        alphas, keeps = [], []
        for slot in range(slots):
            chip, on_near, side = owner(slot, k)
            for f in range(FEATURES):
                entry = jnp.where(on_near, near_ref[chip, f], far_ref[chip, f])
                entry = jnp.where(side == 0, entry[0:2], entry[2:4])
                feature_scr[slot, k, f : f + 1, 0:LANES] = entry[0:1]
                feature_scr[slot, k, f : f + 1, LANES:] = entry[1:2]
            feature = feature_scr.at[slot, k]
            rgb_scr[slot, k] = stacked(feature[6:9, :], 16)
            delta_x = step_x - (feature[0:1, :] - places[slot][0])
            local_y = feature[1:2, :] - places[slot][1]
            curve_x = (-0.5 * LOG2E) * feature[2:3, :] * delta_x * delta_x
            cross_x = (-LOG2E) * feature[3:4, :] * delta_x
            curve = (-0.5 * LOG2E) * feature[4:5, :]
            opacity = jnp.where(k < length_ref[0, slot], feature[5:6, :], 0.0)
            rows = []
            for i in range(TILE):
                delta_y = (i - 7.5) - local_y
                rows.append(curve_x + (cross_x * delta_y + curve * delta_y * delta_y))
            alpha = opacity * jnp.exp2(jnp.concatenate(rows, axis=0))
            keep = alpha * (
                -LOG2E
                - alpha * (LOG2E / 2.0 + alpha * (LOG2E / 3.0 + alpha * (LOG2E / 4.0)))
            )
            ratio_scr[slot, k] = alpha * jnp.exp2(-keep)
            alphas.append(alpha)
            keeps.append(keep)
        inner = [both_dots(split(keep), earlier) for keep in keeps]
        new_remains, new_colours = [], []
        for slot in range(slots):
            before = inner[slot] + remains[slot]
            weight = alphas[slot] * jnp.exp2(before)
            weight_scr[slot, k] = weight
            high, low = split(weight)
            high_scr[slot, k] = high
            low_scr[slot, k] = low
            rgb = rgb_scr[slot, k]
            new_remains.append(before[:, BLOCK - 1 :] + keeps[slot][:, BLOCK - 1 :])
            new_colours.append(
                colours[slot] + transpose_dot(rgb, high) + transpose_dot(rgb, low)
            )
        return tuple(new_remains), tuple(new_colours)

    zero = (jnp.zeros((PIX, 1), F32),) * slots
    _, colours = lax.fori_loop(
        0, longest, forward, (zero, (jnp.zeros((16, PIX), F32),) * slots)
    )
    misfit_rows, misfit_cols = [], []
    for slot in range(slots):
        misfit = colours[slot][0:3] + colours[slot][3:6] - targets[0, slot]
        misfit_rows.append(stacked(misfit, 16))
        turned = jnp.concatenate([misfit, jnp.zeros((5, PIX), F32)], axis=0).T
        misfit_cols.append([turned[:, c : c + 1] for c in range(3)])

    def backward(step, behind):
        k = longest - 1 - step
        throughs = []
        for slot in range(slots):
            feature = feature_scr.at[slot, k]
            throughs.append(
                weight_scr[slot, k]
                * sum(misfit_cols[slot][c] * feature[6 + c : 7 + c, :] for c in range(3))
            )
        inner = [both_dots(split(through), later) for through in throughs]
        new_behind = []
        for slot in range(slots):
            feature = feature_scr.at[slot, k]
            chip, on_near, side = owner(slot, k)
            after = inner[slot] + behind[slot]
            slope = throughs[slot] - after * ratio_scr[slot, k]
            new_behind.append(after[:, 0:1] + throughs[slot][:, 0:1])
            flat = jnp.zeros((TILE, BLOCK), F32)
            tilt = jnp.zeros((TILE, BLOCK), F32)
            bend = jnp.zeros((TILE, BLOCK), F32)
            for i in range(TILE // 2):
                top = slope[i * TILE : (i + 1) * TILE]
                bottom = slope[(TILE - 1 - i) * TILE : (TILE - i) * TILE]
                away = 7.5 - i
                flat = flat + (top + bottom)
                tilt = tilt + away * (bottom - top)
                bend = bend + (away * away) * (top + bottom)
            colour_grad = dot(misfit_rows[slot], high_scr[slot, k]) + dot(
                misfit_rows[slot], low_scr[slot, k]
            )
            delta_x = step_x - (feature[0:1, :] - places[slot][0])
            local_y = feature[1:2, :] - places[slot][1]
            mean = tilt - local_y * flat
            bend = bend - local_y * (tilt + mean)

            def across(value):
                return jnp.sum(value, axis=0, keepdims=True)

            total, mean_x, mean_y = across(flat), across(delta_x * flat), across(mean)
            square_x = across(delta_x * delta_x * flat)
            mixed = across(delta_x * mean)
            square_y = across(bend)
            conic_x, conic_xy, conic_y = feature[2:3, :], feature[3:4, :], feature[4:5, :]
            grads = [
                conic_x * mean_x + conic_xy * mean_y,
                conic_y * mean_y + conic_xy * mean_x,
                -0.5 * square_x,
                -mixed,
                -0.5 * square_y,
                total / feature[5:6, :],
            ] + [colour_grad[i : i + 1] + colour_grad[i + 3 : i + 4] for i in range(3)]
            spots, placed = [], []
            for f in range(FEATURES):
                spot = chip * FEATURES + f
                at = lax.rem(spot, 2) * ROWS + side * 2
                spots.append(lax.div(spot, 2))
                placed.append(
                    jnp.where(
                        part == at,
                        grads[f][:, :LANES],
                        jnp.where(part == at + 1, grads[f][:, LANES:], 0.0),
                    )
                )

            @pl.when(on_near)
            def _():
                for f in range(FEATURES):
                    near_out[spots[f]] += placed[f]

            @pl.when(jnp.logical_not(on_near))
            def _():
                for f in range(FEATURES):
                    far_out[spots[f]] += placed[f]

        return tuple(new_behind)

    lax.fori_loop(0, longest, backward, zero)


def render_scratch(slots, depth):
    return [
        pltpu.VMEM((slots, depth, 16, BLOCK), F32),
        pltpu.VMEM((slots, depth, 16, BLOCK), BF16),
        pltpu.VMEM((slots, depth, PIX, BLOCK), F32),
        pltpu.VMEM((slots, depth, PIX, BLOCK), BF16),
        pltpu.VMEM((slots, depth, PIX, BLOCK), BF16),
        pltpu.VMEM((slots, depth, PIX, BLOCK), F32),
    ]


def collect_kernel(owned, visible_ref, camera_ref, parts_ref, slope_ref, out_ref, camera_out):
    base = lax.axis_index("cell") * owned
    paired = parts_ref[0:FEATURES]
    for i in range(1, parts_ref.shape[0] // FEATURES):
        paired = paired + parts_ref[i * FEATURES : (i + 1) * FEATURES]
    pieces = [paired[i // 2, (i % 2) * ROWS : (i % 2 + 1) * ROWS] for i in range(2 * FEATURES)]
    total = [pieces[f] + pieces[FEATURES + f] for f in range(FEATURES)]
    for f in range(FEATURES):
        out_ref[0, f] = total[f]
    base_rows = [jnp.full((1, LANES), camera_ref[0, i], F32) for i in range(6)] + [
        jnp.full((1, LANES), (visible_ref[0, sub] - base).astype(F32), F32) for sub in range(2)
    ]
    for i in range(2):
        out_ref[0, FEATURES + i] = jnp.concatenate(base_rows[4 * i : 4 * i + 4], axis=0)
    message = out_ref[0]
    for i in range(1, out_ref.shape[0]):
        out_ref[i] = message
    lane = lax.broadcasted_iota(jnp.int32, (1, LANES), 1)
    packed = jnp.zeros((1, LANES), F32)
    for i in range(6):
        across = jnp.sum(
            sum(total[f] * slope_ref[i, f] for f in range(FEATURES)), axis=0, keepdims=True
        )
        packed = packed + jnp.where(lane == i, jnp.sum(across, axis=1, keepdims=True), 0.0)
    for i in range(camera_out.shape[0]):
        camera_out[i] = packed


def update_kernel(
    focal,
    parts_ref,
    gauss_ref,
    first_ref,
    second_ref,
    gauss_out,
    first_out,
    second_out,
    factor_scr,
    sum_scr,
):
    params, owned = gauss_ref.shape[0], gauss_ref.shape[1]
    views = parts_ref.shape[0]
    place = lax.broadcasted_iota(jnp.int32, (owned, LANES), 0).astype(F32)
    whole = (owned, LANES)
    for half in range(HALVES):
        lanes = slice(half * LANES, (half + 1) * LANES)

        def row(k, lanes=lanes):
            return gauss_ref[k, :, lanes]

        factor, factor_pull = jax.vjp(
            shape_factor,
            [row(3 + i) for i in range(3)],
            [row(6 + i) for i in range(4)],
        )
        for i in range(9):
            factor_scr[i] = factor[i]
        sum_scr[...] = jnp.zeros_like(sum_scr)

        def one_view(view, carry):
            def message(f, r):
                return parts_ref[view, f, r : r + 1, :]

            masks = [place == message(FEATURES + 1, 2 + sub) for sub in range(2)]
            screen = [
                sum(
                    jnp.where(masks[sub], message(f, sub * 2 + half), 0.0)
                    for sub in range(2)
                )
                for f in range(FEATURES)
            ]
            frame = [
                jnp.broadcast_to(entry, whole)
                for entry in camera_frame([message(FEATURES + i // 4, i % 4) for i in range(6)])
            ]
            seen, pull = jax.vjp(
                lambda centers, factor: view_of(centers, factor, frame, *focal),
                [row(i) for i in range(3)],
                [factor_scr[i] for i in range(9)],
            )
            basis = seen[5:]
            basis_grad = [jnp.zeros(whole, F32)] * 15
            for channel in range(3):
                first_row = 11 + 16 * channel
                summed = colour_sum(basis, lambda c, k: row(11 + 16 * c + k), channel)
                gate = jnp.where(summed > 0.0, 1.0, jnp.where(summed == 0.0, 0.5, 0.0))
                colour = screen[6 + channel] * gate
                sum_scr[first_row] += HARMONIC_0 * colour
                for k in range(15):
                    basis_grad[k] = basis_grad[k] + colour * row(first_row + 1 + k)
                    sum_scr[first_row + 1 + k] += colour * basis[k]
            centre_grad, factor_grad = pull(screen[:5] + basis_grad)
            for i in range(3):
                sum_scr[i] += centre_grad[i]
            sum_scr[10] += screen[5]
            for i in range(9):
                sum_scr[params + i] += factor_grad[i]
            return carry

        lax.fori_loop(0, views, one_view, 0)
        scale_grad, quaternion_grad = factor_pull([sum_scr[params + i] for i in range(9)])
        opacity = sigmoid(row(10))
        for i in range(3):
            sum_scr[3 + i] = scale_grad[i]
        for i in range(4):
            sum_scr[6 + i] = quaternion_grad[i]
        sum_scr[10] = sum_scr[10] * opacity * (1.0 - opacity)
        for k in range(params):
            gradient = sum_scr[k]
            moment = 0.9 * first_ref[k, :, lanes] + 0.1 * gradient
            second = 0.999 * second_ref[k, :, lanes] + 0.001 * gradient * gradient
            first_out[k, :, lanes] = moment
            second_out[k, :, lanes] = second
            gauss_out[k, :, lanes] = row(k) - (0.05 / (1.0 - 0.9**10)) * moment / (
                jnp.sqrt(second * (1.0 / (1.0 - 0.999**10))) + 1e-08
            )


VMEM = pl.BlockSpec(memory_space=pltpu.VMEM)
SMEM = pl.BlockSpec(memory_space=pltpu.SMEM)
PARAMETERS = pltpu.CompilerParams(vmem_limit_bytes=40 * 1024 * 1024)


def shards(
    gaussians,
    first_moment,
    second_moment,
    cameras,
    visible_blocks,
    tile_ids,
    tile_order,
    tile_length,
    targets,
):
    owned, params = gaussians.shape[0], gaussians.shape[1]
    gaussians, first_moment, second_moment = (
        array.transpose(1, 0, 2) for array in (gaussians, first_moment, second_moment)
    )
    cells = lax.axis_size("cell")
    views = lax.axis_size("view")
    chips = cells // CORES
    tile_total = cells * tile_ids.shape[1]
    focal = (16.0 * TILE, 8.0 * TILE, tile_total * TILE / 32.0)
    same_core = [[chip * CORES + core for chip in range(chips)] for core in range(CORES)]
    swap = [(cell, cell ^ 1) for cell in range(cells)]

    with jax.named_scope("project"):
        message = pl.pallas_call(
            lambda *refs: project_kernel(focal, *refs),
            out_shape=jax.ShapeDtypeStruct((chips, FEATURES, ROWS, LANES), F32),
            in_specs=[SMEM, SMEM, VMEM],
            out_specs=VMEM,
            compiler_params=PARAMETERS,
            name="project",
        )(visible_blocks, cameras, gaussians)
        slopes = pl.pallas_call(
            lambda *refs: slope_kernel(focal, *refs),
            out_shape=jax.ShapeDtypeStruct((6, FEATURES, ROWS, LANES), F32),
            in_specs=[SMEM, SMEM, VMEM],
            out_specs=VMEM,
            compiler_params=PARAMETERS,
            cost_estimate=pl.CostEstimate(
                flops=4_000_000, bytes_accessed=200_000, transcendentals=10_000
            ),
            name="slope",
        )(visible_blocks, cameras, gaussians)
    with jax.named_scope("gather"):
        near = lax.all_to_all(message, "cell", 0, 0, axis_index_groups=same_core, tiled=True)
        far = lax.ppermute(near, "cell", swap)
    with jax.named_scope("render"):
        near_grad, far_grad = pl.pallas_call(
            render_kernel,
            out_shape=[jax.ShapeDtypeStruct((chips * FEATURES * ROWS // 8, 8, LANES), F32)] * 2,
            in_specs=[SMEM, SMEM, SMEM, VMEM, VMEM, VMEM],
            out_specs=[VMEM, VMEM],
            scratch_shapes=render_scratch(*tile_order.shape[1:]),
            compiler_params=PARAMETERS,
            name="render",
        )(tile_order, tile_length, tile_ids, targets, near, far)
    with jax.named_scope("scatter"):
        pair = near_grad + lax.ppermute(far_grad, "cell", swap)
        parts = lax.all_to_all(
            pair.reshape(near.shape), "cell", 0, 0, axis_index_groups=same_core, tiled=True)
    with jax.named_scope("collect"):
        own, camera_part = pl.pallas_call(
            lambda *refs: collect_kernel(owned, *refs),
            out_shape=[
                jax.ShapeDtypeStruct((views, VIEW_MSG, ROWS, LANES), F32),
                jax.ShapeDtypeStruct((1, 1, LANES), F32),
            ],
            in_specs=[SMEM, SMEM, VMEM, VMEM],
            out_specs=[VMEM, VMEM],
            compiler_params=PARAMETERS,
            name="collect",
        )(visible_blocks, cameras, parts.reshape(pair.shape), slopes)
        every = lax.all_to_all(own, "view", 0, 0, tiled=True)
    with jax.named_scope("camera"):
        camera_pair = camera_part + lax.ppermute(camera_part, "cell", swap)
        every, camera_pair = lax.optimization_barrier((every, camera_pair))
        camera_parts = lax.all_to_all(
            jnp.broadcast_to(camera_pair, (chips, 1, LANES)),
            "cell",
            0,
            0,
            axis_index_groups=same_core,
            tiled=True,
        )
    with jax.named_scope("update"):
        state = jax.ShapeDtypeStruct(gaussians.shape, F32)
        new_gaussians, new_first, new_second = pl.pallas_call(
            lambda *refs: update_kernel(focal, *refs),
            out_shape=[state, state, state],
            in_specs=[VMEM] * 4,
            out_specs=[VMEM] * 3,
            scratch_shapes=[
                pltpu.VMEM((9, owned, LANES), F32),
                pltpu.VMEM((params + 9, owned, LANES), F32),
            ],
            compiler_params=PARAMETERS,
            name="update",
        )(every, gaussians, first_moment, second_moment)
    with jax.named_scope("camera"):
        camera_total = jnp.sum(camera_parts, axis=0)[:, :6]
    return (
        new_gaussians.transpose(1, 0, 2),
        new_first.transpose(1, 0, 2),
        new_second.transpose(1, 0, 2),
        camera_total,
    )


def solution(mesh):
    return jax.shard_map(
        shards,
        mesh=mesh,
        in_specs=(
            P("cell", None, None),
            P("cell", None, None),
            P("cell", None, None),
            P("view", None),
            P("view", "cell"),
            P("view", "cell"),
            P("view", "cell", None),
            P("view", "cell"),
            P("view", "cell", None, None),
        ),
        out_specs=(
            P("cell", None, None),
            P("cell", None, None),
            P("cell", None, None),
            P("view", None),
        ),
        check_vma=False,
    )
```

```python
import functools

import jax
import jax.numpy as jnp
from jax import lax
from jax.experimental import pallas as pl
from jax.experimental.pallas import tpu as pltpu
from jax.sharding import PartitionSpec as P

TILE = 16
PIX = 256
BLOCK = 256
LANES = 128
HALVES = 2
FEATURES = 9
CORES = 2
ROWS = 4
VIEW_MSG = 10
LOG2E = 1.4426950408889634
F32 = jnp.float32
BF16 = jnp.bfloat16


def rotation_matrix(real_part, axis_x, axis_y, axis_z):
    return [
        [
            1.0 - 2.0 * (axis_y * axis_y + axis_z * axis_z),
            2.0 * (axis_x * axis_y - real_part * axis_z),
            2.0 * (axis_x * axis_z + real_part * axis_y),
        ],
        [
            2.0 * (axis_x * axis_y + real_part * axis_z),
            1.0 - 2.0 * (axis_x * axis_x + axis_z * axis_z),
            2.0 * (axis_y * axis_z - real_part * axis_x),
        ],
        [
            2.0 * (axis_x * axis_z - real_part * axis_y),
            2.0 * (axis_y * axis_z + real_part * axis_x),
            1.0 - 2.0 * (axis_x * axis_x + axis_y * axis_y),
        ],
    ]


def harmonic_basis(unit_x, unit_y, unit_z):
    square_x = unit_x * unit_x
    square_y = unit_y * unit_y
    square_z = unit_z * unit_z
    return [
        -0.4886025119029199 * unit_y,
        0.4886025119029199 * unit_z,
        -0.4886025119029199 * unit_x,
        1.0925484305920792 * unit_x * unit_y,
        -1.0925484305920792 * unit_y * unit_z,
        0.31539156525252005 * (2.0 * square_z - square_x - square_y),
        -1.0925484305920792 * unit_x * unit_z,
        0.5462742152960396 * (square_x - square_y),
        -0.5900435899266435 * unit_y * (3.0 * square_x - square_y),
        2.890611442640554 * unit_x * unit_y * unit_z,
        -0.4570457994644658 * unit_y * (4.0 * square_z - square_x - square_y),
        0.3731763325901154 * unit_z * (2.0 * square_z - 3.0 * square_x - 3.0 * square_y),
        -0.4570457994644658 * unit_x * (4.0 * square_z - square_x - square_y),
        1.445305721320277 * unit_z * (square_x - square_y),
        -0.5900435899266435 * unit_x * (square_x - 3.0 * square_y),
    ]


HARMONIC_0 = 0.28209479177387814


def camera_frame(camera):
    inverse_norm = 1.0 / jnp.sqrt(
        1.0 + camera[0] * camera[0] + camera[1] * camera[1] + camera[2] * camera[2]
    )
    rotation = rotation_matrix(
        inverse_norm, camera[0] * inverse_norm, camera[1] * inverse_norm, camera[2] * inverse_norm
    )
    shift = [camera[3], camera[4], camera[5]]
    centre = [
        -(rotation[0][i] * shift[0] + rotation[1][i] * shift[1] + rotation[2][i] * shift[2])
        for i in range(3)
    ]
    return [rotation[i][j] for i in range(3) for j in range(3)] + shift + centre


def shape_factor(scales, quaternion):
    inverse_norm = 1.0 / jnp.sqrt(sum(entry * entry for entry in quaternion))
    own = rotation_matrix(*[entry * inverse_norm for entry in quaternion])
    widths = [jnp.exp(entry) for entry in scales]
    return [own[i][j] * widths[j] for i in range(3) for j in range(3)]


def view_of(centers, factor, frame, focal_length, centre_x, centre_y):
    rotation = [frame[3 * i : 3 * i + 3] for i in range(3)]
    shift = frame[9:12]
    origin = frame[12:15]
    in_view = [
        rotation[i][0] * centers[0]
        + rotation[i][1] * centers[1]
        + rotation[i][2] * centers[2]
        + shift[i]
        for i in range(3)
    ]
    inverse_depth = 1.0 / in_view[2]
    near = focal_length * inverse_depth
    ratio_x = in_view[0] * inverse_depth
    ratio_y = in_view[1] * inverse_depth
    screen = [
        [near * (rotation[0][j] - ratio_x * rotation[2][j]) for j in range(3)],
        [near * (rotation[1][j] - ratio_y * rotation[2][j]) for j in range(3)],
    ]
    spread = [
        [sum(screen[a][j] * factor[3 * j + k] for j in range(3)) for k in range(3)]
        for a in range(2)
    ]
    variance_x = sum(spread[0][k] * spread[0][k] for k in range(3)) + 0.3
    covariance = sum(spread[0][k] * spread[1][k] for k in range(3))
    variance_y = sum(spread[1][k] * spread[1][k] for k in range(3)) + 0.3
    inverse_determinant = 1.0 / (variance_x * variance_y - covariance * covariance)
    toward = [centers[i] - origin[i] for i in range(3)]
    inverse_length = 1.0 / jnp.sqrt(
        toward[0] * toward[0] + toward[1] * toward[1] + toward[2] * toward[2]
    )
    basis = harmonic_basis(*[entry * inverse_length for entry in toward])
    return [
        focal_length * ratio_x + centre_x,
        focal_length * ratio_y + centre_y,
        variance_y * inverse_determinant,
        -covariance * inverse_determinant,
        variance_x * inverse_determinant,
    ] + basis


def colour_sum(basis, harmonic_of, channel):
    summed = 0.5 + HARMONIC_0 * harmonic_of(channel, 0)
    for k in range(15):
        summed = summed + basis[k] * harmonic_of(channel, k + 1)
    return summed


def sigmoid(logit):
    return 1.0 / (1.0 + jnp.exp(-logit))


def features_of(row, camera, focal):
    shape = row(0).shape
    frame = [jnp.broadcast_to(entry, shape) for entry in camera_frame(camera)]
    factor = shape_factor([row(3 + i) for i in range(3)], [row(6 + i) for i in range(4)])
    seen = view_of([row(i) for i in range(3)], factor, frame, *focal)
    colours = [
        jnp.maximum(colour_sum(seen[5:], lambda c, k: row(11 + 16 * c + k), channel), 0.0)
        for channel in range(3)
    ]
    return seen[:5] + [sigmoid(row(10))] + colours


def halves_of(gauss_ref):
    return lambda k: jnp.concatenate(
        [gauss_ref[k, :, half * LANES : (half + 1) * LANES] for half in range(HALVES)], axis=0
    )


def pick(visible_ref, owned):
    base = lax.axis_index("cell") * owned
    place = lax.broadcasted_iota(jnp.int32, (owned, LANES), 0)
    masks = [place == visible_ref[0, sub] - base for sub in range(2)]
    return lambda value: [
        jnp.sum(
            jnp.where(mask, value[half * owned : (half + 1) * owned], 0.0), axis=0, keepdims=True
        )
        for mask in masks
        for half in range(HALVES)
    ]


def camera_rows(camera_ref):
    return [jnp.full((1, LANES), camera_ref[0, i], F32) for i in range(6)]


def project_kernel(
    focal,
    visible_any,
    camera_any,
    gauss_any,
    out_ref,
    extra_ref,
    visible_ref,
    camera_ref,
    gauss_ref,
    small_done,
    large_done,
):
    small = [
        pltpu.make_async_copy(visible_any, visible_ref, small_done.at[0]),
        pltpu.make_async_copy(camera_any, camera_ref, small_done.at[1]),
    ]
    cuts = [0, 11, 27, 43, 59]
    large = [
        pltpu.make_async_copy(
            gauss_any.at[low:high], gauss_ref.at[low:high], large_done.at[i]
        )
        for i, (low, high) in enumerate(zip(cuts[:-1], cuts[1:]))
    ]
    for copy in small + large:
        copy.start()
    for copy in small:
        copy.wait()
    owned = gauss_ref.shape[1]
    base = lax.axis_index("cell") * owned
    values = [camera_ref[0, i] for i in range(6)] + [
        (visible_ref[0, sub] - base).astype(F32) for sub in range(2)
    ]
    row = lax.broadcasted_iota(jnp.int32, (ROWS, LANES), 0)
    lane = lax.broadcasted_iota(jnp.int32, (ROWS, LANES), 1)
    place = row + jnp.where(lane < LANES // 2, 0, ROWS)
    extra = jnp.zeros((ROWS, LANES), F32)
    for i, value in enumerate(values):
        extra = jnp.where(place == i, value, extra)
    extra_ref[...] = extra
    for copy in large:
        copy.wait()
    features = features_of(halves_of(gauss_ref), camera_rows(camera_ref), focal)
    picked = pick(visible_ref, owned)
    for f in range(FEATURES):
        out_ref[0, f] = jnp.concatenate(picked(features[f]), axis=0)
    message = out_ref[0]
    for i in range(1, out_ref.shape[0]):
        out_ref[i] = message


def slope_kernel(focal, visible_ref, camera_ref, gauss_ref, out_ref):
    camera = camera_rows(camera_ref)
    whole = halves_of(gauss_ref)
    picked = pick(visible_ref, gauss_ref.shape[1])
    held = [jnp.concatenate(picked(whole(k)), axis=0) for k in range(gauss_ref.shape[0])]
    for i in range(6):
        tangents = [jnp.full((1, LANES), 1.0 if j == i else 0.0, F32) for j in range(6)]
        _, slopes = jax.jvp(
            lambda *entries: features_of(held.__getitem__, entries, focal), camera, tangents
        )
        for f in range(FEATURES):
            out_ref[i, f] = slopes[f]


def split(value):
    high = value.astype(BF16)
    return high, (value - high.astype(F32)).astype(BF16)


def dot(left, right):
    return jnp.dot(left, right, preferred_element_type=F32)


def both_dots(pair, right):
    return dot(pair[0], right) + dot(pair[1], right)


def transpose_dot(left, right):
    return lax.dot_general(
        left, right, (((1,), (1,)), ((), ())), preferred_element_type=F32
    )


def stacked(value, rows):
    high, low = split(value)
    return jnp.concatenate(
        [high.astype(F32), low.astype(F32), jnp.zeros((rows - 6, value.shape[1]), F32)], axis=0
    ).astype(BF16)


def render_kernel(
    order_ref,
    length_ref,
    tile_ref,
    target_ref,
    near_ref,
    far_ref,
    extra_ref,
    near_out,
    far_out,
    extra_out,
    feature_scr,
    rgb_scr,
    weight_scr,
    high_scr,
    low_scr,
    ratio_scr,
):
    slots, depth = order_ref.shape[1], order_ref.shape[2]
    core = lax.rem(lax.axis_index("cell"), CORES)
    extra_out[...] = extra_ref[...]
    near_out[...] = jnp.zeros_like(near_out)
    far_out[...] = jnp.zeros_like(far_out)
    first = lax.broadcasted_iota(jnp.int32, (BLOCK, BLOCK), 0)
    second = lax.broadcasted_iota(jnp.int32, (BLOCK, BLOCK), 1)
    earlier = (first < second).astype(BF16)
    later = (first > second).astype(BF16)
    step_x = lax.broadcasted_iota(jnp.int32, (TILE, BLOCK), 0).astype(F32) - 7.5
    part = lax.broadcasted_iota(jnp.int32, (8, LANES), 0)
    targets = target_ref[...].astype(F32)

    places = []
    for slot in range(slots):
        tile = tile_ref[0, slot]
        places.append(
            (
                (lax.rem(tile, 16) * TILE + 8).astype(F32),
                (lax.div(tile, 16) * TILE + 8).astype(F32),
            )
        )
    def owner(slot, k):
        block = order_ref[0, slot, k]
        on_near = lax.rem(lax.div(block, 2), CORES) == core
        return lax.div(block, 4), on_near, lax.rem(block, 2)

    def forward(k, carry):
        remains, colours = carry
        alphas, keeps = [], []
        for slot in range(slots):
            chip, on_near, side = owner(slot, k)
            for f in range(FEATURES):
                entry = jnp.where(on_near, near_ref[chip, f], far_ref[chip, f])
                entry = jnp.where(side == 0, entry[0:2], entry[2:4])
                feature_scr[slot, k, f : f + 1, 0:LANES] = entry[0:1]
                feature_scr[slot, k, f : f + 1, LANES:] = entry[1:2]
            feature = feature_scr.at[slot, k]
            rgb_scr[slot, k] = stacked(feature[6:9, :], 16)
            delta_x = step_x - (feature[0:1, :] - places[slot][0])
            local_y = feature[1:2, :] - places[slot][1]
            curve_x = (-0.5 * LOG2E) * feature[2:3, :] * delta_x * delta_x
            cross_x = (-LOG2E) * feature[3:4, :] * delta_x
            curve = (-0.5 * LOG2E) * feature[4:5, :]
            opacity = jnp.where(k < length_ref[0, slot], feature[5:6, :], 0.0)
            rows = []
            for i in range(TILE):
                delta_y = (i - 7.5) - local_y
                rows.append(curve_x + (cross_x * delta_y + curve * delta_y * delta_y))
            alpha = opacity * jnp.exp2(jnp.concatenate(rows, axis=0))
            keep = alpha * (
                -LOG2E
                - alpha * (LOG2E / 2.0 + alpha * (LOG2E / 3.0 + alpha * (LOG2E / 4.0)))
            )
            ratio_scr[slot, k] = alpha * jnp.exp2(-keep)
            alphas.append(alpha)
            keeps.append(keep)
        inner = [both_dots(split(keep), earlier) for keep in keeps]
        new_remains, new_colours = [], []
        for slot in range(slots):
            before = inner[slot] + remains[slot]
            weight = alphas[slot] * jnp.exp2(before)
            weight_scr[slot, k] = weight
            high, low = split(weight)
            high_scr[slot, k] = high
            low_scr[slot, k] = low
            rgb = rgb_scr[slot, k]
            new_remains.append(before[:, BLOCK - 1 :] + keeps[slot][:, BLOCK - 1 :])
            new_colours.append(
                colours[slot] + transpose_dot(rgb, high) + transpose_dot(rgb, low)
            )
        return tuple(new_remains), tuple(new_colours)

    zero = (jnp.zeros((PIX, 1), F32),) * slots
    carry = (zero, (jnp.zeros((16, PIX), F32),) * slots)
    for k in range(depth):
        carry = forward(k, carry)
    colours = carry[1]
    misfit_rows, misfit_cols = [], []
    for slot in range(slots):
        misfit = colours[slot][0:3] + colours[slot][3:6] - targets[0, slot]
        misfit_rows.append(stacked(misfit, 16))
        turned = jnp.concatenate([misfit, jnp.zeros((5, PIX), F32)], axis=0).T
        misfit_cols.append([turned[:, c : c + 1] for c in range(3)])

    def backward(step, behind):
        k = depth - 1 - step
        throughs = []
        for slot in range(slots):
            feature = feature_scr.at[slot, k]
            throughs.append(
                weight_scr[slot, k]
                * sum(misfit_cols[slot][c] * feature[6 + c : 7 + c, :] for c in range(3))
            )
        inner = [both_dots(split(through), later) for through in throughs]
        new_behind = []
        for slot in range(slots):
            feature = feature_scr.at[slot, k]
            chip, on_near, side = owner(slot, k)
            after = inner[slot] + behind[slot]
            slope = throughs[slot] - after * ratio_scr[slot, k]
            new_behind.append(after[:, 0:1] + throughs[slot][:, 0:1])
            flat = jnp.zeros((TILE, BLOCK), F32)
            tilt = jnp.zeros((TILE, BLOCK), F32)
            bend = jnp.zeros((TILE, BLOCK), F32)
            for i in range(TILE // 2):
                top = slope[i * TILE : (i + 1) * TILE]
                bottom = slope[(TILE - 1 - i) * TILE : (TILE - i) * TILE]
                away = 7.5 - i
                flat = flat + (top + bottom)
                tilt = tilt + away * (bottom - top)
                bend = bend + (away * away) * (top + bottom)
            colour_grad = dot(misfit_rows[slot], high_scr[slot, k]) + dot(
                misfit_rows[slot], low_scr[slot, k]
            )
            delta_x = step_x - (feature[0:1, :] - places[slot][0])
            local_y = feature[1:2, :] - places[slot][1]
            mean = tilt - local_y * flat
            bend = bend - local_y * (tilt + mean)

            def across(value):
                return jnp.sum(value, axis=0, keepdims=True)

            total, mean_x, mean_y = across(flat), across(delta_x * flat), across(mean)
            square_x = across(delta_x * delta_x * flat)
            mixed = across(delta_x * mean)
            square_y = across(bend)
            conic_x, conic_xy, conic_y = feature[2:3, :], feature[3:4, :], feature[4:5, :]
            grads = [
                conic_x * mean_x + conic_xy * mean_y,
                conic_y * mean_y + conic_xy * mean_x,
                -0.5 * square_x,
                -mixed,
                -0.5 * square_y,
                total / feature[5:6, :],
            ] + [colour_grad[i : i + 1] + colour_grad[i + 3 : i + 4] for i in range(3)]
            spots, placed = [], []
            for f in range(FEATURES):
                spot = chip * FEATURES + f
                at = lax.rem(spot, 2) * ROWS + side * 2
                spots.append(lax.div(spot, 2))
                placed.append(
                    jnp.where(
                        part == at,
                        grads[f][:, :LANES],
                        jnp.where(part == at + 1, grads[f][:, LANES:], 0.0),
                    )
                )

            for f in range(FEATURES):
                near_out[spots[f]] += jnp.where(on_near, placed[f], 0.0)
                far_out[spots[f]] += jnp.where(on_near, 0.0, placed[f])

        return tuple(new_behind)

    carry = zero
    for k in range(depth):
        carry = backward(k, carry)


def render_scratch(slots, depth):
    return [
        pltpu.VMEM((slots, depth, 16, BLOCK), F32),
        pltpu.VMEM((slots, depth, 16, BLOCK), BF16),
        pltpu.VMEM((slots, depth, PIX, BLOCK), F32),
        pltpu.VMEM((slots, depth, PIX, BLOCK), BF16),
        pltpu.VMEM((slots, depth, PIX, BLOCK), BF16),
        pltpu.VMEM((slots, depth, PIX, BLOCK), F32),
    ]


def collect_kernel(parts_ref, extra_ref, out_ref):
    paired = parts_ref[0:FEATURES]
    for i in range(1, parts_ref.shape[0] // FEATURES):
        paired = paired + parts_ref[i * FEATURES : (i + 1) * FEATURES]
    pieces = [paired[i // 2, (i % 2) * ROWS : (i % 2 + 1) * ROWS] for i in range(2 * FEATURES)]
    for f in range(FEATURES):
        out_ref[0, f] = pieces[f] + pieces[FEATURES + f]
    out_ref[0, FEATURES] = extra_ref[...]
    message = out_ref[0]
    for i in range(1, out_ref.shape[0]):
        out_ref[i] = message


def pose_kernel(own_ref, slope_ref, out_ref):
    lane = lax.broadcasted_iota(jnp.int32, (1, LANES), 1)
    packed = jnp.zeros((1, LANES), F32)
    for i in range(6):
        across = jnp.sum(
            sum(own_ref[0, f] * slope_ref[i, f] for f in range(FEATURES)), axis=0, keepdims=True
        )
        packed = packed + jnp.where(lane == i, jnp.sum(across, axis=1, keepdims=True), 0.0)
    for i in range(out_ref.shape[0]):
        out_ref[i] = packed


def update_kernel(
    focal,
    parts_ref,
    gauss_ref,
    first_ref,
    second_ref,
    gauss_out,
    first_out,
    second_out,
    factor_scr,
    sum_scr,
):
    params, owned = gauss_ref.shape[0], gauss_ref.shape[1]
    views = parts_ref.shape[0]
    place = lax.broadcasted_iota(jnp.int32, (owned, LANES), 0).astype(F32)
    whole = (owned, LANES)
    for half in range(HALVES):
        lanes = slice(half * LANES, (half + 1) * LANES)

        def row(k, lanes=lanes):
            return gauss_ref[k, :, lanes]

        factor, factor_pull = jax.vjp(
            shape_factor,
            [row(3 + i) for i in range(3)],
            [row(6 + i) for i in range(4)],
        )
        for i in range(9):
            factor_scr[i] = factor[i]
        sum_scr[...] = jnp.zeros_like(sum_scr)

        def one_view(view, carry):
            def message(f, r):
                return parts_ref[view, f, r : r + 1, :]

            def extra(i):
                at = i // ROWS * (LANES // 2)
                return jnp.broadcast_to(message(FEATURES, i % ROWS)[:, at : at + 1], (1, LANES))

            masks = [place == extra(6 + sub) for sub in range(2)]
            screen = [
                sum(
                    jnp.where(masks[sub], message(f, sub * 2 + half), 0.0)
                    for sub in range(2)
                )
                for f in range(FEATURES)
            ]
            frame = [
                jnp.broadcast_to(entry, whole)
                for entry in camera_frame([extra(i) for i in range(6)])
            ]
            seen, pull = jax.vjp(
                lambda centers, factor: view_of(centers, factor, frame, *focal),
                [row(i) for i in range(3)],
                [factor_scr[i] for i in range(9)],
            )
            basis = seen[5:]
            basis_grad = [jnp.zeros(whole, F32)] * 15
            for channel in range(3):
                first_row = 11 + 16 * channel
                summed = colour_sum(basis, lambda c, k: row(11 + 16 * c + k), channel)
                gate = jnp.where(summed > 0.0, 1.0, jnp.where(summed == 0.0, 0.5, 0.0))
                colour = screen[6 + channel] * gate
                sum_scr[first_row] += HARMONIC_0 * colour
                for k in range(15):
                    basis_grad[k] = basis_grad[k] + colour * row(first_row + 1 + k)
                    sum_scr[first_row + 1 + k] += colour * basis[k]
            centre_grad, factor_grad = pull(screen[:5] + basis_grad)
            for i in range(3):
                sum_scr[i] += centre_grad[i]
            sum_scr[10] += screen[5]
            for i in range(9):
                sum_scr[params + i] += factor_grad[i]
            return carry

        lax.fori_loop(0, views, one_view, 0)
        scale_grad, quaternion_grad = factor_pull([sum_scr[params + i] for i in range(9)])
        opacity = sigmoid(row(10))
        for i in range(3):
            sum_scr[3 + i] = scale_grad[i]
        for i in range(4):
            sum_scr[6 + i] = quaternion_grad[i]
        sum_scr[10] = sum_scr[10] * opacity * (1.0 - opacity)
        for k in range(params):
            gradient = sum_scr[k]
            moment = 0.9 * first_ref[k, :, lanes] + 0.1 * gradient
            second = 0.999 * second_ref[k, :, lanes] + 0.001 * gradient * gradient
            first_out[k, :, lanes] = moment
            second_out[k, :, lanes] = second
            gauss_out[k, :, lanes] = row(k) - (0.05 / (1.0 - 0.9**10)) * moment / (
                jnp.sqrt(second * (1.0 / (1.0 - 0.999**10))) + 1e-08
            )


VMEM = pl.BlockSpec(memory_space=pltpu.VMEM)
SMEM = pl.BlockSpec(memory_space=pltpu.SMEM)
PARAMETERS = pltpu.CompilerParams(vmem_limit_bytes=40 * 1024 * 1024)


def shards(
    gaussians,
    first_moment,
    second_moment,
    cameras,
    visible_blocks,
    tile_ids,
    tile_order,
    tile_length,
    targets,
):
    owned, params = gaussians.shape[0], gaussians.shape[1]
    gaussians, first_moment, second_moment = (
        array.transpose(1, 0, 2) for array in (gaussians, first_moment, second_moment)
    )
    cells = lax.axis_size("cell")
    views = lax.axis_size("view")
    chips = cells // CORES
    tile_total = cells * tile_ids.shape[1]
    focal = (16.0 * TILE, 8.0 * TILE, tile_total * TILE / 32.0)
    same_core = [[chip * CORES + core for chip in range(chips)] for core in range(CORES)]
    swap = [(cell, cell ^ 1) for cell in range(cells)]

    with jax.named_scope("project"):
        message, extra = pl.pallas_call(
            lambda *refs: project_kernel(focal, *refs),
            out_shape=[
                jax.ShapeDtypeStruct((chips, FEATURES, ROWS, LANES), F32),
                jax.ShapeDtypeStruct((ROWS, LANES), F32),
            ],
            in_specs=[pl.BlockSpec(memory_space=pl.ANY)] * 3,
            out_specs=[VMEM, VMEM],
            scratch_shapes=[
                pltpu.SMEM(visible_blocks.shape, jnp.int32),
                pltpu.SMEM(cameras.shape, F32),
                pltpu.VMEM(gaussians.shape, F32),
                pltpu.SemaphoreType.DMA((2,)),
                pltpu.SemaphoreType.DMA((4,)),
            ],
            compiler_params=pltpu.CompilerParams(vmem_limit_bytes=60 * 1024 * 1024),
            name="project",
        )(visible_blocks, cameras, gaussians)
        slopes = pl.pallas_call(
            lambda *refs: slope_kernel(focal, *refs),
            out_shape=jax.ShapeDtypeStruct((6, FEATURES, ROWS, LANES), F32),
            in_specs=[SMEM, SMEM, VMEM],
            out_specs=VMEM,
            compiler_params=PARAMETERS,
            cost_estimate=pl.CostEstimate(
                flops=4_000_000, bytes_accessed=200_000, transcendentals=10_000
            ),
            name="slope",
        )(visible_blocks, cameras, gaussians)
    with jax.named_scope("gather"):
        near = lax.all_to_all(message, "cell", 0, 0, axis_index_groups=same_core, tiled=True)
        far = lax.ppermute(near, "cell", swap)
    with jax.named_scope("render"):
        pairs = jax.ShapeDtypeStruct((chips * FEATURES * ROWS // 8, 8, LANES), F32)
        near_grad, far_grad, extra = pl.pallas_call(
            render_kernel,
            out_shape=[pairs, pairs, jax.ShapeDtypeStruct(extra.shape, F32)],
            in_specs=[SMEM, SMEM, SMEM, VMEM, VMEM, VMEM, VMEM],
            out_specs=[VMEM, VMEM, VMEM],
            scratch_shapes=render_scratch(*tile_order.shape[1:]),
            compiler_params=PARAMETERS,
            name="render",
        )(tile_order, tile_length, tile_ids, targets, near, far, extra)
    with jax.named_scope("scatter"):
        pair = near_grad + lax.ppermute(far_grad, "cell", swap)
        parts = lax.all_to_all(
            pair.reshape(near.shape), "cell", 0, 0, axis_index_groups=same_core, tiled=True)
    with jax.named_scope("collect"):
        own = pl.pallas_call(
            collect_kernel,
            out_shape=jax.ShapeDtypeStruct((views, VIEW_MSG, ROWS, LANES), F32),
            in_specs=[VMEM, VMEM],
            out_specs=VMEM,
            compiler_params=PARAMETERS,
            name="collect",
        )(parts.reshape(pair.shape), extra)
        every = lax.all_to_all(own, "view", 0, 0, tiled=True)
    with jax.named_scope("camera"):
        camera_part = pl.pallas_call(
            pose_kernel,
            out_shape=jax.ShapeDtypeStruct((1, 1, LANES), F32),
            in_specs=[VMEM, VMEM],
            out_specs=VMEM,
            compiler_params=PARAMETERS,
            cost_estimate=pl.CostEstimate(
                flops=100_000, bytes_accessed=250_000, transcendentals=0
            ),
            name="pose",
        )(own, slopes)
        camera_pair = camera_part + lax.ppermute(camera_part, "cell", swap)
        camera_copies = jnp.broadcast_to(camera_pair, (chips, 1, LANES))
        every, camera_copies = lax.optimization_barrier((every, camera_copies))
        camera_parts = lax.all_to_all(
            camera_copies, "cell", 0, 0, axis_index_groups=same_core, tiled=True
        )
    with jax.named_scope("update"):
        state = jax.ShapeDtypeStruct(gaussians.shape, F32)
        new_gaussians, new_first, new_second = pl.pallas_call(
            lambda *refs: update_kernel(focal, *refs),
            out_shape=[state, state, state],
            in_specs=[VMEM] * 4,
            out_specs=[VMEM] * 3,
            scratch_shapes=[
                pltpu.VMEM((9, owned, LANES), F32),
                pltpu.VMEM((params + 9, owned, LANES), F32),
            ],
            compiler_params=PARAMETERS,
            name="update",
        )(every, gaussians, first_moment, second_moment)
    with jax.named_scope("camera"):
        camera_total = jnp.sum(camera_parts, axis=0)[:, :6]
    return (
        new_gaussians.transpose(1, 0, 2),
        new_first.transpose(1, 0, 2),
        new_second.transpose(1, 0, 2),
        camera_total,
    )


def solution(mesh):
    return jax.shard_map(
        shards,
        mesh=mesh,
        in_specs=(
            P("cell", None, None),
            P("cell", None, None),
            P("cell", None, None),
            P("view", None),
            P("view", "cell"),
            P("view", "cell"),
            P("view", "cell", None),
            P("view", "cell"),
            P("view", "cell", None, None),
        ),
        out_specs=(
            P("cell", None, None),
            P("cell", None, None),
            P("cell", None, None),
            P("view", None),
        ),
        check_vma=False,
    )
```

```python
import functools

import jax
import jax.numpy as jnp
from jax import lax
from jax.experimental import pallas as pl
from jax.experimental.pallas import tpu as pltpu
from jax.sharding import PartitionSpec as P

TILE = 16
PIX = 256
BLOCK = 256
LANES = 128
HALVES = 2
FEATURES = 9
CORES = 2
ROWS = 4
VIEW_MSG = 10
LOG2E = 1.4426950408889634
F32 = jnp.float32
BF16 = jnp.bfloat16


def rotation_matrix(real_part, axis_x, axis_y, axis_z):
    return [
        [
            1.0 - 2.0 * (axis_y * axis_y + axis_z * axis_z),
            2.0 * (axis_x * axis_y - real_part * axis_z),
            2.0 * (axis_x * axis_z + real_part * axis_y),
        ],
        [
            2.0 * (axis_x * axis_y + real_part * axis_z),
            1.0 - 2.0 * (axis_x * axis_x + axis_z * axis_z),
            2.0 * (axis_y * axis_z - real_part * axis_x),
        ],
        [
            2.0 * (axis_x * axis_z - real_part * axis_y),
            2.0 * (axis_y * axis_z + real_part * axis_x),
            1.0 - 2.0 * (axis_x * axis_x + axis_y * axis_y),
        ],
    ]


def harmonic_basis(unit_x, unit_y, unit_z):
    square_x = unit_x * unit_x
    square_y = unit_y * unit_y
    square_z = unit_z * unit_z
    return [
        -0.4886025119029199 * unit_y,
        0.4886025119029199 * unit_z,
        -0.4886025119029199 * unit_x,
        1.0925484305920792 * unit_x * unit_y,
        -1.0925484305920792 * unit_y * unit_z,
        0.31539156525252005 * (2.0 * square_z - square_x - square_y),
        -1.0925484305920792 * unit_x * unit_z,
        0.5462742152960396 * (square_x - square_y),
        -0.5900435899266435 * unit_y * (3.0 * square_x - square_y),
        2.890611442640554 * unit_x * unit_y * unit_z,
        -0.4570457994644658 * unit_y * (4.0 * square_z - square_x - square_y),
        0.3731763325901154 * unit_z * (2.0 * square_z - 3.0 * square_x - 3.0 * square_y),
        -0.4570457994644658 * unit_x * (4.0 * square_z - square_x - square_y),
        1.445305721320277 * unit_z * (square_x - square_y),
        -0.5900435899266435 * unit_x * (square_x - 3.0 * square_y),
    ]


HARMONIC_0 = 0.28209479177387814


def camera_frame(camera):
    inverse_norm = 1.0 / jnp.sqrt(
        1.0 + camera[0] * camera[0] + camera[1] * camera[1] + camera[2] * camera[2]
    )
    rotation = rotation_matrix(
        inverse_norm, camera[0] * inverse_norm, camera[1] * inverse_norm, camera[2] * inverse_norm
    )
    shift = [camera[3], camera[4], camera[5]]
    centre = [
        -(rotation[0][i] * shift[0] + rotation[1][i] * shift[1] + rotation[2][i] * shift[2])
        for i in range(3)
    ]
    return [rotation[i][j] for i in range(3) for j in range(3)] + shift + centre


def shape_factor(scales, quaternion):
    inverse_norm = 1.0 / jnp.sqrt(sum(entry * entry for entry in quaternion))
    own = rotation_matrix(*[entry * inverse_norm for entry in quaternion])
    widths = [jnp.exp(entry) for entry in scales]
    return [own[i][j] * widths[j] for i in range(3) for j in range(3)]


def view_of(centers, factor, frame, focal_length, centre_x, centre_y):
    rotation = [frame[3 * i : 3 * i + 3] for i in range(3)]
    shift = frame[9:12]
    origin = frame[12:15]
    in_view = [
        rotation[i][0] * centers[0]
        + rotation[i][1] * centers[1]
        + rotation[i][2] * centers[2]
        + shift[i]
        for i in range(3)
    ]
    inverse_depth = 1.0 / in_view[2]
    near = focal_length * inverse_depth
    ratio_x = in_view[0] * inverse_depth
    ratio_y = in_view[1] * inverse_depth
    screen = [
        [near * (rotation[0][j] - ratio_x * rotation[2][j]) for j in range(3)],
        [near * (rotation[1][j] - ratio_y * rotation[2][j]) for j in range(3)],
    ]
    spread = [
        [sum(screen[a][j] * factor[3 * j + k] for j in range(3)) for k in range(3)]
        for a in range(2)
    ]
    variance_x = sum(spread[0][k] * spread[0][k] for k in range(3)) + 0.3
    covariance = sum(spread[0][k] * spread[1][k] for k in range(3))
    variance_y = sum(spread[1][k] * spread[1][k] for k in range(3)) + 0.3
    inverse_determinant = 1.0 / (variance_x * variance_y - covariance * covariance)
    toward = [centers[i] - origin[i] for i in range(3)]
    inverse_length = 1.0 / jnp.sqrt(
        toward[0] * toward[0] + toward[1] * toward[1] + toward[2] * toward[2]
    )
    basis = harmonic_basis(*[entry * inverse_length for entry in toward])
    return [
        focal_length * ratio_x + centre_x,
        focal_length * ratio_y + centre_y,
        variance_y * inverse_determinant,
        -covariance * inverse_determinant,
        variance_x * inverse_determinant,
    ] + basis


def colour_sum(basis, harmonic_of, channel):
    summed = 0.5 + HARMONIC_0 * harmonic_of(channel, 0)
    for k in range(15):
        summed = summed + basis[k] * harmonic_of(channel, k + 1)
    return summed


def sigmoid(logit):
    return 1.0 / (1.0 + jnp.exp(-logit))


def features_of(row, camera, focal):
    shape = row(0).shape
    frame = [jnp.broadcast_to(entry, shape) for entry in camera_frame(camera)]
    factor = shape_factor([row(3 + i) for i in range(3)], [row(6 + i) for i in range(4)])
    seen = view_of([row(i) for i in range(3)], factor, frame, *focal)
    colours = [
        jnp.maximum(colour_sum(seen[5:], lambda c, k: row(11 + 16 * c + k), channel), 0.0)
        for channel in range(3)
    ]
    return seen[:5] + [sigmoid(row(10))] + colours


def halves_of(gauss_ref):
    return lambda k: jnp.concatenate(
        [gauss_ref[k, :, half * LANES : (half + 1) * LANES] for half in range(HALVES)], axis=0
    )


def pick(visible_ref, owned):
    base = lax.axis_index("cell") * owned
    place = lax.broadcasted_iota(jnp.int32, (owned, LANES), 0)
    masks = [place == visible_ref[0, sub] - base for sub in range(2)]
    return lambda value: [
        jnp.sum(
            jnp.where(mask, value[half * owned : (half + 1) * owned], 0.0), axis=0, keepdims=True
        )
        for mask in masks
        for half in range(HALVES)
    ]


def camera_rows(camera_ref):
    return [jnp.full((1, LANES), camera_ref[0, i], F32) for i in range(6)]


def project_kernel(
    focal,
    visible_any,
    camera_any,
    gauss_any,
    out_ref,
    extra_ref,
    visible_ref,
    camera_ref,
    gauss_ref,
    small_done,
    large_done,
):
    small = [
        pltpu.make_async_copy(visible_any, visible_ref, small_done.at[0]),
        pltpu.make_async_copy(camera_any, camera_ref, small_done.at[1]),
    ]
    cuts = [0, 11, 27, 43, 59]
    large = [
        pltpu.make_async_copy(
            gauss_any.at[low:high], gauss_ref.at[low:high], large_done.at[i]
        )
        for i, (low, high) in enumerate(zip(cuts[:-1], cuts[1:]))
    ]
    for copy in small + large:
        copy.start()
    for copy in small:
        copy.wait()
    owned = gauss_ref.shape[1]
    base = lax.axis_index("cell") * owned
    values = [camera_ref[0, i] for i in range(6)] + [
        (visible_ref[0, sub] - base).astype(F32) for sub in range(2)
    ]
    row = lax.broadcasted_iota(jnp.int32, (ROWS, LANES), 0)
    lane = lax.broadcasted_iota(jnp.int32, (ROWS, LANES), 1)
    place = row + jnp.where(lane < LANES // 2, 0, ROWS)
    extra = jnp.zeros((ROWS, LANES), F32)
    for i, value in enumerate(values):
        extra = jnp.where(place == i, value, extra)
    extra_ref[...] = extra
    for copy in large:
        copy.wait()
    features = features_of(halves_of(gauss_ref), camera_rows(camera_ref), focal)
    picked = pick(visible_ref, owned)
    for f in range(FEATURES):
        out_ref[0, f] = jnp.concatenate(picked(features[f]), axis=0)
    message = out_ref[0]
    for i in range(1, out_ref.shape[0]):
        out_ref[i] = message


def slope_kernel(focal, visible_ref, camera_ref, gauss_ref, out_ref):
    camera = camera_rows(camera_ref)
    whole = halves_of(gauss_ref)
    picked = pick(visible_ref, gauss_ref.shape[1])
    held = [jnp.concatenate(picked(whole(k)), axis=0) for k in range(gauss_ref.shape[0])]
    for i in range(6):
        tangents = [jnp.full((1, LANES), 1.0 if j == i else 0.0, F32) for j in range(6)]
        _, slopes = jax.jvp(
            lambda *entries: features_of(held.__getitem__, entries, focal), camera, tangents
        )
        for f in range(FEATURES):
            out_ref[i, f] = slopes[f]


def split(value):
    high = value.astype(BF16)
    return high, (value - high.astype(F32)).astype(BF16)


def dot(left, right):
    return jnp.dot(left, right, preferred_element_type=F32)


def both_dots(pair, right):
    return dot(pair[0], right) + dot(pair[1], right)


def transpose_dot(left, right):
    return lax.dot_general(
        left, right, (((1,), (1,)), ((), ())), preferred_element_type=F32
    )


def stacked(value, rows):
    high, low = split(value)
    return jnp.concatenate(
        [high.astype(F32), low.astype(F32), jnp.zeros((rows - 6, value.shape[1]), F32)], axis=0
    ).astype(BF16)


def render_kernel(
    order_ref,
    length_ref,
    tile_ref,
    target_ref,
    near_ref,
    far_ref,
    extra_ref,
    near_out,
    far_out,
    extra_out,
    feature_scr,
    rgb_scr,
    weight_scr,
    high_scr,
    low_scr,
    ratio_scr,
):
    slots, depth = order_ref.shape[1], order_ref.shape[2]
    core = lax.rem(lax.axis_index("cell"), CORES)
    extra_out[...] = extra_ref[...]
    near_out[...] = jnp.zeros_like(near_out)
    far_out[...] = jnp.zeros_like(far_out)
    first = lax.broadcasted_iota(jnp.int32, (BLOCK, BLOCK), 0)
    second = lax.broadcasted_iota(jnp.int32, (BLOCK, BLOCK), 1)
    earlier = (first < second).astype(BF16)
    later = (first > second).astype(BF16)
    step_x = lax.broadcasted_iota(jnp.int32, (TILE, BLOCK), 0).astype(F32) - 7.5
    part = lax.broadcasted_iota(jnp.int32, (8, LANES), 0)
    targets = target_ref[...].astype(F32)

    places = []
    for slot in range(slots):
        tile = tile_ref[0, slot]
        places.append(
            (
                (lax.rem(tile, 16) * TILE + 8).astype(F32),
                (lax.div(tile, 16) * TILE + 8).astype(F32),
            )
        )
    def owner(slot, k):
        block = order_ref[0, slot, k]
        on_near = lax.rem(lax.div(block, 2), CORES) == core
        return lax.div(block, 4), on_near, lax.rem(block, 2)

    def forward(k, carry):
        remains, colours = carry
        alphas, keeps = [], []
        for slot in range(slots):
            chip, on_near, side = owner(slot, k)
            for f in range(FEATURES):
                entry = jnp.where(on_near, near_ref[chip, f], far_ref[chip, f])
                entry = jnp.where(side == 0, entry[0:2], entry[2:4])
                feature_scr[slot, k, f : f + 1, 0:LANES] = entry[0:1]
                feature_scr[slot, k, f : f + 1, LANES:] = entry[1:2]
            feature = feature_scr.at[slot, k]
            rgb_scr[slot, k] = stacked(feature[6:9, :], 16)
            delta_x = step_x - (feature[0:1, :] - places[slot][0])
            local_y = feature[1:2, :] - places[slot][1]
            curve_x = (-0.5 * LOG2E) * feature[2:3, :] * delta_x * delta_x
            cross_x = (-LOG2E) * feature[3:4, :] * delta_x
            curve = (-0.5 * LOG2E) * feature[4:5, :]
            opacity = jnp.where(k < length_ref[0, slot], feature[5:6, :], 0.0)
            rows = []
            for i in range(TILE):
                delta_y = (i - 7.5) - local_y
                rows.append(curve_x + (cross_x * delta_y + curve * delta_y * delta_y))
            alpha = opacity * jnp.exp2(jnp.concatenate(rows, axis=0))
            keep = alpha * (
                -LOG2E
                - alpha * (LOG2E / 2.0 + alpha * (LOG2E / 3.0 + alpha * (LOG2E / 4.0)))
            )
            ratio_scr[slot, k] = alpha * jnp.exp2(-keep)
            alphas.append(alpha)
            keeps.append(keep)
        inner = [both_dots(split(keep), earlier) for keep in keeps]
        new_remains, new_colours = [], []
        for slot in range(slots):
            before = inner[slot] + remains[slot]
            weight = alphas[slot] * jnp.exp2(before)
            weight_scr[slot, k] = weight
            high, low = split(weight)
            high_scr[slot, k] = high
            low_scr[slot, k] = low
            rgb = rgb_scr[slot, k]
            new_remains.append(before[:, BLOCK - 1 :] + keeps[slot][:, BLOCK - 1 :])
            new_colours.append(
                colours[slot] + transpose_dot(rgb, high) + transpose_dot(rgb, low)
            )
        return tuple(new_remains), tuple(new_colours)

    zero = (jnp.zeros((PIX, 1), F32),) * slots
    carry = (zero, (jnp.zeros((16, PIX), F32),) * slots)
    for k in range(depth):
        carry = forward(k, carry)
    colours = carry[1]
    misfit_rows, misfit_cols = [], []
    for slot in range(slots):
        misfit = colours[slot][0:3] + colours[slot][3:6] - targets[0, slot]
        misfit_rows.append(stacked(misfit, 16))
        turned = jnp.concatenate([misfit, jnp.zeros((5, PIX), F32)], axis=0).T
        misfit_cols.append([turned[:, c : c + 1] for c in range(3)])

    def backward(step, behind):
        k = depth - 1 - step
        throughs = []
        for slot in range(slots):
            feature = feature_scr.at[slot, k]
            throughs.append(
                weight_scr[slot, k]
                * sum(misfit_cols[slot][c] * feature[6 + c : 7 + c, :] for c in range(3))
            )
        inner = [both_dots(split(through), later) for through in throughs]
        new_behind = []
        for slot in range(slots):
            feature = feature_scr.at[slot, k]
            chip, on_near, side = owner(slot, k)
            after = inner[slot] + behind[slot]
            slope = throughs[slot] - after * ratio_scr[slot, k]
            new_behind.append(after[:, 0:1] + throughs[slot][:, 0:1])
            flat = jnp.zeros((TILE, BLOCK), F32)
            tilt = jnp.zeros((TILE, BLOCK), F32)
            bend = jnp.zeros((TILE, BLOCK), F32)
            for i in range(TILE // 2):
                top = slope[i * TILE : (i + 1) * TILE]
                bottom = slope[(TILE - 1 - i) * TILE : (TILE - i) * TILE]
                away = 7.5 - i
                flat = flat + (top + bottom)
                tilt = tilt + away * (bottom - top)
                bend = bend + (away * away) * (top + bottom)
            colour_grad = dot(misfit_rows[slot], high_scr[slot, k]) + dot(
                misfit_rows[slot], low_scr[slot, k]
            )
            delta_x = step_x - (feature[0:1, :] - places[slot][0])
            local_y = feature[1:2, :] - places[slot][1]
            mean = tilt - local_y * flat
            bend = bend - local_y * (tilt + mean)

            def across(value):
                return jnp.sum(value, axis=0, keepdims=True)

            total, mean_x, mean_y = across(flat), across(delta_x * flat), across(mean)
            square_x = across(delta_x * delta_x * flat)
            mixed = across(delta_x * mean)
            square_y = across(bend)
            conic_x, conic_xy, conic_y = feature[2:3, :], feature[3:4, :], feature[4:5, :]
            grads = [
                conic_x * mean_x + conic_xy * mean_y,
                conic_y * mean_y + conic_xy * mean_x,
                -0.5 * square_x,
                -mixed,
                -0.5 * square_y,
                total / feature[5:6, :],
            ] + [colour_grad[i : i + 1] + colour_grad[i + 3 : i + 4] for i in range(3)]
            spots, placed = [], []
            for f in range(FEATURES):
                spot = chip * FEATURES + f
                at = lax.rem(spot, 2) * ROWS + side * 2
                spots.append(lax.div(spot, 2))
                placed.append(
                    jnp.where(
                        part == at,
                        grads[f][:, :LANES],
                        jnp.where(part == at + 1, grads[f][:, LANES:], 0.0),
                    )
                )

            for f in range(FEATURES):
                near_out[spots[f]] += jnp.where(on_near, placed[f], 0.0)
                far_out[spots[f]] += jnp.where(on_near, 0.0, placed[f])

        return tuple(new_behind)

    carry = zero
    for k in range(depth):
        carry = backward(k, carry)


def render_scratch(slots, depth):
    return [
        pltpu.VMEM((slots, depth, 16, BLOCK), F32),
        pltpu.VMEM((slots, depth, 16, BLOCK), BF16),
        pltpu.VMEM((slots, depth, PIX, BLOCK), F32),
        pltpu.VMEM((slots, depth, PIX, BLOCK), BF16),
        pltpu.VMEM((slots, depth, PIX, BLOCK), BF16),
        pltpu.VMEM((slots, depth, PIX, BLOCK), F32),
    ]


def collect_kernel(parts_ref, extra_ref, out_ref):
    paired = parts_ref[0:FEATURES]
    for i in range(1, parts_ref.shape[0] // FEATURES):
        paired = paired + parts_ref[i * FEATURES : (i + 1) * FEATURES]
    pieces = [paired[i // 2, (i % 2) * ROWS : (i % 2 + 1) * ROWS] for i in range(2 * FEATURES)]
    for f in range(FEATURES):
        out_ref[0, f] = pieces[f] + pieces[FEATURES + f]
    out_ref[0, FEATURES] = extra_ref[...]
    message = out_ref[0]
    for i in range(1, out_ref.shape[0]):
        out_ref[i] = message


def pose_kernel(own_ref, slope_ref, out_ref):
    lane = lax.broadcasted_iota(jnp.int32, (1, LANES), 1)
    packed = jnp.zeros((1, LANES), F32)
    for i in range(6):
        across = jnp.sum(
            sum(own_ref[0, f] * slope_ref[i, f] for f in range(FEATURES)), axis=0, keepdims=True
        )
        packed = packed + jnp.where(lane == i, jnp.sum(across, axis=1, keepdims=True), 0.0)
    for i in range(out_ref.shape[0]):
        out_ref[i] = packed


def update_kernel(
    focal,
    parts_ref,
    gauss_ref,
    first_ref,
    second_ref,
    gauss_out,
    first_out,
    second_out,
    factor_scr,
    sum_scr,
):
    params, owned = gauss_ref.shape[0], gauss_ref.shape[1]
    views = parts_ref.shape[0]
    place = lax.broadcasted_iota(jnp.int32, (owned, LANES), 0).astype(F32)
    whole = (owned, LANES)
    for half in range(HALVES):
        lanes = slice(half * LANES, (half + 1) * LANES)

        def row(k, lanes=lanes):
            return gauss_ref[k, :, lanes]

        factor, factor_pull = jax.vjp(
            shape_factor,
            [row(3 + i) for i in range(3)],
            [row(6 + i) for i in range(4)],
        )
        for i in range(9):
            factor_scr[i] = factor[i]
        sum_scr[...] = jnp.zeros_like(sum_scr)

        def one_view(view, carry):
            def message(f, r):
                return parts_ref[view, f, r : r + 1, :]

            def extra(i):
                at = i // ROWS * (LANES // 2)
                return jnp.broadcast_to(message(FEATURES, i % ROWS)[:, at : at + 1], (1, LANES))

            masks = [place == extra(6 + sub) for sub in range(2)]
            screen = [
                sum(
                    jnp.where(masks[sub], message(f, sub * 2 + half), 0.0)
                    for sub in range(2)
                )
                for f in range(FEATURES)
            ]
            frame = [
                jnp.broadcast_to(entry, whole)
                for entry in camera_frame([extra(i) for i in range(6)])
            ]
            seen, pull = jax.vjp(
                lambda centers, factor: view_of(centers, factor, frame, *focal),
                [row(i) for i in range(3)],
                [factor_scr[i] for i in range(9)],
            )
            basis = seen[5:]
            basis_grad = [jnp.zeros(whole, F32)] * 15
            for channel in range(3):
                first_row = 11 + 16 * channel
                summed = colour_sum(basis, lambda c, k: row(11 + 16 * c + k), channel)
                gate = jnp.where(summed > 0.0, 1.0, jnp.where(summed == 0.0, 0.5, 0.0))
                colour = screen[6 + channel] * gate
                sum_scr[first_row] += HARMONIC_0 * colour
                for k in range(15):
                    basis_grad[k] = basis_grad[k] + colour * row(first_row + 1 + k)
                    sum_scr[first_row + 1 + k] += colour * basis[k]
            centre_grad, factor_grad = pull(screen[:5] + basis_grad)
            for i in range(3):
                sum_scr[i] += centre_grad[i]
            sum_scr[10] += screen[5]
            for i in range(9):
                sum_scr[params + i] += factor_grad[i]
            return carry

        lax.fori_loop(0, views, one_view, 0)
        scale_grad, quaternion_grad = factor_pull([sum_scr[params + i] for i in range(9)])
        opacity = sigmoid(row(10))
        for i in range(3):
            sum_scr[3 + i] = scale_grad[i]
        for i in range(4):
            sum_scr[6 + i] = quaternion_grad[i]
        sum_scr[10] = sum_scr[10] * opacity * (1.0 - opacity)
        for k in range(params):
            gradient = sum_scr[k]
            moment = 0.9 * first_ref[k, :, lanes] + 0.1 * gradient
            second = 0.999 * second_ref[k, :, lanes] + 0.001 * gradient * gradient
            first_out[k, :, lanes] = moment
            second_out[k, :, lanes] = second
            gauss_out[k, :, lanes] = row(k) - (0.05 / (1.0 - 0.9**10)) * moment / (
                jnp.sqrt(second * (1.0 / (1.0 - 0.999**10))) + 1e-08
            )


VMEM = pl.BlockSpec(memory_space=pltpu.VMEM)
SMEM = pl.BlockSpec(memory_space=pltpu.SMEM)
PARAMETERS = pltpu.CompilerParams(vmem_limit_bytes=40 * 1024 * 1024)


def shards(
    gaussians,
    first_moment,
    second_moment,
    cameras,
    visible_blocks,
    tile_ids,
    tile_order,
    tile_length,
    targets,
):
    owned, params = gaussians.shape[0], gaussians.shape[1]
    gaussians, first_moment, second_moment = (
        array.transpose(1, 0, 2) for array in (gaussians, first_moment, second_moment)
    )
    cells = lax.axis_size("cell")
    views = lax.axis_size("view")
    chips = cells // CORES
    tile_total = cells * tile_ids.shape[1]
    focal = (16.0 * TILE, 8.0 * TILE, tile_total * TILE / 32.0)
    same_core = [[chip * CORES + core for chip in range(chips)] for core in range(CORES)]
    swap = [(cell, cell ^ 1) for cell in range(cells)]

    with jax.named_scope("project"):
        message, extra = pl.pallas_call(
            lambda *refs: project_kernel(focal, *refs),
            out_shape=[
                jax.ShapeDtypeStruct((chips, FEATURES, ROWS, LANES), F32),
                jax.ShapeDtypeStruct((ROWS, LANES), F32),
            ],
            in_specs=[pl.BlockSpec(memory_space=pl.ANY)] * 3,
            out_specs=[VMEM, VMEM],
            scratch_shapes=[
                pltpu.SMEM(visible_blocks.shape, jnp.int32),
                pltpu.SMEM(cameras.shape, F32),
                pltpu.VMEM(gaussians.shape, F32),
                pltpu.SemaphoreType.DMA((2,)),
                pltpu.SemaphoreType.DMA((4,)),
            ],
            compiler_params=pltpu.CompilerParams(vmem_limit_bytes=60 * 1024 * 1024),
            name="project",
        )(visible_blocks, cameras, gaussians)
        slopes = pl.pallas_call(
            lambda *refs: slope_kernel(focal, *refs),
            out_shape=jax.ShapeDtypeStruct((6, FEATURES, ROWS, LANES), F32),
            in_specs=[SMEM, SMEM, VMEM],
            out_specs=VMEM,
            compiler_params=PARAMETERS,
            cost_estimate=pl.CostEstimate(
                flops=4_000_000, bytes_accessed=200_000, transcendentals=10_000
            ),
            name="slope",
        )(visible_blocks, cameras, gaussians)
    with jax.named_scope("gather"):
        near = lax.all_to_all(message, "cell", 0, 0, axis_index_groups=same_core, tiled=True)
        far = lax.ppermute(near, "cell", swap)
    with jax.named_scope("render"):
        pairs = jax.ShapeDtypeStruct((chips * FEATURES * ROWS // 8, 8, LANES), F32)
        near_grad, far_grad, extra = pl.pallas_call(
            render_kernel,
            out_shape=[pairs, pairs, jax.ShapeDtypeStruct(extra.shape, F32)],
            in_specs=[SMEM, SMEM, SMEM, VMEM, VMEM, VMEM, VMEM],
            out_specs=[VMEM, VMEM, VMEM],
            scratch_shapes=render_scratch(*tile_order.shape[1:]),
            compiler_params=PARAMETERS,
            name="render",
        )(tile_order, tile_length, tile_ids, targets, near, far, extra)
    with jax.named_scope("scatter"):
        pair = near_grad + lax.ppermute(far_grad, "cell", swap)
        parts = lax.all_to_all(
            pair.reshape(near.shape), "cell", 0, 0, axis_index_groups=same_core, tiled=True)
    with jax.named_scope("collect"):
        own = pl.pallas_call(
            collect_kernel,
            out_shape=jax.ShapeDtypeStruct((views, VIEW_MSG, ROWS, LANES), F32),
            in_specs=[VMEM, VMEM],
            out_specs=VMEM,
            compiler_params=PARAMETERS,
            name="collect",
        )(parts.reshape(pair.shape), extra)
        every = lax.all_to_all(own, "view", 0, 0, tiled=True)
    with jax.named_scope("camera"):
        camera_part = pl.pallas_call(
            pose_kernel,
            out_shape=jax.ShapeDtypeStruct((chips, 1, LANES), F32),
            in_specs=[VMEM, VMEM],
            out_specs=VMEM,
            compiler_params=PARAMETERS,
            cost_estimate=pl.CostEstimate(
                flops=100_000, bytes_accessed=250_000, transcendentals=0
            ),
            name="pose",
        )(own, slopes)
        camera_copies = camera_part + lax.ppermute(camera_part, "cell", swap)
        every, camera_copies = lax.optimization_barrier((every, camera_copies))
        camera_parts = lax.all_to_all(
            camera_copies, "cell", 0, 0, axis_index_groups=same_core, tiled=True
        )
    with jax.named_scope("update"):
        state = jax.ShapeDtypeStruct(gaussians.shape, F32)
        new_gaussians, new_first, new_second = pl.pallas_call(
            lambda *refs: update_kernel(focal, *refs),
            out_shape=[state, state, state],
            in_specs=[VMEM] * 4,
            out_specs=[VMEM] * 3,
            scratch_shapes=[
                pltpu.VMEM((9, owned, LANES), F32),
                pltpu.VMEM((params + 9, owned, LANES), F32),
            ],
            compiler_params=PARAMETERS,
            name="update",
        )(every, gaussians, first_moment, second_moment)
    with jax.named_scope("camera"):
        camera_total = jnp.sum(camera_parts, axis=0)[:, :6]
    return (
        new_gaussians.transpose(1, 0, 2),
        new_first.transpose(1, 0, 2),
        new_second.transpose(1, 0, 2),
        camera_total,
    )


def solution(mesh):
    return jax.shard_map(
        shards,
        mesh=mesh,
        in_specs=(
            P("cell", None, None),
            P("cell", None, None),
            P("cell", None, None),
            P("view", None),
            P("view", "cell"),
            P("view", "cell"),
            P("view", "cell", None),
            P("view", "cell"),
            P("view", "cell", None, None),
        ),
        out_specs=(
            P("cell", None, None),
            P("cell", None, None),
            P("cell", None, None),
            P("view", None),
        ),
        check_vma=False,
    )
```

```python
import functools

import jax
import jax.numpy as jnp
from jax import lax
from jax.experimental import pallas as pl
from jax.experimental.pallas import tpu as pltpu
from jax.sharding import PartitionSpec as P

TILE = 16
PIX = 256
BLOCK = 256
LANES = 128
HALVES = 2
FEATURES = 9
CORES = 2
ROWS = 4
VIEW_MSG = 10
LOG2E = 1.4426950408889634
F32 = jnp.float32
BF16 = jnp.bfloat16


def rotation_matrix(real_part, axis_x, axis_y, axis_z):
    return [
        [
            1.0 - 2.0 * (axis_y * axis_y + axis_z * axis_z),
            2.0 * (axis_x * axis_y - real_part * axis_z),
            2.0 * (axis_x * axis_z + real_part * axis_y),
        ],
        [
            2.0 * (axis_x * axis_y + real_part * axis_z),
            1.0 - 2.0 * (axis_x * axis_x + axis_z * axis_z),
            2.0 * (axis_y * axis_z - real_part * axis_x),
        ],
        [
            2.0 * (axis_x * axis_z - real_part * axis_y),
            2.0 * (axis_y * axis_z + real_part * axis_x),
            1.0 - 2.0 * (axis_x * axis_x + axis_y * axis_y),
        ],
    ]


def harmonic_basis(unit_x, unit_y, unit_z):
    square_x = unit_x * unit_x
    square_y = unit_y * unit_y
    square_z = unit_z * unit_z
    return [
        -0.4886025119029199 * unit_y,
        0.4886025119029199 * unit_z,
        -0.4886025119029199 * unit_x,
        1.0925484305920792 * unit_x * unit_y,
        -1.0925484305920792 * unit_y * unit_z,
        0.31539156525252005 * (2.0 * square_z - square_x - square_y),
        -1.0925484305920792 * unit_x * unit_z,
        0.5462742152960396 * (square_x - square_y),
        -0.5900435899266435 * unit_y * (3.0 * square_x - square_y),
        2.890611442640554 * unit_x * unit_y * unit_z,
        -0.4570457994644658 * unit_y * (4.0 * square_z - square_x - square_y),
        0.3731763325901154 * unit_z * (2.0 * square_z - 3.0 * square_x - 3.0 * square_y),
        -0.4570457994644658 * unit_x * (4.0 * square_z - square_x - square_y),
        1.445305721320277 * unit_z * (square_x - square_y),
        -0.5900435899266435 * unit_x * (square_x - 3.0 * square_y),
    ]


HARMONIC_0 = 0.28209479177387814


def camera_frame(camera):
    inverse_norm = 1.0 / jnp.sqrt(
        1.0 + camera[0] * camera[0] + camera[1] * camera[1] + camera[2] * camera[2]
    )
    rotation = rotation_matrix(
        inverse_norm, camera[0] * inverse_norm, camera[1] * inverse_norm, camera[2] * inverse_norm
    )
    shift = [camera[3], camera[4], camera[5]]
    centre = [
        -(rotation[0][i] * shift[0] + rotation[1][i] * shift[1] + rotation[2][i] * shift[2])
        for i in range(3)
    ]
    return [rotation[i][j] for i in range(3) for j in range(3)] + shift + centre


def shape_factor(scales, quaternion):
    inverse_norm = 1.0 / jnp.sqrt(sum(entry * entry for entry in quaternion))
    own = rotation_matrix(*[entry * inverse_norm for entry in quaternion])
    widths = [jnp.exp(entry) for entry in scales]
    return [own[i][j] * widths[j] for i in range(3) for j in range(3)]


def view_of(centers, factor, frame, focal_length, centre_x, centre_y):
    rotation = [frame[3 * i : 3 * i + 3] for i in range(3)]
    shift = frame[9:12]
    origin = frame[12:15]
    in_view = [
        rotation[i][0] * centers[0]
        + rotation[i][1] * centers[1]
        + rotation[i][2] * centers[2]
        + shift[i]
        for i in range(3)
    ]
    inverse_depth = 1.0 / in_view[2]
    near = focal_length * inverse_depth
    ratio_x = in_view[0] * inverse_depth
    ratio_y = in_view[1] * inverse_depth
    screen = [
        [near * (rotation[0][j] - ratio_x * rotation[2][j]) for j in range(3)],
        [near * (rotation[1][j] - ratio_y * rotation[2][j]) for j in range(3)],
    ]
    spread = [
        [sum(screen[a][j] * factor[3 * j + k] for j in range(3)) for k in range(3)]
        for a in range(2)
    ]
    variance_x = sum(spread[0][k] * spread[0][k] for k in range(3)) + 0.3
    covariance = sum(spread[0][k] * spread[1][k] for k in range(3))
    variance_y = sum(spread[1][k] * spread[1][k] for k in range(3)) + 0.3
    inverse_determinant = 1.0 / (variance_x * variance_y - covariance * covariance)
    toward = [centers[i] - origin[i] for i in range(3)]
    inverse_length = 1.0 / jnp.sqrt(
        toward[0] * toward[0] + toward[1] * toward[1] + toward[2] * toward[2]
    )
    basis = harmonic_basis(*[entry * inverse_length for entry in toward])
    return [
        focal_length * ratio_x + centre_x,
        focal_length * ratio_y + centre_y,
        variance_y * inverse_determinant,
        -covariance * inverse_determinant,
        variance_x * inverse_determinant,
    ] + basis


def colour_sum(basis, harmonic_of, channel):
    summed = 0.5 + HARMONIC_0 * harmonic_of(channel, 0)
    for k in range(15):
        summed = summed + basis[k] * harmonic_of(channel, k + 1)
    return summed


def sigmoid(logit):
    return 1.0 / (1.0 + jnp.exp(-logit))


def features_of(row, camera, focal):
    shape = row(0).shape
    frame = [jnp.broadcast_to(entry, shape) for entry in camera_frame(camera)]
    factor = shape_factor([row(3 + i) for i in range(3)], [row(6 + i) for i in range(4)])
    seen = view_of([row(i) for i in range(3)], factor, frame, *focal)
    colours = [
        jnp.maximum(colour_sum(seen[5:], lambda c, k: row(11 + 16 * c + k), channel), 0.0)
        for channel in range(3)
    ]
    return seen[:5] + [sigmoid(row(10))] + colours


def halves_of(gauss_ref):
    return lambda k: jnp.concatenate(
        [gauss_ref[k, :, half * LANES : (half + 1) * LANES] for half in range(HALVES)], axis=0
    )


def pick(visible_ref, owned):
    base = lax.axis_index("cell") * owned
    place = lax.broadcasted_iota(jnp.int32, (owned, LANES), 0)
    masks = [place == visible_ref[0, sub] - base for sub in range(2)]
    return lambda value: [
        jnp.sum(
            jnp.where(mask, value[half * owned : (half + 1) * owned], 0.0), axis=0, keepdims=True
        )
        for mask in masks
        for half in range(HALVES)
    ]


def camera_rows(camera_ref):
    return [jnp.full((1, LANES), camera_ref[0, i], F32) for i in range(6)]


def project_kernel(
    focal,
    visible_any,
    camera_any,
    gauss_any,
    out_ref,
    extra_ref,
    visible_ref,
    camera_ref,
    gauss_ref,
    small_done,
    large_done,
):
    small = [
        pltpu.make_async_copy(visible_any, visible_ref, small_done.at[0]),
        pltpu.make_async_copy(camera_any, camera_ref, small_done.at[1]),
    ]
    cuts = [0, 11, 27, 43, 59]
    large = [
        pltpu.make_async_copy(
            gauss_any.at[low:high], gauss_ref.at[low:high], large_done.at[i]
        )
        for i, (low, high) in enumerate(zip(cuts[:-1], cuts[1:]))
    ]
    for copy in small + large:
        copy.start()
    for copy in small:
        copy.wait()
    owned = gauss_ref.shape[1]
    base = lax.axis_index("cell") * owned
    values = [camera_ref[0, i] for i in range(6)] + [
        (visible_ref[0, sub] - base).astype(F32) for sub in range(2)
    ]
    row = lax.broadcasted_iota(jnp.int32, (ROWS, LANES), 0)
    lane = lax.broadcasted_iota(jnp.int32, (ROWS, LANES), 1)
    place = row + jnp.where(lane < LANES // 2, 0, ROWS)
    extra = jnp.zeros((ROWS, LANES), F32)
    for i, value in enumerate(values):
        extra = jnp.where(place == i, value, extra)
    extra_ref[...] = extra
    for copy in large:
        copy.wait()
    features = features_of(halves_of(gauss_ref), camera_rows(camera_ref), focal)
    picked = pick(visible_ref, owned)
    for f in range(FEATURES):
        out_ref[0, f] = jnp.concatenate(picked(features[f]), axis=0)
    message = out_ref[0]
    for i in range(1, out_ref.shape[0]):
        out_ref[i] = message


def slope_kernel(focal, visible_ref, camera_ref, gauss_ref, out_ref):
    camera = camera_rows(camera_ref)
    whole = halves_of(gauss_ref)
    picked = pick(visible_ref, gauss_ref.shape[1])
    held = [jnp.concatenate(picked(whole(k)), axis=0) for k in range(gauss_ref.shape[0])]
    for i in range(6):
        tangents = [jnp.full((1, LANES), 1.0 if j == i else 0.0, F32) for j in range(6)]
        _, slopes = jax.jvp(
            lambda *entries: features_of(held.__getitem__, entries, focal), camera, tangents
        )
        for f in range(FEATURES):
            out_ref[i, f] = slopes[f]


def split(value):
    high = value.astype(BF16)
    return high, (value - high.astype(F32)).astype(BF16)


def dot(left, right):
    return jnp.dot(left, right, preferred_element_type=F32)


def both_dots(pair, right):
    return dot(pair[0], right) + dot(pair[1], right)


def transpose_dot(left, right):
    return lax.dot_general(
        left, right, (((1,), (1,)), ((), ())), preferred_element_type=F32
    )


def stacked(value, rows):
    high, low = split(value)
    return jnp.concatenate(
        [high.astype(F32), low.astype(F32), jnp.zeros((rows - 6, value.shape[1]), F32)], axis=0
    ).astype(BF16)


def render_kernel(
    order_ref,
    length_ref,
    tile_ref,
    target_ref,
    near_ref,
    far_ref,
    extra_ref,
    near_out,
    far_out,
    extra_out,
    feature_scr,
    rgb_scr,
    weight_scr,
    high_scr,
    low_scr,
    ratio_scr,
):
    slots, depth = order_ref.shape[1], order_ref.shape[2]
    core = lax.rem(lax.axis_index("cell"), CORES)
    extra_out[...] = extra_ref[...]
    near_out[...] = jnp.zeros_like(near_out)
    far_out[...] = jnp.zeros_like(far_out)
    first = lax.broadcasted_iota(jnp.int32, (BLOCK, BLOCK), 0)
    second = lax.broadcasted_iota(jnp.int32, (BLOCK, BLOCK), 1)
    earlier = (first < second).astype(BF16)
    later = (first > second).astype(BF16)
    step_x = lax.broadcasted_iota(jnp.int32, (TILE, BLOCK), 0).astype(F32) - 7.5
    part = lax.broadcasted_iota(jnp.int32, (8, LANES), 0)
    targets = target_ref[...].astype(F32)

    places = []
    for slot in range(slots):
        tile = tile_ref[0, slot]
        places.append(
            (
                (lax.rem(tile, 16) * TILE + 8).astype(F32),
                (lax.div(tile, 16) * TILE + 8).astype(F32),
            )
        )
    def owner(slot, k):
        block = order_ref[0, slot, k]
        on_near = lax.rem(lax.div(block, 2), CORES) == core
        return lax.div(block, 4), on_near, lax.rem(block, 2)

    def forward(k, carry):
        remains, colours = carry
        alphas, keeps = [], []
        for slot in range(slots):
            chip, on_near, side = owner(slot, k)
            for f in range(FEATURES):
                entry = jnp.where(on_near, near_ref[chip, f], far_ref[chip, f])
                entry = jnp.where(side == 0, entry[0:2], entry[2:4])
                feature_scr[slot, k, f : f + 1, 0:LANES] = entry[0:1]
                feature_scr[slot, k, f : f + 1, LANES:] = entry[1:2]
            feature = feature_scr.at[slot, k]
            rgb_scr[slot, k] = stacked(feature[6:9, :], 16)
            delta_x = step_x - (feature[0:1, :] - places[slot][0])
            local_y = feature[1:2, :] - places[slot][1]
            curve_x = (-0.5 * LOG2E) * feature[2:3, :] * delta_x * delta_x
            cross_x = (-LOG2E) * feature[3:4, :] * delta_x
            curve = (-0.5 * LOG2E) * feature[4:5, :]
            opacity = jnp.where(k < length_ref[0, slot], feature[5:6, :], 0.0)
            rows = []
            for i in range(TILE):
                delta_y = (i - 7.5) - local_y
                rows.append(curve_x + (cross_x * delta_y + curve * delta_y * delta_y))
            alpha = opacity * jnp.exp2(jnp.concatenate(rows, axis=0))
            keep = alpha * (
                -LOG2E
                - alpha * (LOG2E / 2.0 + alpha * (LOG2E / 3.0 + alpha * (LOG2E / 4.0)))
            )
            ratio_scr[slot, k] = alpha * jnp.exp2(-keep)
            alphas.append(alpha)
            keeps.append(keep)
        inner = [both_dots(split(keep), earlier) for keep in keeps]
        new_remains, new_colours = [], []
        for slot in range(slots):
            before = inner[slot] + remains[slot]
            weight = alphas[slot] * jnp.exp2(before)
            weight_scr[slot, k] = weight
            high, low = split(weight)
            high_scr[slot, k] = high
            low_scr[slot, k] = low
            rgb = rgb_scr[slot, k]
            new_remains.append(before[:, BLOCK - 1 :] + keeps[slot][:, BLOCK - 1 :])
            new_colours.append(
                colours[slot] + transpose_dot(rgb, high) + transpose_dot(rgb, low)
            )
        return tuple(new_remains), tuple(new_colours)

    zero = (jnp.zeros((PIX, 1), F32),) * slots
    carry = (zero, (jnp.zeros((16, PIX), F32),) * slots)
    for k in range(depth):
        carry = forward(k, carry)
    colours = carry[1]
    misfit_rows, misfit_cols = [], []
    for slot in range(slots):
        misfit = colours[slot][0:3] + colours[slot][3:6] - targets[0, slot]
        misfit_rows.append(stacked(misfit, 16))
        turned = jnp.concatenate([misfit, jnp.zeros((5, PIX), F32)], axis=0).T
        misfit_cols.append([turned[:, c : c + 1] for c in range(3)])

    def backward(step, behind):
        k = depth - 1 - step
        throughs = []
        for slot in range(slots):
            feature = feature_scr.at[slot, k]
            throughs.append(
                weight_scr[slot, k]
                * sum(misfit_cols[slot][c] * feature[6 + c : 7 + c, :] for c in range(3))
            )
        inner = [both_dots(split(through), later) for through in throughs]
        new_behind = []
        for slot in range(slots):
            feature = feature_scr.at[slot, k]
            chip, on_near, side = owner(slot, k)
            after = inner[slot] + behind[slot]
            slope = throughs[slot] - after * ratio_scr[slot, k]
            new_behind.append(after[:, 0:1] + throughs[slot][:, 0:1])
            flat = jnp.zeros((TILE, BLOCK), F32)
            tilt = jnp.zeros((TILE, BLOCK), F32)
            bend = jnp.zeros((TILE, BLOCK), F32)
            for i in range(TILE // 2):
                top = slope[i * TILE : (i + 1) * TILE]
                bottom = slope[(TILE - 1 - i) * TILE : (TILE - i) * TILE]
                away = 7.5 - i
                flat = flat + (top + bottom)
                tilt = tilt + away * (bottom - top)
                bend = bend + (away * away) * (top + bottom)
            colour_grad = dot(misfit_rows[slot], high_scr[slot, k]) + dot(
                misfit_rows[slot], low_scr[slot, k]
            )
            delta_x = step_x - (feature[0:1, :] - places[slot][0])
            local_y = feature[1:2, :] - places[slot][1]
            mean = tilt - local_y * flat
            bend = bend - local_y * (tilt + mean)

            def across(value):
                return jnp.sum(value, axis=0, keepdims=True)

            total, mean_x, mean_y = across(flat), across(delta_x * flat), across(mean)
            square_x = across(delta_x * delta_x * flat)
            mixed = across(delta_x * mean)
            square_y = across(bend)
            conic_x, conic_xy, conic_y = feature[2:3, :], feature[3:4, :], feature[4:5, :]
            grads = [
                conic_x * mean_x + conic_xy * mean_y,
                conic_y * mean_y + conic_xy * mean_x,
                -0.5 * square_x,
                -mixed,
                -0.5 * square_y,
                total / feature[5:6, :],
            ] + [colour_grad[i : i + 1] + colour_grad[i + 3 : i + 4] for i in range(3)]
            spots, placed = [], []
            for f in range(FEATURES):
                spot = chip * FEATURES + f
                at = lax.rem(spot, 2) * ROWS + side * 2
                spots.append(lax.div(spot, 2))
                placed.append(
                    jnp.where(
                        part == at,
                        grads[f][:, :LANES],
                        jnp.where(part == at + 1, grads[f][:, LANES:], 0.0),
                    )
                )

            for f in range(FEATURES):
                near_out[spots[f]] += jnp.where(on_near, placed[f], 0.0)
                far_out[spots[f]] += jnp.where(on_near, 0.0, placed[f])

        return tuple(new_behind)

    carry = zero
    for k in range(depth):
        carry = backward(k, carry)


def render_scratch(slots, depth):
    return [
        pltpu.VMEM((slots, depth, 16, BLOCK), F32),
        pltpu.VMEM((slots, depth, 16, BLOCK), BF16),
        pltpu.VMEM((slots, depth, PIX, BLOCK), F32),
        pltpu.VMEM((slots, depth, PIX, BLOCK), BF16),
        pltpu.VMEM((slots, depth, PIX, BLOCK), BF16),
        pltpu.VMEM((slots, depth, PIX, BLOCK), F32),
    ]


def collect_kernel(parts_ref, extra_ref, out_ref):
    paired = parts_ref[0:FEATURES]
    for i in range(1, parts_ref.shape[0] // FEATURES):
        paired = paired + parts_ref[i * FEATURES : (i + 1) * FEATURES]
    pieces = [paired[i // 2, (i % 2) * ROWS : (i % 2 + 1) * ROWS] for i in range(2 * FEATURES)]
    for f in range(FEATURES):
        out_ref[0, f] = pieces[f] + pieces[FEATURES + f]
    out_ref[0, FEATURES] = extra_ref[...]
    message = out_ref[0]
    for i in range(1, out_ref.shape[0]):
        out_ref[i] = message


def pose_kernel(own_ref, slope_ref, out_ref):
    lane = lax.broadcasted_iota(jnp.int32, (1, LANES), 1)
    packed = jnp.zeros((1, LANES), F32)
    for i in range(6):
        across = jnp.sum(
            sum(own_ref[0, f] * slope_ref[i, f] for f in range(FEATURES)), axis=0, keepdims=True
        )
        packed = packed + jnp.where(lane == i, jnp.sum(across, axis=1, keepdims=True), 0.0)
    for i in range(out_ref.shape[0]):
        out_ref[i] = packed


def update_kernel(
    focal,
    parts_ref,
    gauss_ref,
    first_ref,
    second_ref,
    gauss_out,
    first_out,
    second_out,
    factor_scr,
    sum_scr,
):
    params, owned = gauss_ref.shape[0], gauss_ref.shape[1]
    views = parts_ref.shape[0]
    place = lax.broadcasted_iota(jnp.int32, (owned, LANES), 0).astype(F32)
    whole = (owned, LANES)
    for half in range(HALVES):
        lanes = slice(half * LANES, (half + 1) * LANES)

        def row(k, lanes=lanes):
            return gauss_ref[k, :, lanes]

        factor, factor_pull = jax.vjp(
            shape_factor,
            [row(3 + i) for i in range(3)],
            [row(6 + i) for i in range(4)],
        )
        for i in range(9):
            factor_scr[i] = factor[i]
        sum_scr[...] = jnp.zeros_like(sum_scr)

        def one_view(view, carry):
            def message(f, r):
                return parts_ref[view, f, r : r + 1, :]

            def extra(i):
                at = i // ROWS * (LANES // 2)
                return jnp.broadcast_to(message(FEATURES, i % ROWS)[:, at : at + 1], (1, LANES))

            masks = [place == extra(6 + sub) for sub in range(2)]
            screen = [
                sum(
                    jnp.where(masks[sub], message(f, sub * 2 + half), 0.0)
                    for sub in range(2)
                )
                for f in range(FEATURES)
            ]
            frame = [
                jnp.broadcast_to(entry, whole)
                for entry in camera_frame([extra(i) for i in range(6)])
            ]
            seen, pull = jax.vjp(
                lambda centers, factor: view_of(centers, factor, frame, *focal),
                [row(i) for i in range(3)],
                [factor_scr[i] for i in range(9)],
            )
            basis = seen[5:]
            basis_grad = [jnp.zeros(whole, F32)] * 15
            for channel in range(3):
                first_row = 11 + 16 * channel
                summed = colour_sum(basis, lambda c, k: row(11 + 16 * c + k), channel)
                gate = jnp.where(summed > 0.0, 1.0, jnp.where(summed == 0.0, 0.5, 0.0))
                colour = screen[6 + channel] * gate
                sum_scr[first_row] += HARMONIC_0 * colour
                for k in range(15):
                    basis_grad[k] = basis_grad[k] + colour * row(first_row + 1 + k)
                    sum_scr[first_row + 1 + k] += colour * basis[k]
            centre_grad, factor_grad = pull(screen[:5] + basis_grad)
            for i in range(3):
                sum_scr[i] += centre_grad[i]
            sum_scr[10] += screen[5]
            for i in range(9):
                sum_scr[params + i] += factor_grad[i]
            return carry

        lax.fori_loop(0, views, one_view, 0)
        scale_grad, quaternion_grad = factor_pull([sum_scr[params + i] for i in range(9)])
        opacity = sigmoid(row(10))
        for i in range(3):
            sum_scr[3 + i] = scale_grad[i]
        for i in range(4):
            sum_scr[6 + i] = quaternion_grad[i]
        sum_scr[10] = sum_scr[10] * opacity * (1.0 - opacity)
        for k in range(params):
            gradient = sum_scr[k]
            moment = 0.9 * first_ref[k, :, lanes] + 0.1 * gradient
            second = 0.999 * second_ref[k, :, lanes] + 0.001 * gradient * gradient
            first_out[k, :, lanes] = moment
            second_out[k, :, lanes] = second
            gauss_out[k, :, lanes] = row(k) - (0.05 / (1.0 - 0.9**10)) * moment / (
                jnp.sqrt(second * (1.0 / (1.0 - 0.999**10))) + 1e-08
            )


VMEM = pl.BlockSpec(memory_space=pltpu.VMEM)
SMEM = pl.BlockSpec(memory_space=pltpu.SMEM)
PARAMETERS = pltpu.CompilerParams(vmem_limit_bytes=40 * 1024 * 1024)


def shards(
    gaussians,
    first_moment,
    second_moment,
    cameras,
    visible_blocks,
    tile_ids,
    tile_order,
    tile_length,
    targets,
):
    owned, params = gaussians.shape[0], gaussians.shape[1]
    gaussians, first_moment, second_moment = (
        array.transpose(1, 0, 2) for array in (gaussians, first_moment, second_moment)
    )
    cells = lax.axis_size("cell")
    views = lax.axis_size("view")
    chips = cells // CORES
    tile_total = cells * tile_ids.shape[1]
    focal = (16.0 * TILE, 8.0 * TILE, tile_total * TILE / 32.0)
    same_core = [[chip * CORES + core for chip in range(chips)] for core in range(CORES)]
    swap = [(cell, cell ^ 1) for cell in range(cells)]

    with jax.named_scope("project"):
        message, extra = pl.pallas_call(
            lambda *refs: project_kernel(focal, *refs),
            out_shape=[
                jax.ShapeDtypeStruct((8, FEATURES, ROWS, LANES), F32),
                jax.ShapeDtypeStruct((ROWS, LANES), F32),
            ],
            in_specs=[pl.BlockSpec(memory_space=pl.ANY)] * 3,
            out_specs=[VMEM, VMEM],
            scratch_shapes=[
                pltpu.SMEM(visible_blocks.shape, jnp.int32),
                pltpu.SMEM(cameras.shape, F32),
                pltpu.VMEM(gaussians.shape, F32),
                pltpu.SemaphoreType.DMA((2,)),
                pltpu.SemaphoreType.DMA((4,)),
            ],
            compiler_params=pltpu.CompilerParams(vmem_limit_bytes=60 * 1024 * 1024),
            name="project",
        )(visible_blocks, cameras, gaussians)
        slopes = pl.pallas_call(
            lambda *refs: slope_kernel(focal, *refs),
            out_shape=jax.ShapeDtypeStruct((6, FEATURES, ROWS, LANES), F32),
            in_specs=[SMEM, SMEM, VMEM],
            out_specs=VMEM,
            compiler_params=PARAMETERS,
            cost_estimate=pl.CostEstimate(
                flops=4_000_000, bytes_accessed=200_000, transcendentals=10_000
            ),
            name="slope",
        )(visible_blocks, cameras, gaussians)
    with jax.named_scope("gather"):
        deep, wide = 8, chips // 8
        z_groups = [
            [(x * deep + z) * CORES + core for z in range(deep)]
            for x in range(wide)
            for core in range(CORES)
        ]
        x_groups = [
            [(x * deep + z) * CORES + core for x in range(wide)]
            for z in range(deep)
            for core in range(CORES)
        ]
        column = lax.all_to_all(
            message, "cell", 0, 0, axis_index_groups=z_groups, tiled=True
        )
        columns = lax.optimization_barrier(jnp.broadcast_to(column, (wide, *column.shape)))
        near = lax.all_to_all(
            columns, "cell", 0, 0, axis_index_groups=x_groups, tiled=True
        ).reshape(chips, FEATURES, ROWS, LANES)
        far = lax.ppermute(near, "cell", swap)
    with jax.named_scope("render"):
        pairs = jax.ShapeDtypeStruct((chips * FEATURES * ROWS // 8, 8, LANES), F32)
        near_grad, far_grad, extra = pl.pallas_call(
            render_kernel,
            out_shape=[pairs, pairs, jax.ShapeDtypeStruct(extra.shape, F32)],
            in_specs=[SMEM, SMEM, SMEM, VMEM, VMEM, VMEM, VMEM],
            out_specs=[VMEM, VMEM, VMEM],
            scratch_shapes=render_scratch(*tile_order.shape[1:]),
            compiler_params=PARAMETERS,
            name="render",
        )(tile_order, tile_length, tile_ids, targets, near, far, extra)
    with jax.named_scope("scatter"):
        pair = near_grad + lax.ppermute(far_grad, "cell", swap)
        parts = lax.all_to_all(
            pair.reshape(near.shape), "cell", 0, 0, axis_index_groups=same_core, tiled=True)
    with jax.named_scope("collect"):
        own = pl.pallas_call(
            collect_kernel,
            out_shape=jax.ShapeDtypeStruct((views, VIEW_MSG, ROWS, LANES), F32),
            in_specs=[VMEM, VMEM],
            out_specs=VMEM,
            compiler_params=PARAMETERS,
            name="collect",
        )(parts.reshape(pair.shape), extra)
        every = lax.all_to_all(own, "view", 0, 0, tiled=True)
    with jax.named_scope("camera"):
        camera_part = pl.pallas_call(
            pose_kernel,
            out_shape=jax.ShapeDtypeStruct((chips, 1, LANES), F32),
            in_specs=[VMEM, VMEM],
            out_specs=VMEM,
            compiler_params=PARAMETERS,
            cost_estimate=pl.CostEstimate(
                flops=100_000, bytes_accessed=250_000, transcendentals=0
            ),
            name="pose",
        )(own, slopes)
        camera_copies = camera_part + lax.ppermute(camera_part, "cell", swap)
        every, camera_copies = lax.optimization_barrier((every, camera_copies))
        camera_parts = lax.all_to_all(
            camera_copies, "cell", 0, 0, axis_index_groups=same_core, tiled=True
        )
    with jax.named_scope("update"):
        state = jax.ShapeDtypeStruct(gaussians.shape, F32)
        new_gaussians, new_first, new_second = pl.pallas_call(
            lambda *refs: update_kernel(focal, *refs),
            out_shape=[state, state, state],
            in_specs=[VMEM] * 4,
            out_specs=[VMEM] * 3,
            scratch_shapes=[
                pltpu.VMEM((9, owned, LANES), F32),
                pltpu.VMEM((params + 9, owned, LANES), F32),
            ],
            compiler_params=PARAMETERS,
            name="update",
        )(every, gaussians, first_moment, second_moment)
    with jax.named_scope("camera"):
        camera_total = jnp.sum(camera_parts, axis=0)[:, :6]
    return (
        new_gaussians.transpose(1, 0, 2),
        new_first.transpose(1, 0, 2),
        new_second.transpose(1, 0, 2),
        camera_total,
    )


def solution(mesh):
    return jax.shard_map(
        shards,
        mesh=mesh,
        in_specs=(
            P("cell", None, None),
            P("cell", None, None),
            P("cell", None, None),
            P("view", None),
            P("view", "cell"),
            P("view", "cell"),
            P("view", "cell", None),
            P("view", "cell"),
            P("view", "cell", None, None),
        ),
        out_specs=(
            P("cell", None, None),
            P("cell", None, None),
            P("cell", None, None),
            P("view", None),
        ),
        check_vma=False,
    )
```

```python
import functools

import jax
import jax.numpy as jnp
from jax import lax
from jax.experimental import pallas as pl
from jax.experimental.pallas import tpu as pltpu
from jax.sharding import PartitionSpec as P

TILE = 16
PIX = 256
BLOCK = 256
LANES = 128
HALVES = 2
FEATURES = 9
CORES = 2
ROWS = 4
VIEW_MSG = 10
LOG2E = 1.4426950408889634
F32 = jnp.float32
BF16 = jnp.bfloat16


def rotation_matrix(real_part, axis_x, axis_y, axis_z):
    return [
        [
            1.0 - 2.0 * (axis_y * axis_y + axis_z * axis_z),
            2.0 * (axis_x * axis_y - real_part * axis_z),
            2.0 * (axis_x * axis_z + real_part * axis_y),
        ],
        [
            2.0 * (axis_x * axis_y + real_part * axis_z),
            1.0 - 2.0 * (axis_x * axis_x + axis_z * axis_z),
            2.0 * (axis_y * axis_z - real_part * axis_x),
        ],
        [
            2.0 * (axis_x * axis_z - real_part * axis_y),
            2.0 * (axis_y * axis_z + real_part * axis_x),
            1.0 - 2.0 * (axis_x * axis_x + axis_y * axis_y),
        ],
    ]


def harmonic_basis(unit_x, unit_y, unit_z):
    square_x = unit_x * unit_x
    square_y = unit_y * unit_y
    square_z = unit_z * unit_z
    return [
        -0.4886025119029199 * unit_y,
        0.4886025119029199 * unit_z,
        -0.4886025119029199 * unit_x,
        1.0925484305920792 * unit_x * unit_y,
        -1.0925484305920792 * unit_y * unit_z,
        0.31539156525252005 * (2.0 * square_z - square_x - square_y),
        -1.0925484305920792 * unit_x * unit_z,
        0.5462742152960396 * (square_x - square_y),
        -0.5900435899266435 * unit_y * (3.0 * square_x - square_y),
        2.890611442640554 * unit_x * unit_y * unit_z,
        -0.4570457994644658 * unit_y * (4.0 * square_z - square_x - square_y),
        0.3731763325901154 * unit_z * (2.0 * square_z - 3.0 * square_x - 3.0 * square_y),
        -0.4570457994644658 * unit_x * (4.0 * square_z - square_x - square_y),
        1.445305721320277 * unit_z * (square_x - square_y),
        -0.5900435899266435 * unit_x * (square_x - 3.0 * square_y),
    ]


HARMONIC_0 = 0.28209479177387814


def camera_frame(camera):
    inverse_norm = 1.0 / jnp.sqrt(
        1.0 + camera[0] * camera[0] + camera[1] * camera[1] + camera[2] * camera[2]
    )
    rotation = rotation_matrix(
        inverse_norm, camera[0] * inverse_norm, camera[1] * inverse_norm, camera[2] * inverse_norm
    )
    shift = [camera[3], camera[4], camera[5]]
    centre = [
        -(rotation[0][i] * shift[0] + rotation[1][i] * shift[1] + rotation[2][i] * shift[2])
        for i in range(3)
    ]
    return [rotation[i][j] for i in range(3) for j in range(3)] + shift + centre


def shape_factor(scales, quaternion):
    inverse_norm = 1.0 / jnp.sqrt(sum(entry * entry for entry in quaternion))
    own = rotation_matrix(*[entry * inverse_norm for entry in quaternion])
    widths = [jnp.exp(entry) for entry in scales]
    return [own[i][j] * widths[j] for i in range(3) for j in range(3)]


def view_of(centers, factor, frame, focal_length, centre_x, centre_y):
    rotation = [frame[3 * i : 3 * i + 3] for i in range(3)]
    shift = frame[9:12]
    origin = frame[12:15]
    in_view = [
        rotation[i][0] * centers[0]
        + rotation[i][1] * centers[1]
        + rotation[i][2] * centers[2]
        + shift[i]
        for i in range(3)
    ]
    inverse_depth = 1.0 / in_view[2]
    near = focal_length * inverse_depth
    ratio_x = in_view[0] * inverse_depth
    ratio_y = in_view[1] * inverse_depth
    screen = [
        [near * (rotation[0][j] - ratio_x * rotation[2][j]) for j in range(3)],
        [near * (rotation[1][j] - ratio_y * rotation[2][j]) for j in range(3)],
    ]
    spread = [
        [sum(screen[a][j] * factor[3 * j + k] for j in range(3)) for k in range(3)]
        for a in range(2)
    ]
    variance_x = sum(spread[0][k] * spread[0][k] for k in range(3)) + 0.3
    covariance = sum(spread[0][k] * spread[1][k] for k in range(3))
    variance_y = sum(spread[1][k] * spread[1][k] for k in range(3)) + 0.3
    inverse_determinant = 1.0 / (variance_x * variance_y - covariance * covariance)
    toward = [centers[i] - origin[i] for i in range(3)]
    inverse_length = 1.0 / jnp.sqrt(
        toward[0] * toward[0] + toward[1] * toward[1] + toward[2] * toward[2]
    )
    basis = harmonic_basis(*[entry * inverse_length for entry in toward])
    return [
        focal_length * ratio_x + centre_x,
        focal_length * ratio_y + centre_y,
        variance_y * inverse_determinant,
        -covariance * inverse_determinant,
        variance_x * inverse_determinant,
    ] + basis


def colour_sum(basis, harmonic_of, channel):
    summed = 0.5 + HARMONIC_0 * harmonic_of(channel, 0)
    for k in range(15):
        summed = summed + basis[k] * harmonic_of(channel, k + 1)
    return summed


def sigmoid(logit):
    return 1.0 / (1.0 + jnp.exp(-logit))


def features_of(row, camera, focal):
    shape = row(0).shape
    frame = [jnp.broadcast_to(entry, shape) for entry in camera_frame(camera)]
    factor = shape_factor([row(3 + i) for i in range(3)], [row(6 + i) for i in range(4)])
    seen = view_of([row(i) for i in range(3)], factor, frame, *focal)
    colours = [
        jnp.maximum(colour_sum(seen[5:], lambda c, k: row(11 + 16 * c + k), channel), 0.0)
        for channel in range(3)
    ]
    return seen[:5] + [sigmoid(row(10))] + colours


def halves_of(gauss_ref):
    return lambda k: jnp.concatenate(
        [gauss_ref[k, :, half * LANES : (half + 1) * LANES] for half in range(HALVES)], axis=0
    )


def pick(visible_ref, owned):
    base = lax.axis_index("cell") * owned
    place = lax.broadcasted_iota(jnp.int32, (owned, LANES), 0)
    masks = [place == visible_ref[0, sub] - base for sub in range(2)]
    return lambda value: [
        jnp.sum(
            jnp.where(mask, value[half * owned : (half + 1) * owned], 0.0), axis=0, keepdims=True
        )
        for mask in masks
        for half in range(HALVES)
    ]


def camera_rows(camera_ref):
    return [jnp.full((1, LANES), camera_ref[0, i], F32) for i in range(6)]


def project_kernel(
    focal,
    visible_any,
    camera_any,
    gauss_any,
    out_ref,
    extra_ref,
    visible_ref,
    camera_ref,
    gauss_ref,
    basis_scr,
    small_done,
    large_done,
):
    small = [
        pltpu.make_async_copy(visible_any, visible_ref, small_done.at[0]),
        pltpu.make_async_copy(camera_any, camera_ref, small_done.at[1]),
    ]
    cuts = [0, 11, 27, 43, 59]
    large = [
        pltpu.make_async_copy(
            gauss_any.at[low:high], gauss_ref.at[low:high], large_done.at[i]
        )
        for i, (low, high) in enumerate(zip(cuts[:-1], cuts[1:]))
    ]
    for copy in small + large:
        copy.start()
    for copy in small:
        copy.wait()
    owned = gauss_ref.shape[1]
    base = lax.axis_index("cell") * owned
    values = [camera_ref[0, i] for i in range(6)] + [
        (visible_ref[0, sub] - base).astype(F32) for sub in range(2)
    ]
    row = lax.broadcasted_iota(jnp.int32, (ROWS, LANES), 0)
    lane = lax.broadcasted_iota(jnp.int32, (ROWS, LANES), 1)
    place = row + jnp.where(lane < LANES // 2, 0, ROWS)
    extra = jnp.zeros((ROWS, LANES), F32)
    for i, value in enumerate(values):
        extra = jnp.where(place == i, value, extra)
    extra_ref[...] = extra
    large[0].wait()
    whole = halves_of(gauss_ref)
    picked = pick(visible_ref, owned)
    frame = [
        jnp.broadcast_to(entry, (HALVES * owned, LANES))
        for entry in camera_frame(camera_rows(camera_ref))
    ]
    factor = shape_factor([whole(3 + i) for i in range(3)], [whole(6 + i) for i in range(4)])
    seen = view_of([whole(i) for i in range(3)], factor, frame, *focal)
    basis_scr[...] = jnp.stack(seen[5:])
    for f, feature in enumerate(seen[:5] + [sigmoid(whole(10))]):
        out_ref[0, f] = jnp.concatenate(picked(feature), axis=0)
    for channel in range(3):
        large[1 + channel].wait()
        summed = colour_sum(basis_scr, lambda c, k: whole(11 + 16 * c + k), channel)
        out_ref[0, 6 + channel] = jnp.concatenate(picked(jnp.maximum(summed, 0.0)), axis=0)
    message = out_ref[0]
    for i in range(1, out_ref.shape[0]):
        out_ref[i] = message


def slope_kernel(focal, visible_ref, camera_ref, gauss_ref, out_ref):
    camera = camera_rows(camera_ref)
    whole = halves_of(gauss_ref)
    picked = pick(visible_ref, gauss_ref.shape[1])
    held = [jnp.concatenate(picked(whole(k)), axis=0) for k in range(gauss_ref.shape[0])]
    for i in range(6):
        tangents = [jnp.full((1, LANES), 1.0 if j == i else 0.0, F32) for j in range(6)]
        _, slopes = jax.jvp(
            lambda *entries: features_of(held.__getitem__, entries, focal), camera, tangents
        )
        for f in range(FEATURES):
            out_ref[i, f] = slopes[f]


def split(value):
    high = value.astype(BF16)
    return high, (value - high.astype(F32)).astype(BF16)


def dot(left, right):
    return jnp.dot(left, right, preferred_element_type=F32)


def both_dots(pair, right):
    return dot(pair[0], right) + dot(pair[1], right)


def transpose_dot(left, right):
    return lax.dot_general(
        left, right, (((1,), (1,)), ((), ())), preferred_element_type=F32
    )


def stacked(value, rows):
    high, low = split(value)
    return jnp.concatenate(
        [high.astype(F32), low.astype(F32), jnp.zeros((rows - 6, value.shape[1]), F32)], axis=0
    ).astype(BF16)


def render_kernel(
    order_ref,
    length_ref,
    tile_ref,
    target_ref,
    near_ref,
    far_ref,
    extra_ref,
    near_out,
    far_out,
    extra_out,
    feature_scr,
    rgb_scr,
    weight_scr,
    high_scr,
    low_scr,
    ratio_scr,
):
    slots, depth = order_ref.shape[1], order_ref.shape[2]
    core = lax.rem(lax.axis_index("cell"), CORES)
    extra_out[...] = extra_ref[...]
    near_out[...] = jnp.zeros_like(near_out)
    far_out[...] = jnp.zeros_like(far_out)
    first = lax.broadcasted_iota(jnp.int32, (BLOCK, BLOCK), 0)
    second = lax.broadcasted_iota(jnp.int32, (BLOCK, BLOCK), 1)
    earlier = (first < second).astype(BF16)
    later = (first > second).astype(BF16)
    step_x = lax.broadcasted_iota(jnp.int32, (TILE, BLOCK), 0).astype(F32) - 7.5
    part = lax.broadcasted_iota(jnp.int32, (8, LANES), 0)
    targets = target_ref[...].astype(F32)

    places = []
    for slot in range(slots):
        tile = tile_ref[0, slot]
        places.append(
            (
                (lax.rem(tile, 16) * TILE + 8).astype(F32),
                (lax.div(tile, 16) * TILE + 8).astype(F32),
            )
        )
    def owner(slot, k):
        block = order_ref[0, slot, k]
        on_near = lax.rem(lax.div(block, 2), CORES) == core
        return lax.div(block, 4), on_near, lax.rem(block, 2)

    def forward(k, carry):
        remains, colours = carry
        alphas, keeps = [], []
        for slot in range(slots):
            chip, on_near, side = owner(slot, k)
            for f in range(FEATURES):
                entry = jnp.where(on_near, near_ref[chip, f], far_ref[chip, f])
                entry = jnp.where(side == 0, entry[0:2], entry[2:4])
                feature_scr[slot, k, f : f + 1, 0:LANES] = entry[0:1]
                feature_scr[slot, k, f : f + 1, LANES:] = entry[1:2]
            feature = feature_scr.at[slot, k]
            rgb_scr[slot, k] = stacked(feature[6:9, :], 16)
            delta_x = step_x - (feature[0:1, :] - places[slot][0])
            local_y = feature[1:2, :] - places[slot][1]
            curve_x = (-0.5 * LOG2E) * feature[2:3, :] * delta_x * delta_x
            cross_x = (-LOG2E) * feature[3:4, :] * delta_x
            curve = (-0.5 * LOG2E) * feature[4:5, :]
            opacity = jnp.where(k < length_ref[0, slot], feature[5:6, :], 0.0)
            rows = []
            for i in range(TILE):
                delta_y = (i - 7.5) - local_y
                rows.append(curve_x + (cross_x * delta_y + curve * delta_y * delta_y))
            alpha = opacity * jnp.exp2(jnp.concatenate(rows, axis=0))
            keep = alpha * (
                -LOG2E
                - alpha * (LOG2E / 2.0 + alpha * (LOG2E / 3.0 + alpha * (LOG2E / 4.0)))
            )
            ratio_scr[slot, k] = alpha * jnp.exp2(-keep)
            alphas.append(alpha)
            keeps.append(keep)
        inner = [both_dots(split(keep), earlier) for keep in keeps]
        new_remains, new_colours = [], []
        for slot in range(slots):
            before = inner[slot] + remains[slot]
            weight = alphas[slot] * jnp.exp2(before)
            weight_scr[slot, k] = weight
            high, low = split(weight)
            high_scr[slot, k] = high
            low_scr[slot, k] = low
            rgb = rgb_scr[slot, k]
            new_remains.append(before[:, BLOCK - 1 :] + keeps[slot][:, BLOCK - 1 :])
            new_colours.append(
                colours[slot] + transpose_dot(rgb, high) + transpose_dot(rgb, low)
            )
        return tuple(new_remains), tuple(new_colours)

    zero = (jnp.zeros((PIX, 1), F32),) * slots
    carry = (zero, (jnp.zeros((16, PIX), F32),) * slots)
    for k in range(depth):
        carry = forward(k, carry)
    colours = carry[1]
    misfit_rows, misfit_cols = [], []
    for slot in range(slots):
        misfit = colours[slot][0:3] + colours[slot][3:6] - targets[0, slot]
        misfit_rows.append(stacked(misfit, 16))
        turned = jnp.concatenate([misfit, jnp.zeros((5, PIX), F32)], axis=0).T
        misfit_cols.append([turned[:, c : c + 1] for c in range(3)])

    def backward(step, behind):
        k = depth - 1 - step
        throughs = []
        for slot in range(slots):
            feature = feature_scr.at[slot, k]
            throughs.append(
                weight_scr[slot, k]
                * sum(misfit_cols[slot][c] * feature[6 + c : 7 + c, :] for c in range(3))
            )
        inner = [both_dots(split(through), later) for through in throughs]
        new_behind = []
        for slot in range(slots):
            feature = feature_scr.at[slot, k]
            chip, on_near, side = owner(slot, k)
            after = inner[slot] + behind[slot]
            slope = throughs[slot] - after * ratio_scr[slot, k]
            new_behind.append(after[:, 0:1] + throughs[slot][:, 0:1])
            flat = jnp.zeros((TILE, BLOCK), F32)
            tilt = jnp.zeros((TILE, BLOCK), F32)
            bend = jnp.zeros((TILE, BLOCK), F32)
            for i in range(TILE // 2):
                top = slope[i * TILE : (i + 1) * TILE]
                bottom = slope[(TILE - 1 - i) * TILE : (TILE - i) * TILE]
                away = 7.5 - i
                flat = flat + (top + bottom)
                tilt = tilt + away * (bottom - top)
                bend = bend + (away * away) * (top + bottom)
            colour_grad = dot(misfit_rows[slot], high_scr[slot, k]) + dot(
                misfit_rows[slot], low_scr[slot, k]
            )
            delta_x = step_x - (feature[0:1, :] - places[slot][0])
            local_y = feature[1:2, :] - places[slot][1]
            mean = tilt - local_y * flat
            bend = bend - local_y * (tilt + mean)

            def across(value):
                return jnp.sum(value, axis=0, keepdims=True)

            total, mean_x, mean_y = across(flat), across(delta_x * flat), across(mean)
            square_x = across(delta_x * delta_x * flat)
            mixed = across(delta_x * mean)
            square_y = across(bend)
            conic_x, conic_xy, conic_y = feature[2:3, :], feature[3:4, :], feature[4:5, :]
            grads = [
                conic_x * mean_x + conic_xy * mean_y,
                conic_y * mean_y + conic_xy * mean_x,
                -0.5 * square_x,
                -mixed,
                -0.5 * square_y,
                total / feature[5:6, :],
            ] + [colour_grad[i : i + 1] + colour_grad[i + 3 : i + 4] for i in range(3)]
            spots, placed = [], []
            for f in range(FEATURES):
                spot = chip * FEATURES + f
                at = lax.rem(spot, 2) * ROWS + side * 2
                spots.append(lax.div(spot, 2))
                placed.append(
                    jnp.where(
                        part == at,
                        grads[f][:, :LANES],
                        jnp.where(part == at + 1, grads[f][:, LANES:], 0.0),
                    )
                )

            for f in range(FEATURES):
                near_out[spots[f]] += jnp.where(on_near, placed[f], 0.0)
                far_out[spots[f]] += jnp.where(on_near, 0.0, placed[f])

        return tuple(new_behind)

    carry = zero
    for k in range(depth):
        carry = backward(k, carry)


def render_scratch(slots, depth):
    return [
        pltpu.VMEM((slots, depth, 16, BLOCK), F32),
        pltpu.VMEM((slots, depth, 16, BLOCK), BF16),
        pltpu.VMEM((slots, depth, PIX, BLOCK), F32),
        pltpu.VMEM((slots, depth, PIX, BLOCK), BF16),
        pltpu.VMEM((slots, depth, PIX, BLOCK), BF16),
        pltpu.VMEM((slots, depth, PIX, BLOCK), F32),
    ]


def collect_kernel(parts_ref, extra_ref, out_ref):
    paired = parts_ref[0:FEATURES]
    for i in range(1, parts_ref.shape[0] // FEATURES):
        paired = paired + parts_ref[i * FEATURES : (i + 1) * FEATURES]
    pieces = [paired[i // 2, (i % 2) * ROWS : (i % 2 + 1) * ROWS] for i in range(2 * FEATURES)]
    for f in range(FEATURES):
        out_ref[0, f] = pieces[f] + pieces[FEATURES + f]
    out_ref[0, FEATURES] = extra_ref[...]
    message = out_ref[0]
    for i in range(1, out_ref.shape[0]):
        out_ref[i] = message


def pose_kernel(own_ref, slope_ref, out_ref):
    lane = lax.broadcasted_iota(jnp.int32, (1, LANES), 1)
    packed = jnp.zeros((1, LANES), F32)
    for i in range(6):
        across = jnp.sum(
            sum(own_ref[0, f] * slope_ref[i, f] for f in range(FEATURES)), axis=0, keepdims=True
        )
        packed = packed + jnp.where(lane == i, jnp.sum(across, axis=1, keepdims=True), 0.0)
    for i in range(out_ref.shape[0]):
        out_ref[i] = packed


def update_kernel(
    focal,
    parts_ref,
    gauss_ref,
    first_ref,
    second_ref,
    gauss_out,
    first_out,
    second_out,
    factor_scr,
    sum_scr,
):
    params, owned = gauss_ref.shape[0], gauss_ref.shape[1]
    views = parts_ref.shape[0]
    place = lax.broadcasted_iota(jnp.int32, (owned, LANES), 0).astype(F32)
    whole = (owned, LANES)
    for half in range(HALVES):
        lanes = slice(half * LANES, (half + 1) * LANES)

        def row(k, lanes=lanes):
            return gauss_ref[k, :, lanes]

        factor, factor_pull = jax.vjp(
            shape_factor,
            [row(3 + i) for i in range(3)],
            [row(6 + i) for i in range(4)],
        )
        for i in range(9):
            factor_scr[i] = factor[i]
        sum_scr[...] = jnp.zeros_like(sum_scr)

        def one_view(view, carry):
            def message(f, r):
                return parts_ref[view, f, r : r + 1, :]

            def extra(i):
                at = i // ROWS * (LANES // 2)
                return jnp.broadcast_to(message(FEATURES, i % ROWS)[:, at : at + 1], (1, LANES))

            masks = [place == extra(6 + sub) for sub in range(2)]
            screen = [
                sum(
                    jnp.where(masks[sub], message(f, sub * 2 + half), 0.0)
                    for sub in range(2)
                )
                for f in range(FEATURES)
            ]
            frame = [
                jnp.broadcast_to(entry, whole)
                for entry in camera_frame([extra(i) for i in range(6)])
            ]
            seen, pull = jax.vjp(
                lambda centers, factor: view_of(centers, factor, frame, *focal),
                [row(i) for i in range(3)],
                [factor_scr[i] for i in range(9)],
            )
            basis = seen[5:]
            basis_grad = [jnp.zeros(whole, F32)] * 15
            for channel in range(3):
                first_row = 11 + 16 * channel
                summed = colour_sum(basis, lambda c, k: row(11 + 16 * c + k), channel)
                gate = jnp.where(summed > 0.0, 1.0, jnp.where(summed == 0.0, 0.5, 0.0))
                colour = screen[6 + channel] * gate
                sum_scr[first_row] += HARMONIC_0 * colour
                for k in range(15):
                    basis_grad[k] = basis_grad[k] + colour * row(first_row + 1 + k)
                    sum_scr[first_row + 1 + k] += colour * basis[k]
            centre_grad, factor_grad = pull(screen[:5] + basis_grad)
            for i in range(3):
                sum_scr[i] += centre_grad[i]
            sum_scr[10] += screen[5]
            for i in range(9):
                sum_scr[params + i] += factor_grad[i]
            return carry

        lax.fori_loop(0, views, one_view, 0)
        scale_grad, quaternion_grad = factor_pull([sum_scr[params + i] for i in range(9)])
        opacity = sigmoid(row(10))
        for i in range(3):
            sum_scr[3 + i] = scale_grad[i]
        for i in range(4):
            sum_scr[6 + i] = quaternion_grad[i]
        sum_scr[10] = sum_scr[10] * opacity * (1.0 - opacity)
        for k in range(params):
            gradient = sum_scr[k]
            moment = 0.9 * first_ref[k, :, lanes] + 0.1 * gradient
            second = 0.999 * second_ref[k, :, lanes] + 0.001 * gradient * gradient
            first_out[k, :, lanes] = moment
            second_out[k, :, lanes] = second
            gauss_out[k, :, lanes] = row(k) - (0.05 / (1.0 - 0.9**10)) * moment / (
                jnp.sqrt(second * (1.0 / (1.0 - 0.999**10))) + 1e-08
            )


VMEM = pl.BlockSpec(memory_space=pltpu.VMEM)
SMEM = pl.BlockSpec(memory_space=pltpu.SMEM)
PARAMETERS = pltpu.CompilerParams(vmem_limit_bytes=40 * 1024 * 1024)


def shards(
    gaussians,
    first_moment,
    second_moment,
    cameras,
    visible_blocks,
    tile_ids,
    tile_order,
    tile_length,
    targets,
):
    owned, params = gaussians.shape[0], gaussians.shape[1]
    gaussians, first_moment, second_moment = (
        array.transpose(1, 0, 2) for array in (gaussians, first_moment, second_moment)
    )
    cells = lax.axis_size("cell")
    views = lax.axis_size("view")
    chips = cells // CORES
    tile_total = cells * tile_ids.shape[1]
    focal = (16.0 * TILE, 8.0 * TILE, tile_total * TILE / 32.0)
    same_core = [[chip * CORES + core for chip in range(chips)] for core in range(CORES)]
    swap = [(cell, cell ^ 1) for cell in range(cells)]

    with jax.named_scope("project"):
        message, extra = pl.pallas_call(
            lambda *refs: project_kernel(focal, *refs),
            out_shape=[
                jax.ShapeDtypeStruct((8, FEATURES, ROWS, LANES), F32),
                jax.ShapeDtypeStruct((ROWS, LANES), F32),
            ],
            in_specs=[pl.BlockSpec(memory_space=pl.ANY)] * 3,
            out_specs=[VMEM, VMEM],
            scratch_shapes=[
                pltpu.SMEM(visible_blocks.shape, jnp.int32),
                pltpu.SMEM(cameras.shape, F32),
                pltpu.VMEM(gaussians.shape, F32),
                pltpu.VMEM((15, HALVES * owned, LANES), F32),
                pltpu.SemaphoreType.DMA((2,)),
                pltpu.SemaphoreType.DMA((4,)),
            ],
            compiler_params=pltpu.CompilerParams(vmem_limit_bytes=60 * 1024 * 1024),
            name="project",
        )(visible_blocks, cameras, gaussians)
        slopes = pl.pallas_call(
            lambda *refs: slope_kernel(focal, *refs),
            out_shape=jax.ShapeDtypeStruct((6, FEATURES, ROWS, LANES), F32),
            in_specs=[SMEM, SMEM, VMEM],
            out_specs=VMEM,
            compiler_params=PARAMETERS,
            cost_estimate=pl.CostEstimate(
                flops=4_000_000, bytes_accessed=200_000, transcendentals=10_000
            ),
            name="slope",
        )(visible_blocks, cameras, gaussians)
    with jax.named_scope("gather"):
        deep, wide = 8, chips // 8
        z_groups = [
            [(x * deep + z) * CORES + core for z in range(deep)]
            for x in range(wide)
            for core in range(CORES)
        ]
        x_groups = [
            [(x * deep + z) * CORES + core for x in range(wide)]
            for z in range(deep)
            for core in range(CORES)
        ]
        column = lax.all_to_all(
            message, "cell", 0, 0, axis_index_groups=z_groups, tiled=True
        )
        columns = lax.optimization_barrier(jnp.broadcast_to(column, (wide, *column.shape)))
        near = lax.all_to_all(
            columns, "cell", 0, 0, axis_index_groups=x_groups, tiled=True
        ).reshape(chips, FEATURES, ROWS, LANES)
        far = lax.ppermute(near, "cell", swap)
    with jax.named_scope("render"):
        pairs = jax.ShapeDtypeStruct((chips * FEATURES * ROWS // 8, 8, LANES), F32)
        near_grad, far_grad, extra = pl.pallas_call(
            render_kernel,
            out_shape=[pairs, pairs, jax.ShapeDtypeStruct(extra.shape, F32)],
            in_specs=[SMEM, SMEM, SMEM, VMEM, VMEM, VMEM, VMEM],
            out_specs=[VMEM, VMEM, VMEM],
            scratch_shapes=render_scratch(*tile_order.shape[1:]),
            compiler_params=PARAMETERS,
            name="render",
        )(tile_order, tile_length, tile_ids, targets, near, far, extra)
    with jax.named_scope("scatter"):
        pair = near_grad + lax.ppermute(far_grad, "cell", swap)
        parts = lax.all_to_all(
            pair.reshape(near.shape), "cell", 0, 0, axis_index_groups=same_core, tiled=True)
    with jax.named_scope("collect"):
        own = pl.pallas_call(
            collect_kernel,
            out_shape=jax.ShapeDtypeStruct((views, VIEW_MSG, ROWS, LANES), F32),
            in_specs=[VMEM, VMEM],
            out_specs=VMEM,
            compiler_params=PARAMETERS,
            name="collect",
        )(parts.reshape(pair.shape), extra)
        every = lax.all_to_all(own, "view", 0, 0, tiled=True)
    with jax.named_scope("camera"):
        camera_part = pl.pallas_call(
            pose_kernel,
            out_shape=jax.ShapeDtypeStruct((chips, 1, LANES), F32),
            in_specs=[VMEM, VMEM],
            out_specs=VMEM,
            compiler_params=PARAMETERS,
            cost_estimate=pl.CostEstimate(
                flops=100_000, bytes_accessed=250_000, transcendentals=0
            ),
            name="pose",
        )(own, slopes)
        camera_copies = camera_part + lax.ppermute(camera_part, "cell", swap)
        every, camera_copies = lax.optimization_barrier((every, camera_copies))
        camera_parts = lax.all_to_all(
            camera_copies, "cell", 0, 0, axis_index_groups=same_core, tiled=True
        )
    with jax.named_scope("update"):
        state = jax.ShapeDtypeStruct(gaussians.shape, F32)
        new_gaussians, new_first, new_second = pl.pallas_call(
            lambda *refs: update_kernel(focal, *refs),
            out_shape=[state, state, state],
            in_specs=[VMEM] * 4,
            out_specs=[VMEM] * 3,
            scratch_shapes=[
                pltpu.VMEM((9, owned, LANES), F32),
                pltpu.VMEM((params + 9, owned, LANES), F32),
            ],
            compiler_params=PARAMETERS,
            name="update",
        )(every, gaussians, first_moment, second_moment)
    with jax.named_scope("camera"):
        camera_total = jnp.sum(camera_parts, axis=0)[:, :6]
    return (
        new_gaussians.transpose(1, 0, 2),
        new_first.transpose(1, 0, 2),
        new_second.transpose(1, 0, 2),
        camera_total,
    )


def solution(mesh):
    return jax.shard_map(
        shards,
        mesh=mesh,
        in_specs=(
            P("cell", None, None),
            P("cell", None, None),
            P("cell", None, None),
            P("view", None),
            P("view", "cell"),
            P("view", "cell"),
            P("view", "cell", None),
            P("view", "cell"),
            P("view", "cell", None, None),
        ),
        out_specs=(
            P("cell", None, None),
            P("cell", None, None),
            P("cell", None, None),
            P("view", None),
        ),
        check_vma=False,
    )
```
